32 devices in a mesh: section: 2 (over x), dp: 4 (over y, core), tensor: 4 (over z).
Axes of the slice: x: 2, y: 2, z: 4, core: 2. Of those that a mesh axis runs over, the one named last changes fastest.
Arguments:
- images_in: bfloat16 [2, 3152, 1024], P(None, ('dp', 'tensor')), may hold values from -6 to 6
- cotangent: bfloat16 [2, 3152, 1024], P(None, ('dp', 'tensor')), may hold values from -6 to 6
- w_qkv: bfloat16 [2, 1024, 3, 1024], P('section', 'dp', None, 'tensor'), may hold values from -0.1875 to 0.1875
- w_out: bfloat16 [2, 1024, 1024], P('section', 'dp', 'tensor'), may hold values from -0.75 to 0.75
- w_up: bfloat16 [2, 1024, 4096], P('section', 'dp', 'tensor'), may hold values from -0.1875 to 0.1875
- w_down: bfloat16 [2, 1024, 4096], P('section', 'dp', 'tensor'), may hold values from -0.09375 to 0.09375
- norm_gains: bfloat16 [2, 2, 1024], P('section', None, ('dp', 'tensor')), may hold values from 0.5 to 1.5
- row_shifts: bfloat16 [2, 4, 1024], P('section', None, ('dp', 'tensor')), may hold values from -3 to 3
- head_bias: bfloat16 [2, 2, 16, 64], P('section', None, 'tensor', 'dp'), may hold values from -3 to 3
- unit_bias: bfloat16 [2, 16, 256], P('section', 'tensor', 'dp'), may hold values from -3 to 3
Outputs:
- layer_out: bfloat16 [2, 2, 3152, 1024], P('section', None, ('dp', 'tensor'))
- input_grads: bfloat16 [2, 2, 3152, 1024], P('section', None, ('dp', 'tensor'))
- grad_qkv: float32 [2, 1024, 3, 1024], P('section', 'dp', None, 'tensor')
- grad_out: float32 [2, 1024, 1024], P('section', 'dp', 'tensor')
- grad_up: float32 [2, 1024, 4096], P('section', 'dp', 'tensor')
- grad_down: float32 [2, 1024, 4096], P('section', 'dp', 'tensor')
- grad_gains: float32 [2, 2, 1024], P('section', None, ('dp', 'tensor'))
- grad_shifts: float32 [2, 4, 1024], P('section', None, ('dp', 'tensor'))
- grad_head_bias: float32 [2, 2, 16, 64], P('section', None, 'tensor', 'dp')
- grad_unit_bias: float32 [2, 16, 256], P('section', 'tensor', 'dp')
The draws below stay inside these ranges and needn't reach their ends.
All inputs are finite; a program needn't handle non-finite values.
Results may differ from the reference program's by a relative error of at most 0.018.
Values may be sent and summed in bfloat16 or wider, within the bound.
A program may use at most 256 MiB of HBM per device.

```python
import jax
import jax.numpy as jnp
from jax import lax

D = 1024
HEADS = 16
HD = 64
FF = 4096
SEQ = 197
MICRO = 2
IMG_DEV = 4
TOKENS = 3152


def block_levels(rng, shape, pieces, smallest, largest):
    gain = 1.0
    for position, blocks in pieces:
        heights = jax.random.uniform(jax.random.fold_in(jax.random.fold_in(rng, 6), position), (blocks,), jnp.float32, smallest / len(pieces), largest / len(pieces))
        gain = gain * jnp.repeat(jnp.exp(heights), shape[position] // blocks).reshape((-1,) + (1,) * (len(shape) - 1 - position))
    return gain


def noise(own_key, shape, deviation, bound, split=(), held_as=jnp.bfloat16):
    gain = block_levels(own_key, shape, split, -0.22, 0.18) if split else 1.0
    array = jax.random.normal(own_key, shape, jnp.float32) * deviation * gain
    return jnp.minimum(jnp.maximum(array, -bound), bound).astype(held_as)


def setup_inputs(seed: int = 0) -> dict:
    streams_of = jax.random.split(jax.random.key(seed), 11)
    return {
        "images_in": noise(streams_of[0], (MICRO, TOKENS, D), 1.0, 6.0, ((1, 16),)),
        "cotangent": noise(streams_of[1], (MICRO, TOKENS, D), 1.0, 6.0, ((1, 16),)),
        "w_qkv": noise(streams_of[2], (2, D, 3, D), D ** -0.5, 0.1875, ((0, 2), (1, 4), (3, 4))),
        "w_out": noise(streams_of[3], (2, D, D), (D // 16) ** -0.5, 0.75, ((0, 2), (1, 4), (2, 4))),
        "w_up": noise(streams_of[4], (2, D, FF), D ** -0.5, 0.1875, ((0, 2), (1, 4), (2, 4))),
        "w_down": noise(streams_of[5], (2, D, FF), FF ** -0.5, 0.09375, ((0, 2), (1, 4), (2, 4))),
        "norm_gains": jnp.clip(1.0 + 0.1 * jax.random.normal(streams_of[6], (2, 2, D), jnp.float32), 0.5, 1.5).astype(jnp.bfloat16),
        "row_shifts": noise(streams_of[7], (2, 4, D), 0.5, 3.0, ((0, 2), (2, 16))),
        "head_bias": noise(streams_of[8], (2, 2, HEADS, HD), 0.5, 3.0, ((0, 2), (2, 4), (3, 4))),
        "unit_bias": noise(streams_of[9], (2, HEADS, FF // HEADS), 0.5, 3.0, ((0, 2), (1, 4), (2, 4))),
    }


PRECISE = lax.Precision.HIGHEST
SCORE_SCALE = 0.125
NORM_EPS = 1e-06

@jax.custom_vjp
def low(v):
    return lax.optimization_barrier(v.astype(jnp.bfloat16)).astype(jnp.float32)

@jax.custom_vjp
def low_back(v):
    return v

def low_keep(v):
    return (low(v), None)

def low_pass(kept, grad):
    return (grad,)

def back_keep(v):
    return (v, None)

def back_low(kept, grad):
    return (low(grad),)
low.defvjp(low_keep, low_pass)
low_back.defvjp(back_keep, back_low)

def normalize(values, scales, offsets):
    average = lax.optimization_barrier(jnp.mean(values, axis=-1, keepdims=True))
    centred = values - average
    spread = lax.optimization_barrier(jnp.mean(centred * centred, axis=-1, keepdims=True))
    return centred * lax.rsqrt(spread + NORM_EPS) * scales + offsets

def attend_group(operands):
    queries, key_rows, value_rows = operands
    scores = low_back(jnp.einsum('isha,itha->ihst', queries, key_rows, precision=PRECISE) * SCORE_SCALE)
    highest = lax.optimization_barrier(jnp.max(scores, axis=-1, keepdims=True))
    weights = jnp.exp(scores - highest)
    probabilities = low(weights / lax.optimization_barrier(jnp.sum(weights, axis=-1, keepdims=True)))
    return jnp.einsum('ihst,itha->isha', probabilities, value_rows, precision=PRECISE)

def layer(inputs, qkv_weight, out_weight, up_weight, down_weight, gains, shifts, head_terms, unit_terms):
    row_total = inputs.shape[0]
    normed = low(normalize(inputs, gains[0], shifts[0]))
    projected = jnp.dot(normed, qkv_weight.reshape(D, 3 * D), precision=PRECISE).reshape(row_total, 3, D)
    queries = low_back(low(projected[:, 0] + head_terms[0].reshape(D)))
    key_rows = low_back(low(projected[:, 1]))
    value_rows = low_back(low(projected[:, 2] + head_terms[1].reshape(D)))
    group_shape = (row_total // (IMG_DEV * SEQ), IMG_DEV, SEQ, HEADS, HD)
    mixed_rows = lax.map(jax.checkpoint(attend_group), (queries.reshape(group_shape), key_rows.reshape(group_shape), value_rows.reshape(group_shape)))
    mixed_rows = low_back(low(mixed_rows.reshape(row_total, D)))
    branch = low_back(jnp.dot(mixed_rows, out_weight.T, precision=PRECISE))
    middle = inputs + branch + shifts[1]
    normed_two = low(normalize(middle, gains[1], shifts[2]))
    hidden_pre = low_back(jnp.dot(normed_two, up_weight, precision=PRECISE) + unit_terms.reshape(FF))
    hidden = low(jax.nn.gelu(hidden_pre, approximate=False))
    branch_two = low_back(jnp.dot(hidden, down_weight.T, precision=PRECISE))
    return middle + branch_two + shifts[3]

def add_trees(first_tree, second_tree):
    if first_tree is None:
        return second_tree
    return jax.tree.map(jnp.add, first_tree, second_tree)

def reference(images_in, cotangent, w_qkv, w_out, w_up, w_down, norm_gains, row_shifts, head_bias, unit_bias):
    stacks = (w_qkv, w_out, w_up, w_down, norm_gains, row_shifts, head_bias, unit_bias)
    params_first = tuple((stacked[0].astype(jnp.float32) for stacked in stacks))
    params_second = tuple((stacked[1].astype(jnp.float32) for stacked in stacks))
    outs_first, outs_second, input_first, input_second = ([], [], [], [])
    totals_first = None
    totals_second = None
    for micro_index in range(MICRO):
        layer_input = images_in[micro_index].astype(jnp.float32)
        middle_out, back_first = jax.vjp(layer, layer_input, *params_first)
        middle_low = middle_out.astype(jnp.bfloat16)
        final_out, back_second = jax.vjp(layer, middle_low.astype(jnp.float32), *params_second)
        second_grads = back_second(cotangent[micro_index].astype(jnp.float32))
        middle_grad = second_grads[0].astype(jnp.bfloat16)
        first_grads = back_first(middle_grad.astype(jnp.float32))
        outs_first.append(middle_low)
        outs_second.append(final_out.astype(jnp.bfloat16))
        input_first.append(first_grads[0].astype(jnp.bfloat16))
        input_second.append(middle_grad)
        totals_first = add_trees(totals_first, tuple(first_grads[1:]))
        totals_second = add_trees(totals_second, tuple(second_grads[1:]))
    layer_out = jnp.stack([jnp.stack(outs_first), jnp.stack(outs_second)])
    input_grads = jnp.stack([jnp.stack(input_first), jnp.stack(input_second)])
    joined = tuple((jnp.stack([one_grad, two_grad]) for one_grad, two_grad in zip(totals_first, totals_second)))
    return (layer_out, input_grads, joined[0], joined[1], joined[2], joined[3], joined[4], joined[5], joined[6], joined[7])
```

```python
import math

import jax
import jax.numpy as jnp
from jax import lax
from jax.experimental import pallas as pl
from jax.experimental.pallas import tpu as pltpu
from jax.sharding import PartitionSpec as P

D = 1024
HD = 64
SEQ = 197
RP = 208
RC = 16
TILE = 256
SCALE = 0.125
EPS = 1e-06
MESH = pl.DeviceIdType.MESH
BF = jnp.bfloat16
F32 = jnp.float32
NN = (((1,), (0,)), ((), ()))
NT = (((1,), (1,)), ((), ()))
TN = (((0,), (0,)), ((), ()))
VMEM_LIMIT = 60 * 2**20


def mm(a, b, dims):
    return lax.dot_general(a, b, dims, preferred_element_type=F32)


def blk(i, size):
    if isinstance(i, int):
        return pl.ds(i * size, size)
    return pl.ds(pl.multiple_of(i * size, size), size)


class Place:
    def __init__(self, dpn, nz):
        self.Y, self.nz = dpn // 2, nz
        self.x = lax.axis_index("section")
        dp = lax.axis_index("dp")
        self.z = lax.axis_index("tensor")
        self.y, self.c = dp // 2, lax.rem(dp, 2)
        self.j = 2 * self.x + self.c

    def dev(self, x=None, y=None, c=None, z=None):
        x = self.x if x is None else x
        y = self.y if y is None else y
        c = self.c if c is None else c
        z = self.z if z is None else z
        return (x, 2 * y + c, z)

    def cell(self, k):
        jp = lax.rem(self.j + k, 4)
        return jp, jp // 2, lax.rem(jp, 2)

    def yk(self, k):
        return lax.rem(self.y + k, self.Y)

    def zk(self, k):
        return lax.rem(self.z + k, self.nz)

    def barrier(self):
        bar = pltpu.get_barrier_semaphore()
        n = 0
        for k in range(1, 4):
            _, xp, cp = self.cell(k)
            pl.semaphore_signal(bar, inc=1, device_id=self.dev(x=xp, c=cp), device_id_type=MESH)
            n += 1
        for k in range(1, self.nz):
            pl.semaphore_signal(bar, inc=1, device_id=self.dev(z=self.zk(k)), device_id_type=MESH)
            n += 1
        for k in range(1, self.Y):
            pl.semaphore_signal(bar, inc=1, device_id=self.dev(y=self.yk(k)), device_id_type=MESH)
            n += 1
        pl.semaphore_wait(bar, n)


def rcopy(src, dst, ss, rs, dev):
    return pltpu.make_async_remote_copy(
        src_ref=src, dst_ref=dst, send_sem=ss, recv_sem=rs, device_id=dev, device_id_type=MESH
    )


class Exchange:
    def __init__(self, p, op, rb, cs, xr, gs, gr, ss, sr):
        self.p, self.op, self.rb, self.cs, self.xr = p, op, rb, cs, xr
        self.gs, self.gr, self.ss, self.sr = gs, gr, ss, sr

    def rows(self, m, c):
        return blk(2 * m + c, RP)

    def gather(self, buf, s):
        return Gather(self, buf, s)

    def send_core(self, m, s):
        p = self.p
        cp = self._core(m, s)
        cp.start()

    def _core(self, m, s):
        p = self.p
        return rcopy(
            self.op.at[self.rows(m, 1 - p.c)], self.rb.at[m], self.ss.at[s, m], self.sr.at[s, m], p.dev(c=1 - p.c)
        )

    def send_chip(self, s):
        p = self.p
        far = 1 - p.x
        self._core(far, s).wait_recv()
        both = self.op[self.rows(far, p.c), :].astype(F32) + self.rb[far].astype(F32)
        self.cs[...] = both.astype(BF)
        self._chip(s).start()

    def _chip(self, s):
        p = self.p
        return rcopy(self.cs, self.xr, self.ss.at[s, 2], self.sr.at[s, 2], p.dev(x=1 - p.x))

    def wait_sums(self, s):
        self._core(self.p.x, s).wait_recv()
        self._chip(s).wait_recv()

    def sums(self, r):
        p = self.p
        own = self.op[pl.ds(pl.multiple_of((2 * p.x + p.c) * RP + r * RC, RC), RC), :].astype(F32)
        rs = blk(r, RC)
        return own + self.rb[p.x, rs, :].astype(F32) + self.xr[rs, :].astype(F32)

    def done(self, s):
        for m in range(2):
            self._core(m, s).wait_send()
        self._chip(s).wait_send()


class Gather:
    def __init__(self, ex, buf, s):
        p = ex.p
        own, rel = buf.at[ex.rows(p.x, p.c)], buf.at[ex.rows(1 - p.x, p.c)]
        sib = p.dev(c=1 - p.c)
        self.core = rcopy(own, own, ex.gs.at[s, 0], ex.gr.at[s, 0], sib)
        self.chip = rcopy(own, own, ex.gs.at[s, 1], ex.gr.at[s, 1], p.dev(x=1 - p.x))
        self.relay = rcopy(rel, rel, ex.gs.at[s, 2], ex.gr.at[s, 2], sib)

    def start(self):
        self.chip.start()
        self.core.start()

    def near(self):
        self.core.wait_recv()

    def pass_on(self):
        self.chip.wait_recv()
        self.relay.start()

    def far(self):
        self.relay.wait_recv()

    def done(self):
        self.core.wait_send()
        self.chip.wait_send()
        self.relay.wait_send()


def norm_row(v, g, b):
    cen = v - jnp.sum(v, axis=-1, keepdims=True) * (1.0 / D)
    var = jnp.sum(cen * cen, axis=-1, keepdims=True) * (1.0 / D)
    return cen * lax.rsqrt(var + EPS) * g + b


def half(h):
    return blk(h, 2 * RP)


def forward_kernel(dpn, nz, rows):
    Y, R = dpn // 2, rows
    R2 = 2 * R

    def body(
        img, wa, wu, wd, sp,
        lo, o_w, o_nf, o_pr, o_mx, o_n2, o_h, o_gd, o_pb, o_x, o_mid, o_sp,
        W, SPB, SPS, G, NF, PR, MX, N2, H, GD, PB, XO, MID, OUT, LOB, OP, RB, CS, XR,
        red_s, red_r, z_s, z_r, y_s, y_r, ps, pr, gs, gr, ss, sr, lo_s, lo_r, keep,
    ):
        p = Place(dpn, nz)
        x, y, c, z, j = p.x, p.y, p.c, p.z, p.j
        src = (wa, wu, wd)
        ex = Exchange(p, OP, RB, CS, XR, gs, gr, ss, sr)

        XO[0] = jnp.zeros((2, RP, D), BF)
        for m in range(2):
            XO[0, m, 0:SEQ, :] = img[m]
        p.barrier()

        def small_red(k):
            jp, xp, cp = p.cell(k)
            dst = SPB.at[x, y, z, c]
            if k == 0:
                return pltpu.make_async_copy(sp.at[jp], dst, pr.at[x, c])
            return rcopy(sp.at[jp], dst, ps.at[k], pr.at[x, c], p.dev(x=xp, c=cp))

        def small_z(l, k):
            t = SPB.at[l, y, z]
            return rcopy(t, t, ps.at[4 + l * nz + k], pr.at[2 + l, k], p.dev(z=p.zk(k)))

        def small_y(l, k):
            t = SPB.at[l, y]
            return rcopy(t, t, ps.at[4 + 2 * nz + l * Y + k], pr.at[4 + l, k], p.dev(y=p.yk(k)))

        for k in range(4):
            small_red(k).start()

        def red(m, k):
            jp, xp, cp = p.cell(k)
            s = src[m].at[jp] if m == 0 else src[m].at[:, blk(jp, TILE)]
            dst = W.at[x * 3 + m, blk(2 * y + c, R), blk(z, TILE)]
            if k == 0:
                return pltpu.make_async_copy(s, dst, red_r.at[x * 3 + m, c])
            return rcopy(s, dst, red_s.at[m, k], red_r.at[x * 3 + m, c], p.dev(x=xp, c=cp))

        for m in range(3):
            for k in (1, 2, 3, 0):
                red(m, k).start()

        def chunk(lm, zz):
            return W.at[lm, blk(y, R2), blk(zz, TILE)]

        def wz(lm, k):
            t = chunk(lm, z)
            return rcopy(t, t, z_s.at[lm, k], z_r.at[lm, k], p.dev(z=p.zk(k)))

        def wy(lm, kz, ky):
            t = chunk(lm, p.zk(nz - kz))
            return rcopy(t, t, y_s.at[lm, kz, ky], y_r.at[lm, kz, ky], p.dev(y=p.yk(ky)))

        def release(lm):
            for cs_ in range(2):
                t = W.at[lm, blk(2 * y + cs_, R), blk(z, TILE)]
                pltpu.make_async_copy(t, t, red_r.at[lm, cs_]).wait()
            for k in (2, 1, 3):
                if k < nz:
                    wz(lm, k).start()
            for ky in range(1, Y):
                wy(lm, 0, ky).start()

        def hand_on(lm, k):
            wz(lm, k).wait_recv()
            for ky in range(1, Y):
                wy(lm, k, ky).start()

        def hand_all(lm):
            for k in (1, 3, 2):
                hand_on(lm, k)

        def ready(lm):
            for kz in range(nz):
                for ky in range(1, Y):
                    wy(lm, kz, ky).wait_recv()

        for l in range(2):
            for cs_ in range(2):
                t = SPB.at[l, y, z, cs_]
                pltpu.make_async_copy(t, t, pr.at[l, cs_]).wait()
            for k in range(1, nz):
                small_z(l, k).start()
        release(0)
        for l in range(2):
            for k in range(1, nz):
                small_z(l, k).wait_recv()
            for k in range(1, Y):
                small_y(l, k).start()
        for l in range(2):
            for k in range(1, Y):
                small_y(l, k).wait_recv()
            SPS[l] = jnp.sum(SPB[l].astype(F32).reshape(Y * nz * 2, 32, TILE), axis=0)
            for r in range(6):
                for q in range(4):
                    G[l, r : r + 1, q * TILE : (q + 1) * TILE] = SPS[l, 4 * r + q : 4 * r + q + 1, :]

        def put(src_ref, dst_ref, i):
            return pltpu.make_async_copy(src_ref, dst_ref, keep.at[i])

        def ln_first(l, slot, load):
            g, b = G[l, 0:1, :], G[l, 2:3, :]

            def step(r, _):
                v = load(r)
                NF[l, pl.ds(pl.multiple_of(slot * RP + r * RC, RC), RC), :] = norm_row(v, g, b).astype(BF)
                return 0

            lax.fori_loop(0, RP // RC, step, 0)

        def qkv(l, h):
            rows_ = half(h)

            def step(n, _):
                cols = blk(n, TILE)
                t = mm(NF[l, rows_, :], W[3 * l, :, cols], NN)
                PR[l, rows_, cols] = (t + SPS[l, pl.ds(24 + n, 1), :]).astype(BF)
                return 0

            lax.fori_loop(0, 4, step, 0)

        def attend(l, h):
            live = lax.broadcasted_iota(jnp.int32, (RP, RP), 1) < SEQ

            def step(i, _):
                im = 2 * h + i
                rows_ = blk(im, RP)
                for zz in range(4):
                    cols = blk(zz, TILE)
                    t = PR[l, rows_, cols]
                    q, k, v = t[:, 0:HD], t[:, HD : 2 * HD], t[:, 2 * HD : 3 * HD]
                    s = jnp.where(live, mm(q, k, NT) * SCALE, -1e30)
                    w = jnp.exp(s - jnp.max(s, axis=-1, keepdims=True))
                    pb = (w * (1.0 / jnp.sum(w, axis=-1, keepdims=True))).astype(BF)
                    PB[l, 4 * im + zz] = pb
                    o = mm(pb, v, NN).astype(BF)
                    MX[l, rows_, cols] = jnp.concatenate([jnp.zeros((RP, 3 * HD), BF), o], axis=1)
                return 0

            lax.fori_loop(0, 2, step, 0)

        def project(lhs, l, m, h):
            rows_ = half(h)

            def step(n, _):
                cols = blk(n, TILE)
                OP[rows_, cols] = mm(lhs[l, rows_, :], W[3 * l + m, cols, :], NT).astype(BF)
                return 0

            lax.fori_loop(0, 4, step, 0)

        def up(l, h):
            rows_ = half(h)

            def step(n, _):
                cols = blk(n, TILE)
                u = mm(N2[l, rows_, :], W[3 * l + 1, :, cols], NN) + SPS[l, pl.ds(28 + n, 1), :]
                cdf = 0.5 + 0.5 * lax.erf(u * (1.0 / math.sqrt(2.0)))
                H[l, rows_, cols] = (u * cdf).astype(BF)
                GD[l, rows_, cols] = (cdf + u * jnp.exp(-0.5 * u * u) * (1.0 / math.sqrt(2.0 * math.pi))).astype(BF)
                return 0

            lax.fori_loop(0, 4, step, 0)

        near, far = x, 1 - x
        for l in range(2):
            A, U, DN = 3 * l, 3 * l + 1, 3 * l + 2
            if l == 0:
                for m in range(2):
                    ln_first(0, 2 * m + c, lambda r, m=m: XO[0, m, blk(r, RC), :].astype(F32))
                own = [
                    rcopy(NF.at[0, ex.rows(m, c)], NF.at[0, ex.rows(m, c)], gs.at[0, m], gr.at[0, m], p.dev(c=1 - c))
                    for m in range(2)
                ]
                for cp in own:
                    cp.start()
                release(1)
                hand_all(0)
                for cp in own:
                    cp.wait_recv()
            else:
                ln_first(1, 2 * x + c, lambda r: OUT[0, blk(r, RC), :].astype(F32))
                ga = ex.gather(NF.at[1], 2)
                ga.start()
                ga.near()
            ready(A)
            qkv(l, near)
            if l == 1:
                ga.pass_on()
            attend(l, near)
            if l == 0:
                release(2)
                hand_all(1)
            else:
                release(5)
                ga.far()
            qkv(l, far)
            attend(l, far)
            s = 2 * l
            project(MX, l, 0, far)
            ex.send_core(far, s)
            project(MX, l, 0, near)
            ex.send_core(near, s)
            ex.send_chip(s)
            if l == 0:
                release(3)
                hand_all(2)
            else:
                hand_all(4)
            ex.wait_sums(s)
            slot = 2 * x + c
            g, b, sh = G[l, 1:2, :], G[l, 4:5, :], G[l, 3:4, :]

            def second(r, _):
                rs = blk(r, RC)
                v = XO[0, x, rs, :] if l == 0 else OUT[0, rs, :]
                mid = v.astype(F32) + ex.sums(r) + sh
                MID[l, rs, :] = mid
                N2[l, pl.ds(pl.multiple_of(slot * RP + r * RC, RC), RC), :] = norm_row(mid, g, b).astype(BF)
                return 0

            lax.fori_loop(0, RP // RC, second, 0)
            ex.done(s)
            gb = ex.gather(N2.at[l], 1 + 2 * l)
            gb.start()
            ready(U)
            gb.near()
            up(l, near)
            gb.pass_on()
            if l == 0:
                release(4)
                hand_all(3)
            else:
                hand_all(5)
            gb.far()
            up(l, far)
            ready(DN)
            s = 2 * l + 1
            project(H, l, 2, far)
            ex.send_core(far, s)
            project(H, l, 2, near)
            ex.send_core(near, s)
            ex.send_chip(s)
            ex.wait_sums(s)
            sh3 = G[l, 5:6, :]

            def last(r, _):
                rs = blk(r, RC)
                OUT[l, rs, :] = (MID[l, rs, :] + ex.sums(r) + sh3).astype(BF)
                return 0

            lax.fori_loop(0, RP // RC, last, 0)
            ex.done(s)
            if l == 0:
                for cp in own:
                    cp.wait_send()
            else:
                ga.done()
            gb.done()

            @pl.when(x != l)
            def _():
                rcopy(OUT.at[l], LOB, lo_s, lo_r, p.dev(x=1 - x)).start()

            for i, (a, o) in enumerate(
                ((NF, o_nf), (PR, o_pr), (MX, o_mx), (N2, o_n2), (H, o_h), (GD, o_gd), (PB, o_pb), (MID, o_mid))
            ):
                put(a.at[l], o.at[l], 8 * l + i).start()

        put(W, o_w, 16).start()
        put(XO.at[0, x], o_x.at[0], 17).start()
        put(OUT.at[0], o_x.at[1], 18).start()
        put(SPS, o_sp, 19).start()
        for k in range(4):
            if k:
                small_red(k).wait_send()
        for l in range(2):
            for k in range(1, nz):
                small_z(l, k).wait_send()
            for k in range(1, Y):
                small_y(l, k).wait_send()
        for m in range(3):
            for k in range(1, 4):
                red(m, k).wait_send()
        for lm in range(6):
            for k in range(1, nz):
                wz(lm, k).wait_send()
            for kz in range(nz):
                for ky in range(1, Y):
                    wy(lm, kz, ky).wait_send()
        cp = rcopy(OUT.at[x], LOB, lo_s, lo_r, p.dev(x=1 - x))
        cp.wait_recv()
        cp.wait_send()
        lo[x] = OUT[x, 0:SEQ, :]
        lo[1 - x] = LOB[0:SEQ, :]
        for l in range(2):
            for i, (a, o) in enumerate(
                ((NF, o_nf), (PR, o_pr), (MX, o_mx), (N2, o_n2), (H, o_h), (GD, o_gd), (PB, o_pb), (MID, o_mid))
            ):
                put(a.at[l], o.at[l], 8 * l + i).wait()
        put(W, o_w, 16).wait()
        put(XO.at[0, x], o_x.at[0], 17).wait()
        put(OUT.at[0], o_x.at[1], 18).wait()
        put(SPS, o_sp, 19).wait()

    full = (2, 4 * RP, D)
    states = [
        ((6, D, D), BF), (full, BF), (full, BF), (full, BF), (full, BF), (full, BF), (full, BF),
        ((2, 16, RP, RP), BF), ((2, RP, D), BF), ((2, RP, D), F32), ((2, 32, TILE), F32),
    ]
    vm = pl.BlockSpec(memory_space=pltpu.VMEM)
    hbm = pl.BlockSpec(memory_space=pl.ANY)
    dma = pltpu.SemaphoreType.DMA
    return pl.pallas_call(
        body,
        out_shape=[jax.ShapeDtypeStruct((2, SEQ, D), BF)] + [jax.ShapeDtypeStruct(s, t) for s, t in states],
        in_specs=[vm, hbm, hbm, hbm, hbm],
        out_specs=[vm] + [hbm] * len(states),
        scratch_shapes=[
            pltpu.VMEM((6, D, D), BF),
            pltpu.VMEM((2, Y, nz, 2, 32, TILE), BF),
            pltpu.VMEM((2, 32, TILE), F32),
            pltpu.VMEM((2, 8, D), F32),
            pltpu.VMEM(full, BF), pltpu.VMEM(full, BF), pltpu.VMEM(full, BF),
            pltpu.VMEM(full, BF), pltpu.VMEM(full, BF), pltpu.VMEM(full, BF),
            pltpu.VMEM((2, 16, RP, RP), BF),
            pltpu.VMEM((1, 2, RP, D), BF),
            pltpu.VMEM((2, RP, D), F32),
            pltpu.VMEM((2, RP, D), BF),
            pltpu.VMEM((RP, D), BF),
            pltpu.VMEM((4 * RP, D), BF),
            pltpu.VMEM((2, RP, D), BF),
            pltpu.VMEM((RP, D), BF),
            pltpu.VMEM((RP, D), BF),
            dma((3, 4)), dma((6, 2)), dma((6, nz)), dma((6, nz)), dma((6, nz, Y)), dma((6, nz, Y)),
            dma((4 + 2 * nz + 2 * Y,)), dma((6, max(nz, Y, 2))),
            dma((4, 3)), dma((4, 3)), dma((4, 3)), dma((4, 3)), dma, dma, dma((20,)),
        ],
        compiler_params=pltpu.CompilerParams(
            collective_id=0, has_side_effects=True, vmem_limit_bytes=VMEM_LIMIT
        ),
    )


def backward_kernel(dpn, nz, rows):
    Y, R = dpn // 2, rows
    R2 = 2 * R

    def body(
        cot, i_w, i_nf, i_pr, i_mx, i_n2, i_h, i_gd, i_pb, i_x, i_mid, i_sp,
        ig, ga, gu, gd, gs_out,
        W, NF, PR, MX, N2, H, GD, PB, XO, MID, SPS, G,
        GT, GP, GB, GJ, GM, GMID, IGB, LGB, OP, RB, CS, XR,
        DW, YR, ZR, RD, CR, SG, SYR, SZR, SRD, SCR,
        load, gs, gr, ss, sr, lo_s, lo_r,
        y_s, y_r, z_s, z_r, c_s, c_r, sy_s, sy_r, sz_s, sz_r, sc_s, sc_r,
    ):
        p = Place(dpn, nz)
        x, y, c, z, j = p.x, p.y, p.c, p.z, p.j
        ex = Exchange(p, OP, RB, CS, XR, gs, gr, ss, sr)
        near, far = x, 1 - x

        places = {
            "D": (lambda l: i_w.at[3 * l + 2], W.at[2]),
            "GD": (lambda l: i_gd.at[l], GD),
            "H": (lambda l: i_h.at[l], H),
            "U": (lambda l: i_w.at[3 * l + 1], W.at[1]),
            "N2": (lambda l: i_n2.at[l], N2),
            "MID": (lambda l: i_mid.at[l], MID),
            "A": (lambda l: i_w.at[3 * l], W.at[0]),
            "PB": (lambda l: i_pb.at[l], PB),
            "PR": (lambda l: i_pr.at[l], PR),
            "MX": (lambda l: i_mx.at[l], MX),
            "NF": (lambda l: i_nf.at[l], NF),
            "X": (lambda l: i_x.at[l], XO),
        }
        names = list(places)

        def fetch(l, name):
            s, d = places[name]
            return pltpu.make_async_copy(s(l), d, load.at[l, names.index(name)])

        fetch_sp = pltpu.make_async_copy(i_sp, SPS, load.at[0, len(names)])
        fetch_sp.start()
        for name in ("H", "D", "GD", "U", "N2", "MID", "A", "PB", "PR", "MX", "NF", "X"):
            fetch(1, name).start()

        GT[...] = jnp.zeros((4 * RP, D), BF)
        for m in range(2):
            GT[pl.ds(pl.multiple_of((2 * m + c) * RP, RC), SEQ), :] = cot[m]
        SG[...] = jnp.zeros((2, 32, TILE), F32)
        p.barrier()
        first = [
            rcopy(GT.at[ex.rows(m, c)], GT.at[ex.rows(m, c)], gs.at[0, m], gr.at[0, m], p.dev(c=1 - c)) for m in range(2)
        ]
        for cp in first:
            cp.start()
        fetch_sp.wait()
        for l in range(2):
            for r in range(2):
                for q in range(4):
                    G[l, r : r + 1, q * TILE : (q + 1) * TILE] = SPS[l, 4 * r + q : 4 * r + q + 1, :]

        def y_part(l, m, k, kz):
            cols = blk(p.zk(kz), TILE)
            return rcopy(
                DW.at[m, blk(p.yk(k), R2), cols], YR.at[m, k - 1, :, cols],
                y_s.at[3 * l + m, k, kz], y_r.at[3 * l + m, k, kz], p.dev(y=p.yk(k)),
            )

        def z_part(l, m, k):
            return rcopy(
                DW.at[m, blk(y, R2), blk(p.zk(k), TILE)], ZR.at[m, k - 1],
                z_s.at[3 * l + m, k], z_r.at[3 * l + m, k], p.dev(z=p.zk(k)),
            )

        order = (2, 1, 3, 0)

        def y_start(l, m):
            for kz in order:
                for k in range(1, Y):
                    y_part(l, m, k, kz).start()

        def y_sum(l, m):
            for kz in order:
                cols = blk(p.zk(kz), TILE)
                for k in range(1, Y):
                    y_part(l, m, k, kz).wait_recv()
                t = DW[m, blk(y, R2), cols].astype(F32)
                for k in range(1, Y):
                    t = t + YR[m, k - 1, :, cols].astype(F32)
                DW[m, blk(y, R2), cols] = t.astype(BF)
                if kz:
                    z_part(l, m, kz).start()

        def c_part(l, m, cp):
            lm = 3 * l + m
            return rcopy(RD.at[lm, cp], CR.at[m, j], c_s.at[lm, cp], c_r.at[m, j], p.dev(x=l, c=cp))

        def z_sum(l, m):
            for k in range(1, nz):
                z_part(l, m, k).wait_recv()
            t = DW[m, blk(y, R2), blk(z, TILE)].astype(F32)
            for k in range(1, nz):
                t = t + ZR[m, k - 1].astype(F32)
            RD[3 * l + m] = t.astype(BF).reshape(2, R, TILE)
            for cp in range(2):
                mine = jnp.logical_and(x == l, c == cp)

                @pl.when(mine)
                def _():
                    pltpu.make_async_copy(RD.at[3 * l + m, cp], CR.at[m, j], c_r.at[m, j]).start()

                @pl.when(jnp.logical_not(mine))
                def _():
                    c_part(l, m, cp).start()

        def reuse(m):
            for kz in range(nz):
                for k in range(1, Y):
                    y_part(1, m, k, kz).wait_send()
                if kz:
                    z_part(1, m, kz).wait_send()

        def s_y(l, k):
            return rcopy(SG.at[l], SYR.at[l, k - 1], sy_s.at[l, k], sy_r.at[l, k], p.dev(y=p.yk(k)))

        def s_z(l, k):
            return rcopy(SRD.at[l], SZR.at[l, k - 1], sz_s.at[l, k], sz_r.at[l, k], p.dev(z=p.zk(k)))

        def s_c(l, cp):
            return rcopy(SRD.at[2 + l], SCR.at[j], sc_s.at[l, cp], sc_r.at[j], p.dev(x=l, c=cp))

        def s_start(l):
            for k in range(1, Y):
                s_y(l, k).start()

        def s_mid(l):
            for k in range(1, Y):
                s_y(l, k).wait_recv()
            SRD[l] = SG[l] + jnp.sum(SYR[l], axis=0)
            for k in range(1, nz):
                s_z(l, k).start()

        def s_end(l):
            for k in range(1, nz):
                s_z(l, k).wait_recv()
            SRD[2 + l] = SRD[l] + jnp.sum(SZR[l], axis=0)
            for cp in range(2):
                mine = jnp.logical_and(x == l, c == cp)

                @pl.when(mine)
                def _():
                    pltpu.make_async_copy(SRD.at[2 + l], SCR.at[j], sc_r.at[j]).start()

                @pl.when(jnp.logical_not(mine))
                def _():
                    s_c(l, cp).start()

        def add_small(l, row, v):
            SG[l, pl.ds(row, 1), :] += v

        def pre(l, h):
            rows_ = half(h)

            def step(n, _):
                cols = blk(n, TILE)
                t = mm(GT[rows_, :], W[2, :, cols], NN) * GD[rows_, cols].astype(F32)
                gp = t.astype(BF)
                GP[rows_, cols] = gp
                add_small(l, 28 + n, jnp.sum(gp.astype(F32), axis=0, keepdims=True))
                return 0

            lax.fori_loop(0, 4, step, 0)

        def project(lhs, m, h):
            rows_ = half(h)

            def step(n, _):
                cols = blk(n, TILE)
                OP[rows_, cols] = mm(lhs[rows_, :], W[m, cols, :], NT).astype(BF)
                return 0

            lax.fori_loop(0, 4, step, 0)

        def weight_grad(m, pairs):
            def step(r, _):
                cols = blk(r, TILE)
                t = mm(pairs[0][0][:, cols], pairs[0][1][...], TN)
                for a, b in pairs[1:]:
                    t = t + mm(a[:, cols], b[...], TN)
                DW[m, cols, :] = t.astype(BF)
                return 0

            lax.fori_loop(0, 4, step, 0)

        def mixed_grad(h):
            rows_ = half(h)

            def step(n, _):
                cols = blk(n, TILE)
                GM[rows_, cols] = mm(GB[rows_, :], W[0, :, cols], NN).astype(BF)
                return 0

            lax.fori_loop(0, 4, step, 0)

        def attend_back(l, h):
            def step(i, _):
                im = 2 * h + i
                rows_ = blk(im, RP)
                for zz in range(4):
                    cols = blk(zz, TILE)
                    t = PR[rows_, cols]
                    q, k, v = t[:, 0:HD], t[:, HD : 2 * HD], t[:, 2 * HD : 3 * HD]
                    gm = GM[rows_, cols][:, 3 * HD : 4 * HD]
                    pb = PB[4 * im + zz]
                    pf = pb.astype(F32)
                    gp = mm(gm, v, NT)
                    cen = jnp.sum(pf * gp, axis=-1, keepdims=True)
                    gsc = (pf * (gp - cen)).astype(BF)
                    gq = mm(gsc, k, NN) * SCALE
                    gk = mm(gsc, q, TN) * SCALE
                    gv = mm(pb, gm, TN)
                    out = jnp.concatenate([gq, gk, gv, jnp.zeros((RP, HD), F32)], axis=1).astype(BF)
                    GJ[rows_, cols] = out
                    add_small(l, 24 + zz, jnp.sum(out.astype(F32), axis=0, keepdims=True))
                return 0

            lax.fori_loop(0, 2, step, 0)

        def fold(v):
            return v[0:8] + v[8:16]

        def put_small(l, row, acc):
            t = jnp.sum(acc, axis=0, keepdims=True)
            for q in range(4):
                add_small(l, 4 * row + q, t[:, q * TILE : (q + 1) * TILE])

        def norm_back(v, g, dy):
            cen = v - jnp.sum(v, axis=-1, keepdims=True) * (1.0 / D)
            rstd = lax.rsqrt(jnp.sum(cen * cen, axis=-1, keepdims=True) * (1.0 / D) + EPS)
            hat = cen * rstd
            dh = dy * g
            a = jnp.sum(dh, axis=-1, keepdims=True) * (1.0 / D)
            b = jnp.sum(dh * hat, axis=-1, keepdims=True) * (1.0 / D)
            return rstd * (dh - a - hat * b), dy * hat

        slot = 2 * x + c

        def own_rows(r):
            return pl.ds(pl.multiple_of(slot * RP + r * RC, RC), RC)

        zero8 = jnp.zeros((8, D), F32)

        for l in (1, 0):
            if l == 1:
                for cp in first:
                    cp.wait_recv()
                fetch(1, "H").wait()
                weight_grad(2, [(GT, H)])
                y_start(1, 2)
                fetch(0, "H").start()
                fetch(1, "D").wait()
                fetch(1, "GD").wait()
                pre(1, far)
                pre(1, near)
                for cp in first:
                    cp.wait_send()
            else:
                gt = ex.gather(GT, 1)
                gt.start()
                z_sum(1, 1)
                y_sum(1, 0)
                fetch(0, "D").wait()
                fetch(0, "GD").wait()
                gt.near()
                pre(0, near)
                gt.pass_on()
                gt.far()
                pre(0, far)
            fetch(l, "U").wait()
            s = 2 * (1 - l)
            project(GP, 1, far)
            ex.send_core(far, s)
            project(GP, 1, near)
            ex.send_core(near, s)
            ex.send_chip(s)
            if l == 1:
                for name in ("D", "GD", "U"):
                    fetch(0, name).start()
                fetch(1, "N2").wait()
                weight_grad(1, [(N2, GP)])
                y_start(1, 1)
                fetch(0, "N2").start()
            else:
                z_sum(1, 0)
                s_end(1)
                reuse(2)
                fetch(0, "H").wait()
                weight_grad(2, [(GT, H)])
                y_start(0, 2)
            ex.wait_sums(s)
            fetch(l, "MID").wait()

            def mid_back(r, acc):
                rs = blk(r, RC)
                dy = ex.sums(r)
                top = GT[own_rows(r), :].astype(F32)
                dx, dg = norm_back(MID[rs, :], G[l, 1:2, :], dy)
                gmid = top + dx
                GMID[rs, :] = gmid
                GB[own_rows(r), :] = gmid.astype(BF)
                return acc[0] + fold(dg), acc[1] + fold(dy), acc[2] + fold(gmid), acc[3] + fold(top)

            acc = lax.fori_loop(0, RP // RC, mid_back, (zero8,) * 4)
            put_small(l, 1, acc[0])
            put_small(l, 4, acc[1])
            put_small(l, 3, acc[2])
            put_small(l, 5, acc[3])
            ex.done(s)
            gb = ex.gather(GB, 2 + (1 - l))
            gb.start()
            if l == 1:
                fetch(0, "MID").start()
                y_sum(1, 2)
            else:
                reuse(1)
                fetch(0, "N2").wait()
                weight_grad(1, [(N2, GP)])
                y_start(0, 1)
            fetch(l, "A").wait()
            fetch(l, "PR").wait()
            fetch(l, "PB").wait()
            gb.near()
            mixed_grad(near)
            gb.pass_on()
            attend_back(l, near)
            if l == 1:
                y_sum(1, 1)
            else:
                y_sum(0, 2)
            gb.far()
            mixed_grad(far)
            attend_back(l, far)
            fetch(l, "MX").wait()
            fetch(l, "NF").wait()
            if l == 0:
                reuse(0)
                weight_grad(0, [(NF, GJ), (GB, MX)])
                y_start(0, 0)
            s = 2 * (1 - l) + 1
            project(GJ, 0, far)
            ex.send_core(far, s)
            project(GJ, 0, near)
            ex.send_core(near, s)
            ex.send_chip(s)
            if l == 1:
                weight_grad(0, [(NF, GJ), (GB, MX)])
                z_sum(1, 2)
                y_start(1, 0)
                for name in ("A", "PB", "PR", "MX", "NF"):
                    fetch(0, name).start()
            else:
                y_sum(0, 1)
                z_sum(0, 2)
            ex.wait_sums(s)
            fetch(l, "X").wait()

            def first_back(r, acc):
                rs = blk(r, RC)
                dy = ex.sums(r)
                dx, dg = norm_back(XO[rs, :].astype(F32), G[l, 0:1, :], dy)
                gx = (GMID[rs, :] + dx).astype(BF)
                IGB[l, rs, :] = gx
                if l == 1:
                    GT[own_rows(r), :] = gx
                return acc[0] + fold(dg), acc[1] + fold(dy)

            acc = lax.fori_loop(0, RP // RC, first_back, (zero8,) * 2)
            put_small(l, 0, acc[0])
            put_small(l, 2, acc[1])
            ex.done(s)
            gb.done()
            if l == 1:
                fetch(0, "X").start()
            else:
                gt.done()
            s_start(l)

            @pl.when(x != l)
            def _():
                rcopy(IGB.at[l], LGB, lo_s, lo_r, p.dev(x=1 - x)).start()

            if l == 1:
                s_mid(1)

        s_mid(0)
        y_sum(0, 0)
        z_sum(0, 1)
        s_end(0)
        z_sum(0, 0)
        cp = rcopy(IGB.at[x], LGB, lo_s, lo_r, p.dev(x=1 - x))
        cp.wait_recv()
        cp.wait_send()
        ig[x] = IGB[x, 0:SEQ, :]
        ig[1 - x] = LGB[0:SEQ, :]
        for m in (2, 1, 0):
            for jj in range(4):
                pltpu.make_async_copy(CR.at[m, jj], CR.at[m, jj], c_r.at[m, jj]).wait()
                t = CR[m, jj].astype(F32)
                if m == 0:
                    ga[jj] = t
                elif m == 1:
                    gu[:, jj * TILE : (jj + 1) * TILE] = t
                else:
                    gd[:, jj * TILE : (jj + 1) * TILE] = t
        for jj in range(4):
            pltpu.make_async_copy(SCR.at[jj], SCR.at[jj], sc_r.at[jj]).wait()
            gs_out[jj] = SCR[jj]
        for m in range(3):
            for kz in range(nz):
                for k in range(1, Y):
                    y_part(0, m, k, kz).wait_send()
                if kz:
                    z_part(0, m, kz).wait_send()
        for l in range(2):
            for k in range(1, Y):
                s_y(l, k).wait_send()
            for k in range(1, nz):
                s_z(l, k).wait_send()
            for cp in range(2):

                @pl.when(jnp.logical_not(jnp.logical_and(x == l, c == cp)))
                def _():
                    s_c(l, cp).wait_send()
                    for m in range(3):
                        c_part(l, m, cp).wait_send()

    full = (4 * RP, D)
    vm = pl.BlockSpec(memory_space=pltpu.VMEM)
    hbm = pl.BlockSpec(memory_space=pl.ANY)
    dma = pltpu.SemaphoreType.DMA
    return pl.pallas_call(
        body,
        out_shape=[
            jax.ShapeDtypeStruct((2, SEQ, D), BF),
            jax.ShapeDtypeStruct((4, R, TILE), F32),
            jax.ShapeDtypeStruct((R, D), F32),
            jax.ShapeDtypeStruct((R, D), F32),
            jax.ShapeDtypeStruct((4, 32, TILE), F32),
        ],
        in_specs=[vm] + [hbm] * 11,
        out_specs=[vm] * 5,
        scratch_shapes=[
            pltpu.VMEM((3, D, D), BF),
            pltpu.VMEM(full, BF), pltpu.VMEM(full, BF), pltpu.VMEM(full, BF),
            pltpu.VMEM(full, BF), pltpu.VMEM(full, BF), pltpu.VMEM(full, BF),
            pltpu.VMEM((16, RP, RP), BF),
            pltpu.VMEM((RP, D), BF),
            pltpu.VMEM((RP, D), F32),
            pltpu.VMEM((2, 32, TILE), F32),
            pltpu.VMEM((2, 8, D), F32),
            pltpu.VMEM(full, BF), pltpu.VMEM(full, BF), pltpu.VMEM(full, BF),
            pltpu.VMEM(full, BF), pltpu.VMEM(full, BF),
            pltpu.VMEM((RP, D), F32),
            pltpu.VMEM((2, RP, D), BF),
            pltpu.VMEM((RP, D), BF),
            pltpu.VMEM(full, BF),
            pltpu.VMEM((2, RP, D), BF),
            pltpu.VMEM((RP, D), BF),
            pltpu.VMEM((RP, D), BF),
            pltpu.VMEM((3, D, D), BF),
            pltpu.VMEM((3, Y - 1, R2, D), BF),
            pltpu.VMEM((3, nz - 1, R2, TILE), BF),
            pltpu.VMEM((6, 2, R, TILE), BF),
            pltpu.VMEM((3, 4, R, TILE), BF),
            pltpu.VMEM((2, 32, TILE), F32),
            pltpu.VMEM((2, Y - 1, 32, TILE), F32),
            pltpu.VMEM((2, nz - 1, 32, TILE), F32),
            pltpu.VMEM((4, 32, TILE), F32),
            pltpu.VMEM((4, 32, TILE), F32),
            dma((2, 13)), dma((4, 3)), dma((4, 3)), dma((4, 3)), dma((4, 3)), dma, dma,
            dma((6, Y, nz)), dma((6, Y, nz)), dma((6, nz)), dma((6, nz)), dma((6, 2)), dma((3, 4)),
            dma((2, Y)), dma((2, Y)), dma((2, nz)), dma((2, nz)), dma((2, 2)), dma((4,)),
        ],
        compiler_params=pltpu.CompilerParams(
            collective_id=1, has_side_effects=True, vmem_limit_bytes=VMEM_LIMIT
        ),
    )


def small_pack(norm_gains, row_shifts, head_bias, unit_bias, dpn, nz):
    dp, z = lax.axis_index("dp"), lax.axis_index("tensor")
    rows = jnp.concatenate([norm_gains[0], row_shifts[0]], axis=0)
    w = rows.shape[1]
    rows = lax.dynamic_update_slice(jnp.zeros((6, D), BF), rows, (0, (dp * nz + z) * w)).reshape(1, 24, TILE)
    hw, uw = head_bias.shape[3], unit_bias.shape[2]
    head = jnp.zeros((4, 4, TILE), BF)
    head = lax.dynamic_update_slice(head, head_bias[0, 0][:, None], (0, z, dp * hw))
    head = lax.dynamic_update_slice(head, head_bias[0, 1][:, None], (0, z, 2 * HD + dp * hw))
    unit = lax.dynamic_update_slice(jnp.zeros((4, 4, TILE), BF), unit_bias[0][:, None], (0, z, dp * uw))
    return jnp.concatenate([jnp.broadcast_to(rows, (4, 24, TILE)), head, unit], axis=1)


def solution(mesh):
    dpn, nz = mesh.shape["dp"], mesh.shape["tensor"]

    def on_device(
        images_in, cotangent, w_qkv, w_out, w_up, w_down, norm_gains, row_shifts, head_bias, unit_bias
    ):
        R = w_up.shape[1]
        qkv = w_qkv[0].reshape(R, 3, 4, HD).transpose(2, 0, 1, 3).reshape(4, R, 3 * HD)
        wo = w_out[0].reshape(R, 4, HD).transpose(1, 0, 2)
        wa = jnp.concatenate([qkv, wo], axis=2)
        sp = small_pack(norm_gains, row_shifts, head_bias, unit_bias, dpn, nz)
        res = forward_kernel(dpn, nz, R)(images_in, wa, w_up[0], w_down[0], sp)
        ig, ga, gu, gd, gs = backward_kernel(dpn, nz, R)(cotangent, *res[1:])
        dp, z = lax.axis_index("dp"), lax.axis_index("tensor")
        g_qkv = ga[:, :, : 3 * HD].reshape(4, R, 3, HD).transpose(1, 2, 0, 3).reshape(w_qkv.shape)
        g_out = ga[:, :, 3 * HD :].transpose(1, 0, 2).reshape(w_out.shape)
        w, hw, uw = norm_gains.shape[2], head_bias.shape[3], unit_bias.shape[2]
        rows = lax.dynamic_slice(jnp.sum(gs[:, :24], axis=0).reshape(6, D), (0, (dp * nz + z) * w), (6, w))
        head = lax.dynamic_slice(gs, (0, 24 + z, 0), (4, 1, TILE))[:, 0]
        unit = lax.dynamic_slice(gs, (0, 28 + z, dp * uw), (4, 1, uw))[:, 0]
        g_head = jnp.stack([lax.dynamic_slice(head, (0, o + dp * hw), (4, hw)) for o in (0, 2 * HD)])
        return (
            res[0][None], ig[None], g_qkv, g_out, gu[None], gd[None],
            rows[None, :2], rows[None, 2:], g_head[None], unit[None],
        )

    in_specs = (
        P(None, ("dp", "tensor"), None),
        P(None, ("dp", "tensor"), None),
        P("section", "dp", None, "tensor"),
        P("section", "dp", "tensor"),
        P("section", "dp", "tensor"),
        P("section", "dp", "tensor"),
        P("section", None, ("dp", "tensor")),
        P("section", None, ("dp", "tensor")),
        P("section", None, "tensor", "dp"),
        P("section", "tensor", "dp"),
    )
    out_specs = (
        P("section", None, ("dp", "tensor"), None),
        P("section", None, ("dp", "tensor"), None),
        P("section", "dp", None, "tensor"),
        P("section", "dp", "tensor"),
        P("section", "dp", "tensor"),
        P("section", "dp", "tensor"),
        P("section", None, ("dp", "tensor")),
        P("section", None, ("dp", "tensor")),
        P("section", None, "tensor", "dp"),
        P("section", "tensor", "dp"),
    )
    return jax.shard_map(
        on_device, mesh=mesh, in_specs=in_specs, out_specs=out_specs, check_vma=False
    )
```

```python
import math
import types

import jax
import jax.numpy as jnp
from jax import lax
from jax.experimental import pallas as pl
from jax.experimental.pallas import tpu as pltpu
from jax.sharding import PartitionSpec as P

D = 1024
HD = 64
SEQ = 197
RP = 208
RC = 16
TILE = 256
SCALE = 0.125
EPS = 1e-06
MESH = pl.DeviceIdType.MESH
BF = jnp.bfloat16
F32 = jnp.float32
NN = (((1,), (0,)), ((), ()))
NT = (((1,), (1,)), ((), ()))
TN = (((0,), (0,)), ((), ()))
VMEM_LIMIT = 62 * 2**20


def mm(a, b, dims):
    return lax.dot_general(a, b, dims, preferred_element_type=F32)


def blk(i, size):
    if isinstance(i, int):
        return pl.ds(i * size, size)
    return pl.ds(pl.multiple_of(i * size, size), size)


class Place:
    def __init__(self, dpn, nz):
        self.Y, self.nz = dpn // 2, nz
        self.x = lax.axis_index("section")
        dp = lax.axis_index("dp")
        self.z = lax.axis_index("tensor")
        self.y, self.c = dp // 2, lax.rem(dp, 2)
        self.j = 2 * self.x + self.c

    def dev(self, x=None, y=None, c=None, z=None):
        x = self.x if x is None else x
        y = self.y if y is None else y
        c = self.c if c is None else c
        z = self.z if z is None else z
        return (x, 2 * y + c, z)

    def cell(self, k):
        jp = lax.rem(self.j + k, 4)
        return jp, jp // 2, lax.rem(jp, 2)

    def yk(self, k):
        return lax.rem(self.y + k, self.Y)

    def zk(self, k):
        return lax.rem(self.z + k, self.nz)

    def barrier(self):
        bar = pltpu.get_barrier_semaphore()
        n = 0
        for k in range(1, 4):
            _, xp, cp = self.cell(k)
            pl.semaphore_signal(bar, inc=1, device_id=self.dev(x=xp, c=cp), device_id_type=MESH)
            n += 1
        for k in range(1, self.nz):
            pl.semaphore_signal(bar, inc=1, device_id=self.dev(z=self.zk(k)), device_id_type=MESH)
            n += 1
        for k in range(1, self.Y):
            pl.semaphore_signal(bar, inc=1, device_id=self.dev(y=self.yk(k)), device_id_type=MESH)
            n += 1
        pl.semaphore_wait(bar, n)


def rcopy(src, dst, ss, rs, dev):
    return pltpu.make_async_remote_copy(
        src_ref=src, dst_ref=dst, send_sem=ss, recv_sem=rs, device_id=dev, device_id_type=MESH
    )


def norm_row(v, g, b):
    cen = v - jnp.sum(v, axis=-1, keepdims=True) * (1.0 / D)
    var = jnp.sum(cen * cen, axis=-1, keepdims=True) * (1.0 / D)
    return cen * lax.rsqrt(var + EPS) * g + b


def norm_back(v, g, dy):
    cen = v - jnp.sum(v, axis=-1, keepdims=True) * (1.0 / D)
    rstd = lax.rsqrt(jnp.sum(cen * cen, axis=-1, keepdims=True) * (1.0 / D) + EPS)
    hat = cen * rstd
    dh = dy * g
    a = jnp.sum(dh, axis=-1, keepdims=True) * (1.0 / D)
    b = jnp.sum(dh * hat, axis=-1, keepdims=True) * (1.0 / D)
    return rstd * (dh - a - hat * b), dy * hat


def fold(v):
    return v[0:8] + v[8:16]


def half(g):
    return blk(g, 2 * RP)


def row(g, m):
    return blk(2 * g + m, RP)


def both_layers(dpn, nz, rows):
    Y, R = dpn // 2, rows
    R2 = 2 * R
    full = (4 * RP, D)
    dma = pltpu.SemaphoreType.DMA
    inputs = ["img", "cot", "wa", "wu", "wd", "sp"]
    outputs = {
        "lo": ((2, SEQ, D), BF), "ig": ((2, SEQ, D), BF), "ga": ((4, R, TILE), F32), "gu": ((R, D), F32),
        "gd": ((R, D), F32), "gs_out": ((4, 32, TILE), F32),
    }
    spilled = {"NF": full, "PR": full, "N2": full, "H": full, "GD": full, "PB": (16, RP, RP)}
    vmem = {
        "W": ((6, D, D), BF), "DX": ((D, D), BF), "SPB": ((2, Y, nz, 2, 32, TILE), BF), "SPS": ((2, 32, TILE), F32),
        "G": ((2, 8, D), F32), "NF": (full, BF), "PR": (full, BF), "N2": (full, BF), "H": (full, BF), "GD": (full, BF),
        "PB": ((16, RP, RP), BF), "MX": (full, BF), "GT": (full, BF), "OP": (full, BF), "RB": ((2, 2, RP, D), BF),
        "CS": ((2, RP, D), BF), "XR": ((2, RP, D), BF), "XO": ((2, RP, D), BF), "MID": ((2, RP, D), F32),
        "OUT": ((2, RP, D), BF), "LOB": ((RP, D), BF), "GMID": ((RP, D), F32), "IGB": ((2, RP, D), BF),
        "LGB": ((RP, D), BF), "YR": ((3, Y - 1, R2, D), BF), "ZR": ((6, nz - 1, R2, TILE), BF),
        "RD": ((6, 2, R, TILE), BF), "CR": ((3, 4, R, TILE), BF), "SG": ((2, 32, TILE), F32),
        "SYR": ((2, Y - 1, 32, TILE), F32), "SZR": ((2, nz - 1, 32, TILE), F32), "SRD": ((4, 32, TILE), F32),
        "SCR": ((4, 32, TILE), F32),
    }
    sems = {
        "red_s": (3, 4), "red_r": (6, 2), "fz_s": (6, 4), "fz_r": (6, 4), "fy_s": (6, 4, Y), "fy_r": (6, 4, Y),
        "ps": (4 + 2 * nz + 2 * Y,), "pr": (6, max(nz, Y, 2)), "gs": (8, 3), "gr": (8, 3), "ss": (8, 3), "sr": (8, 3),
        "lo_s": (2,), "lo_r": (2,), "keep": (2, 6), "y_s": (6, Y, nz), "y_r": (6, Y, nz), "z_s": (6, nz), "z_r": (6, nz),
        "c_s": (6, 2), "c_r": (3, 4), "sy_s": (2, Y), "sy_r": (2, Y), "sz_s": (2, nz), "sz_r": (2, nz), "sc_s": (2, 2),
        "sc_r": (4,),
    }
    names = inputs + list(outputs) + ["o_" + n for n in spilled] + list(vmem) + list(sems)

    def body(*refs):
        t = types.SimpleNamespace(**dict(zip(names, refs)))
        p = Place(dpn, nz)
        x, y, c, z, j = p.x, p.y, p.c, p.z, p.j
        near, far = x, 1 - x
        W, OP, RB, CS, XR = t.W, t.OP, t.RB, t.CS, t.XR

        def core_part(g, m, s):
            return rcopy(OP.at[row(g, m)], RB.at[int(s == 3), m], t.ss.at[s, m], t.sr.at[s, m], p.dev(c=1 - c))

        def chip_part(s):
            k = int(s == 3)
            return rcopy(CS.at[k], XR.at[k], t.ss.at[s, 2], t.sr.at[s, 2], p.dev(x=1 - x))

        def rs_out(g, s):
            @pl.when(c != g)
            def _():
                core_part(g, far, s).start()
                core_part(g, near, s).start()

            @pl.when(c == g)
            def _():
                core_part(g, far, s).wait_recv()
                k = int(s == 3)
                CS[k] = (OP[row(g, far), :].astype(F32) + RB[k, far].astype(F32)).astype(BF)
                chip_part(s).start()

        def rs_in(g, s, fn):
            @pl.when(c == g)
            def _():
                core_part(g, near, s).wait_recv()
                chip_part(s).wait_recv()
                fn()

        def rs_done(g, s):
            @pl.when(c != g)
            def _():
                for m in range(2):
                    core_part(g, m, s).wait_send()

            @pl.when(c == g)
            def _():
                chip_part(s).wait_send()

        def sums(g, r):
            rs = blk(r, RC)
            own = OP[pl.ds(pl.multiple_of((2 * g + x) * RP + r * RC, RC), RC), :].astype(F32)
            return own + RB[0, x, rs, :].astype(F32) + XR[0, rs, :].astype(F32)

        def ag_part(buf, g, s, k):
            b = buf.at[row(g, far if k == 2 else near)]
            return rcopy(b, b, t.gs.at[s, k], t.gr.at[s, k], p.dev(x=1 - x) if k == 1 else p.dev(c=1 - c))

        def ag_send(buf, g, s):
            ag_part(buf, g, s, 1).start()
            ag_part(buf, g, s, 0).start()

        def ag_mid(buf, g, s):
            @pl.when(c == g)
            def _():
                ag_part(buf, g, s, 1).wait_recv()
                ag_part(buf, g, s, 2).start()

        def ag_in(buf, g, s):
            @pl.when(c != g)
            def _():
                ag_part(buf, g, s, 0).wait_recv()
                ag_part(buf, g, s, 2).wait_recv()

        def ag_done(buf, s):
            for g in range(2):

                @pl.when(c == g)
                def _():
                    for k in range(3):
                        ag_part(buf, g, s, k).wait_send()

        def ag_local(buf, s):
            return [
                rcopy(buf.at[row(c, m)], buf.at[row(c, m)], t.gs.at[s, m], t.gr.at[s, m], p.dev(c=1 - c))
                for m in range(2)
            ]

        def small_red(k):
            jp, xp, cp = p.cell(k)
            dst = t.SPB.at[x, y, z, c]
            if k == 0:
                return pltpu.make_async_copy(t.sp.at[jp], dst, t.pr.at[x, c])
            return rcopy(t.sp.at[jp], dst, t.ps.at[k], t.pr.at[x, c], p.dev(x=xp, c=cp))

        def small_z(l, k):
            b = t.SPB.at[l, y, z]
            return rcopy(b, b, t.ps.at[4 + l * nz + k], t.pr.at[2 + l, k], p.dev(z=p.zk(k)))

        def small_y(l, k):
            b = t.SPB.at[l, y]
            return rcopy(b, b, t.ps.at[4 + 2 * nz + l * Y + k], t.pr.at[4 + l, k], p.dev(y=p.yk(k)))

        src = (t.wa, t.wu, t.wd)
        inner = lax.rem((z + 1) // 2, 2)
        mate = z + 1 - 2 * lax.rem(z, 2)
        cross = 2 - z // 2
        holds = (z, mate, cross, 3 - 3 * (z // 2))

        def red(m, k):
            jp, xp, cp = p.cell(k)
            b = src[m].at[jp] if m == 0 else src[m].at[:, blk(jp, TILE)]
            dst = W.at[x * 3 + m, blk(2 * y + c, R), blk(z, TILE)]
            if k == 0:
                return pltpu.make_async_copy(b, dst, t.red_r.at[x * 3 + m, c])
            return rcopy(b, dst, t.red_s.at[m, k], t.red_r.at[x * 3 + m, c], p.dev(x=xp, c=cp))

        def chunk(lm, k):
            return W.at[lm, blk(y, R2), blk(holds[k], TILE)]

        def wz(lm, k):
            b = chunk(lm, 0)
            if k == 1:
                return rcopy(b, b, t.fz_s.at[lm, 0], t.fz_r.at[lm, 1], p.dev(z=mate))
            return rcopy(b, b, t.fz_s.at[lm, 1], t.fz_r.at[lm, 3 - inner], p.dev(z=cross))

        def wrelay(lm, k):
            b = chunk(lm, k)
            return rcopy(b, b, t.fz_s.at[lm, k], t.fz_r.at[lm, k], p.dev(z=mate))

        def wy(lm, k, ky):
            b = chunk(lm, k)
            return rcopy(b, b, t.fy_s.at[lm, k, ky], t.fy_r.at[lm, k, ky], p.dev(y=p.yk(ky)))

        def release(lm):
            for cs in range(2):
                b = W.at[lm, blk(2 * y + cs, R), blk(z, TILE)]
                pltpu.make_async_copy(b, b, t.red_r.at[lm, cs]).wait()
            wz(lm, 2).start()
            wz(lm, 1).start()
            for ky in range(1, Y):
                wy(lm, 0, ky).start()

        def hand_on(lm, k):
            pltpu.make_async_copy(chunk(lm, k), chunk(lm, k), t.fz_r.at[lm, k]).wait()
            if k >= 2:

                @pl.when(inner == 1)
                def _():
                    wrelay(lm, k).start()

            for ky in range(1, Y):
                wy(lm, k, ky).start()
            if k == 3 and lm + 2 < 6:
                release(lm + 2)

        queue = [(lm, k) for lm in range(6) for k in (1, 2, 3)]
        handed = []

        def pump(n=1):
            for _ in range(n):
                if queue:
                    lm, k = queue.pop(0)
                    hand_on(lm, k)
                    handed.append((lm, k))

        def ready(lm, k):
            while k and (lm, k) not in handed:
                pump()
            for ky in range(1, Y):
                wy(lm, k, ky).wait_recv()

        def where(l, m):
            return t.DX if (l, m) == (1, 2) else W.at[3 * l + m]

        def y_part(l, m, k, kz):
            cols = blk(p.zk(kz), TILE)
            return rcopy(
                where(l, m).at[blk(p.yk(k), R2), cols], t.YR.at[m, k - 1, :, cols],
                t.y_s.at[3 * l + m, k, kz], t.y_r.at[3 * l + m, k, kz], p.dev(y=p.yk(k)),
            )

        def z_part(l, m, k):
            return rcopy(
                where(l, m).at[blk(y, R2), blk(p.zk(k), TILE)], t.ZR.at[3 * l + m, k - 1],
                t.z_s.at[3 * l + m, k], t.z_r.at[3 * l + m, k], p.dev(z=p.zk(k)),
            )

        order = (2, 1, 3, 0)

        begun = set()

        def y_start(l, m):
            begun.add((l, m))
            for kz in order:
                for k in range(1, Y):
                    y_part(l, m, k, kz).start()

        def y_sum(l, m, kz):
            cols = blk(p.zk(kz), TILE)
            buf = where(l, m)
            for k in range(1, Y):
                y_part(l, m, k, kz).wait_recv()
            v = buf[blk(y, R2), cols].astype(F32)
            for k in range(1, Y):
                v = v + t.YR[m, k - 1, :, cols].astype(F32)
            buf[blk(y, R2), cols] = v.astype(BF)
            if kz:
                z_part(l, m, kz).start()

        def c_part(l, m, cp):
            lm = 3 * l + m
            return rcopy(t.RD.at[lm, cp], t.CR.at[m, j], t.c_s.at[lm, cp], t.c_r.at[m, j], p.dev(x=l, c=cp))

        def to_owner(l, remote, local):
            for cp in range(2):
                mine = jnp.logical_and(x == l, c == cp)

                @pl.when(mine)
                def _():
                    local(cp).start()

                @pl.when(jnp.logical_not(mine))
                def _():
                    remote(cp).start()

        def z_sum(l, m):
            for k in range(1, nz):
                z_part(l, m, k).wait_recv()
            lm = 3 * l + m
            v = where(l, m)[blk(y, R2), blk(z, TILE)].astype(F32)
            for k in range(1, nz):
                v = v + t.ZR[lm, k - 1].astype(F32)
            t.RD[lm] = v.astype(BF).reshape(2, R, TILE)
            to_owner(
                l, lambda cp: c_part(l, m, cp),
                lambda cp: pltpu.make_async_copy(t.RD.at[lm, cp], t.CR.at[m, j], t.c_r.at[m, j]),
            )

        steps = []
        for n in range(6):
            l, m = 1 - n // 3, 2 - n % 3
            steps += [(y_sum, (l, m, kz)) for kz in order]
            if n:
                steps.append((z_sum, (1 - (n - 1) // 3, 2 - (n - 1) % 3)))
        steps.append((z_sum, (0, 0)))

        def push(n=1):
            for _ in range(n):
                if steps and steps[0][1][:2] in begun:
                    f, a = steps.pop(0)
                    f(*a)

        def push_through(f, l, m):
            while any(g is f and a[:2] == (l, m) for g, a in steps):
                push()

        def s_y(l, k):
            return rcopy(t.SG.at[l], t.SYR.at[l, k - 1], t.sy_s.at[l, k], t.sy_r.at[l, k], p.dev(y=p.yk(k)))

        def s_z(l, k):
            return rcopy(t.SRD.at[l], t.SZR.at[l, k - 1], t.sz_s.at[l, k], t.sz_r.at[l, k], p.dev(z=p.zk(k)))

        def s_c(l, cp):
            return rcopy(t.SRD.at[2 + l], t.SCR.at[j], t.sc_s.at[l, cp], t.sc_r.at[j], p.dev(x=l, c=cp))

        def s_start(l):
            for k in range(1, Y):
                s_y(l, k).start()

        def s_mid(l):
            for k in range(1, Y):
                s_y(l, k).wait_recv()
            t.SRD[l] = t.SG[l] + jnp.sum(t.SYR[l], axis=0)
            for k in range(1, nz):
                s_z(l, k).start()

        def s_end(l):
            for k in range(1, nz):
                s_z(l, k).wait_recv()
            t.SRD[2 + l] = t.SRD[l] + jnp.sum(t.SZR[l], axis=0)
            to_owner(
                l, lambda cp: s_c(l, cp), lambda cp: pltpu.make_async_copy(t.SRD.at[2 + l], t.SCR.at[j], t.sc_r.at[j])
            )

        kept = list(spilled)

        def save(name):
            i = kept.index(name)
            return pltpu.make_async_copy(getattr(t, name), getattr(t, "o_" + name), t.keep.at[0, i])

        def fetch(name):
            i = kept.index(name)
            return pltpu.make_async_copy(getattr(t, "o_" + name), getattr(t, name), t.keep.at[1, i])

        def add_small(l, r, v):
            t.SG[l, pl.ds(r, 1), :] += v

        def put_small(l, r, acc):
            v = jnp.sum(acc, axis=0, keepdims=True)
            for q in range(4):
                add_small(l, 4 * r + q, v[:, q * TILE : (q + 1) * TILE])

        def own_rows(g, r):
            return pl.ds(pl.multiple_of((2 * g + x) * RP + r * RC, RC), RC)

        def attend(l, g, zz):
            rows_, cols = half(g), blk(zz, TILE)
            v = mm(t.NF[rows_, :], W[3 * l, :, cols], NN)
            t.PR[rows_, cols] = (v + t.SPS[l, pl.ds(24 + zz, 1), :]).astype(BF)
            live = lax.broadcasted_iota(jnp.int32, (RP, RP), 1) < SEQ
            for i in range(2):
                im = 2 * g + i
                b = t.PR[row(g, i), cols]
                q, k, v = b[:, 0:HD], b[:, HD : 2 * HD], b[:, 2 * HD : 3 * HD]
                s = jnp.where(live, mm(q, k, NT) * SCALE, -1e30)
                w = jnp.exp(s - jnp.max(s, axis=-1, keepdims=True))
                pb = (w * (1.0 / jnp.sum(w, axis=-1, keepdims=True))).astype(BF)
                t.PB[4 * im + zz] = pb
                o = mm(pb, v, NN).astype(BF)
                t.MX[row(g, i), cols] = jnp.concatenate([jnp.zeros((RP, 3 * HD), BF), o], axis=1)
                t.PR[row(g, i), cols] = jnp.concatenate([b[:, : 3 * HD], o], axis=1)

        def project(lhs, lm, g):
            rows_ = half(g)

            def step(n, _):
                cols = blk(n, TILE)
                OP[rows_, cols] = mm(lhs[rows_, :], W[lm, cols, :], NT).astype(BF)
                return 0

            lax.fori_loop(0, 4, step, 0)

        def up(l, g, zz):
            rows_, cols = half(g), blk(zz, TILE)
            u = mm(t.N2[rows_, :], W[3 * l + 1, :, cols], NN) + t.SPS[l, pl.ds(28 + zz, 1), :]
            cdf = 0.5 + 0.5 * lax.erf(u * (1.0 / math.sqrt(2.0)))
            t.H[rows_, cols] = (u * cdf).astype(BF)
            t.GD[rows_, cols] = (cdf + u * jnp.exp(-0.5 * u * u) * (1.0 / math.sqrt(2.0 * math.pi))).astype(BF)

        def pre(l, g):
            rows_ = half(g)

            def step(n, _):
                cols = blk(n, TILE)
                v = mm(t.GT[rows_, :], W[3 * l + 2, :, cols], NN) * t.GD[rows_, cols].astype(F32)
                gp = v.astype(BF)
                t.GD[rows_, cols] = gp
                add_small(l, 28 + n, jnp.sum(gp.astype(F32), axis=0, keepdims=True))
                return 0

            lax.fori_loop(0, 4, step, 0)

        def weight_grad(buf, pairs):
            def step(r, _):
                cols = blk(r, TILE)
                v = mm(pairs[0][0][:, cols], pairs[0][1][...], TN)
                for a, b in pairs[1:]:
                    v = v + mm(a[:, cols], b[...], TN)
                buf[cols, :] = v.astype(BF)
                return 0

            lax.fori_loop(0, 4, step, 0)

        def attend_back(l, g):
            rows_ = half(g)

            def mixed(n, _):
                cols = blk(n, TILE)
                t.H[rows_, cols] = mm(t.MX[rows_, :], W[3 * l, :, cols], NN).astype(BF)
                return 0

            lax.fori_loop(0, 4, mixed, 0)

            def step(i, _):
                im = 2 * g + i
                ri = blk(im, RP)
                for zz in range(4):
                    cols = blk(zz, TILE)
                    b = t.PR[ri, cols]
                    q, k, v = b[:, 0:HD], b[:, HD : 2 * HD], b[:, 2 * HD : 3 * HD]
                    gm = t.H[ri, cols][:, 3 * HD : 4 * HD]
                    pb = t.PB[4 * im + zz]
                    pf = pb.astype(F32)
                    gp = mm(gm, v, NT)
                    cen = jnp.sum(pf * gp, axis=-1, keepdims=True)
                    gsc = (pf * (gp - cen)).astype(BF)
                    gq = mm(gsc, k, NN) * SCALE
                    gk = mm(gsc, q, TN) * SCALE
                    gv = mm(pb, gm, TN)
                    out = jnp.concatenate([gq, gk, gv, jnp.zeros((RP, HD), F32)], axis=1).astype(BF)
                    t.H[ri, cols] = out
                    t.PR[ri, cols] = jnp.concatenate([jnp.zeros((RP, 3 * HD), BF), b[:, 3 * HD :]], axis=1)
                    add_small(l, 24 + zz, jnp.sum(out.astype(F32), axis=0, keepdims=True))
                return 0

            lax.fori_loop(0, 2, step, 0)

        def rows_loop(step, init=0):
            return lax.fori_loop(0, RP // RC, step, init)

        t.XO[...] = jnp.zeros((2, RP, D), BF)
        t.GT[...] = jnp.zeros(full, BF)
        for m in range(2):
            t.XO[m, 0:SEQ, :] = t.img[m]
            t.GT[pl.ds(pl.multiple_of((2 * c + m) * RP, RC), SEQ), :] = t.cot[m]
        t.SG[...] = jnp.zeros((2, 32, TILE), F32)
        p.barrier()
        for k in range(4):
            small_red(k).start()
        for m in range(3):
            for k in (1, 2, 3, 0):
                red(m, k).start()
        for l in range(2):
            for cs in range(2):
                b = t.SPB.at[l, y, z, cs]
                pltpu.make_async_copy(b, b, t.pr.at[l, cs]).wait()
            for k in range(1, nz):
                small_z(l, k).start()
        release(0)
        for l in range(2):
            for k in range(1, nz):
                small_z(l, k).wait_recv()
            for k in range(1, Y):
                small_y(l, k).start()
        for l in range(2):
            for k in range(1, Y):
                small_y(l, k).wait_recv()
            t.SPS[l] = jnp.sum(t.SPB[l].astype(F32).reshape(Y * nz * 2, 32, TILE), axis=0)
            for r in range(6):
                for q in range(4):
                    t.G[l, r : r + 1, q * TILE : (q + 1) * TILE] = t.SPS[l, 4 * r + q : 4 * r + q + 1, :]

        def ln(l, g, b, load, buf, at):
            gain, shift = t.G[l, g : g + 1, :], t.G[l, b : b + 1, :]

            def step(r, _):
                buf[at(r), :] = norm_row(load(r), gain, shift).astype(BF)
                return 0

            rows_loop(step)

        for m in range(2):
            ln(
                0, 0, 2, lambda r, m=m: t.XO[m, blk(r, RC), :].astype(F32), t.NF,
                lambda r, m=m: pl.ds(pl.multiple_of((2 * c + m) * RP + r * RC, RC), RC),
            )
        first = ag_local(t.NF, 0)
        for cp in first:
            cp.start()
        tops = ag_local(t.GT, 4)
        for cp in tops:
            cp.start()
        release(1)
        pump(1)
        for cp in first:
            cp.wait_recv()

        for l in range(2):
            A, U, DN = 3 * l, 3 * l + 1, 3 * l + 2
            s = 2 * l
            if l:
                ag_in(t.NF, 0, 2)
            for k in range(4):
                ready(A, k)
                attend(l, 0, holds[k])
                if l == 0 or k < 2:
                    pump()
            if l:
                rs_done(0, 1)
                rs_done(1, 1)
            project(t.MX, A, 0)
            rs_out(0, s)
            if l:
                ag_mid(t.NF, 1, 2)
                ag_in(t.NF, 1, 2)
            for k in range(4):
                attend(l, 1, holds[k])
                if k % 2:
                    pump()
            project(t.MX, A, 1)
            rs_out(1, s)
            if l == 0:
                for cp in first:
                    cp.wait_send()
                for name in ("NF", "PR", "PB"):
                    save(name).start()
            else:
                ag_done(t.NF, 2)

            def second(g):
                gain, shift, bias = t.G[l, 1:2, :], t.G[l, 4:5, :], t.G[l, 3:4, :]

                def step(r, _):
                    rs = blk(r, RC)
                    v = t.XO[x, rs, :] if l == 0 else t.OUT[0, rs, :]
                    mid = v.astype(F32) + sums(g, r) + bias
                    t.MID[l, rs, :] = mid
                    t.N2[own_rows(g, r), :] = norm_row(mid, gain, shift).astype(BF)
                    return 0

                rows_loop(step)
                ag_send(t.N2, g, 1 + 2 * l)

            pump()
            for g in range(2):
                rs_in(g, s, lambda g=g: second(g))
            pump()
            ag_mid(t.N2, 0, 1 + 2 * l)
            ag_in(t.N2, 0, 1 + 2 * l)
            if l:
                save("H").wait()
                save("GD").wait()
            for k in range(4):
                ready(U, k)
                up(l, 0, holds[k])
            ag_mid(t.N2, 1, 1 + 2 * l)
            pump()
            ag_in(t.N2, 1, 1 + 2 * l)
            for k in range(4):
                up(l, 1, holds[k])
            pump()
            ag_done(t.N2, 1 + 2 * l)
            rs_done(0, s)
            rs_done(1, s)
            if l == 0:
                for name in ("N2", "H", "GD"):
                    save(name).start()
                for name in ("NF", "PR", "PB"):
                    save(name).wait()
            else:
                for cp in tops:
                    cp.wait_recv()
                weight_grad(t.DX, [(t.GT, t.H)])
                y_start(1, 2)
            for k in range(4):
                ready(DN, k)
            s = 2 * l + 1
            project(t.H, DN, 0)
            rs_out(0, s)
            pump()
            project(t.H, DN, 1)
            rs_out(1, s)
            pump()
            if l == 0:
                save("N2").wait()

                def last(g):
                    gain, shift, bias = t.G[1, 0:1, :], t.G[1, 2:3, :], t.G[0, 5:6, :]

                    def step(r, _):
                        rs = blk(r, RC)
                        o = (t.MID[0, rs, :] + sums(g, r) + bias).astype(BF)
                        t.OUT[0, rs, :] = o
                        t.NF[own_rows(g, r), :] = norm_row(o.astype(F32), gain, shift).astype(BF)
                        return 0

                    rows_loop(step)
                    ag_send(t.NF, g, 2)

                for g in range(2):
                    rs_in(g, s, lambda g=g: last(g))
                pump()
                ag_mid(t.NF, 0, 2)

                @pl.when(x != 0)
                def _():
                    rcopy(t.OUT.at[0], t.LOB, t.lo_s.at[0], t.lo_r.at[0], p.dev(x=1 - x)).start()
            else:
                for g in range(2):

                    @pl.when(c == g)
                    def _():
                        def step(r, _):
                            rs = blk(r, RC)
                            t.GMID[rs, :] = t.MID[1, rs, :] + OP[own_rows(g, r), :].astype(F32) + t.G[1, 5:6, :]
                            return 0

                        rows_loop(step)

        for k in range(1, 4):
            small_red(k).wait_send()
        for l in range(2):
            for k in range(1, nz):
                small_z(l, k).wait_send()
            for k in range(1, Y):
                small_y(l, k).wait_send()
        for m in range(3):
            for k in range(1, 4):
                red(m, k).wait_send()
        for lm in range(6):
            wz(lm, 1).wait_send()
            wz(lm, 2).wait_send()
            for k in (2, 3):

                @pl.when(inner == 1)
                def _():
                    wrelay(lm, k).wait_send()

            for k in range(4):
                for ky in range(1, Y):
                    wy(lm, k, ky).wait_send()

        def final_out(g):
            def step(r, _):
                rs = blk(r, RC)
                v = t.GMID[rs, :] + RB[1, x, rs, :].astype(F32) + XR[1, rs, :].astype(F32)
                t.OUT[1, rs, :] = v.astype(BF)
                return 0

            rows_loop(step)

        zero8 = jnp.zeros((8, D), F32)
        for l in (1, 0):
            A, U, DN = 3 * l, 3 * l + 1, 3 * l + 2
            s = 4 + 2 * (1 - l)
            if l == 0:
                ag_in(t.GT, 0, 6)
                fetch("GD").wait()
            rs_done(0, s - 1)
            rs_done(1, s - 1)
            pre(l, 0)
            project(t.GD, U, 0)
            rs_out(0, s)
            push()
            if l == 0:
                ag_mid(t.GT, 1, 6)
                ag_in(t.GT, 1, 6)
            pre(l, 1)
            project(t.GD, U, 1)
            rs_out(1, s)
            push()
            if l == 1:
                for cp in tops:
                    cp.wait_send()
                weight_grad(W.at[U], [(t.N2, t.GD)])
                y_start(1, 1)
                fetch("N2").start()
                fetch("GD").start()
                for g in range(2):
                    rs_in(g, 3, lambda g=g: final_out(g))
                push()

                @pl.when(x != 1)
                def _():
                    rcopy(t.OUT.at[1], t.LOB, t.lo_s.at[0], t.lo_r.at[0], p.dev(x=1 - x)).start()
            else:
                ag_done(t.GT, 6)
                fetch("H").wait()
                push_through(y_sum, 1, 0)
                weight_grad(W.at[DN], [(t.GT, t.H)])
                y_start(0, 2)

            def mid_back(g):
                def step(r, acc):
                    rs = blk(r, RC)
                    dy = sums(g, r)
                    top = t.GT[own_rows(g, r), :].astype(F32)
                    dx, dg = norm_back(t.MID[l, rs, :], t.G[l, 1:2, :], dy)
                    gmid = top + dx
                    t.GMID[rs, :] = gmid
                    t.MX[own_rows(g, r), :] = gmid.astype(BF)
                    return acc[0] + fold(dg), acc[1] + fold(dy), acc[2] + fold(gmid), acc[3] + fold(top)

                acc = rows_loop(step, (zero8,) * 4)
                put_small(l, 1, acc[0])
                put_small(l, 4, acc[1])
                put_small(l, 3, acc[2])
                put_small(l, 5, acc[3])
                ag_send(t.MX, g, s + 1)

            for g in range(2):
                rs_in(g, s, lambda g=g: mid_back(g))
            push()
            if l == 0:
                fetch("N2").wait()
                weight_grad(W.at[U], [(t.N2, t.GD)])
                y_start(0, 1)
                for name in ("PR", "PB"):
                    fetch(name).wait()
            ag_mid(t.MX, 0, s + 1)
            ag_in(t.MX, 0, s + 1)
            push()
            attend_back(l, 0)
            push()
            rs_done(0, s)
            rs_done(1, s)
            project(t.H, A, 0)
            rs_out(0, s + 1)
            push()
            ag_mid(t.MX, 1, s + 1)
            ag_in(t.MX, 1, s + 1)
            attend_back(l, 1)
            push()
            project(t.H, A, 1)
            rs_out(1, s + 1)
            ag_done(t.MX, s + 1)
            if l == 1:
                push_through(y_sum, 1, 1)
            else:
                fetch("NF").wait()
                push_through(y_sum, 0, 2)
            weight_grad(W.at[A], [(t.NF, t.H), (t.MX, t.PR)])
            y_start(l, 0)
            if l == 1:
                for name in ("H", "PR", "PB", "NF"):
                    fetch(name).start()

            def first_back(g):
                def step(r, acc):
                    rs = blk(r, RC)
                    dy = sums(g, r)
                    v = (t.XO[x, rs, :] if l == 0 else t.OUT[0, rs, :]).astype(F32)
                    dx, dg = norm_back(v, t.G[l, 0:1, :], dy)
                    gx = (t.GMID[rs, :] + dx).astype(BF)
                    t.IGB[l, rs, :] = gx
                    if l == 1:
                        t.GT[own_rows(g, r), :] = gx
                    return acc[0] + fold(dg), acc[1] + fold(dy)

                acc = rows_loop(step, (zero8,) * 2)
                put_small(l, 0, acc[0])
                put_small(l, 2, acc[1])
                if l == 1:
                    ag_send(t.GT, g, 6)

            for g in range(2):
                rs_in(g, s + 1, lambda g=g: first_back(g))
            s_start(l)

            @pl.when(x != l)
            def _():
                rcopy(t.IGB.at[l], t.LGB, t.lo_s.at[1], t.lo_r.at[1], p.dev(x=1 - x)).start()

            if l == 1:
                ag_mid(t.GT, 0, 6)
                s_mid(1)

        s_end(1)
        push(3)
        s_mid(0)
        push(100)
        s_end(0)
        for i, (buf, got, out) in enumerate(((t.OUT, t.LOB, t.lo), (t.IGB, t.LGB, t.ig))):
            cp = rcopy(buf.at[x], got, t.lo_s.at[i], t.lo_r.at[i], p.dev(x=1 - x))
            cp.wait_recv()
            cp.wait_send()
            out[x] = buf[x, 0:SEQ, :]
            out[1 - x] = got[0:SEQ, :]
        for m in (2, 1, 0):
            for jj in range(4):
                b = t.CR.at[m, jj]
                pltpu.make_async_copy(b, b, t.c_r.at[m, jj]).wait()
                v = t.CR[m, jj].astype(F32)
                if m == 0:
                    t.ga[jj] = v
                elif m == 1:
                    t.gu[:, jj * TILE : (jj + 1) * TILE] = v
                else:
                    t.gd[:, jj * TILE : (jj + 1) * TILE] = v
        for jj in range(4):
            b = t.SCR.at[jj]
            pltpu.make_async_copy(b, b, t.sc_r.at[jj]).wait()
            t.gs_out[jj] = t.SCR[jj]
        for g in range(2):
            rs_done(g, 7)
        for l in range(2):
            for m in range(3):
                for kz in range(nz):
                    for k in range(1, Y):
                        y_part(l, m, k, kz).wait_send()
                    if kz:
                        z_part(l, m, kz).wait_send()
            for k in range(1, Y):
                s_y(l, k).wait_send()
            for k in range(1, nz):
                s_z(l, k).wait_send()
            for cp in range(2):

                @pl.when(jnp.logical_not(jnp.logical_and(x == l, c == cp)))
                def _():
                    s_c(l, cp).wait_send()
                    for m in range(3):
                        c_part(l, m, cp).wait_send()

    vm = pl.BlockSpec(memory_space=pltpu.VMEM)
    hbm = pl.BlockSpec(memory_space=pl.ANY)
    return pl.pallas_call(
        body,
        out_shape=[jax.ShapeDtypeStruct(*a) for a in outputs.values()]
        + [jax.ShapeDtypeStruct(a, BF) for a in spilled.values()],
        in_specs=[vm, vm] + [hbm] * 4,
        out_specs=[vm] * len(outputs) + [hbm] * len(spilled),
        scratch_shapes=[pltpu.VMEM(*a) for a in vmem.values()] + [dma(a) for a in sems.values()],
        compiler_params=pltpu.CompilerParams(
            collective_id=0, has_side_effects=True, vmem_limit_bytes=VMEM_LIMIT
        ),
    )


def small_pack(norm_gains, row_shifts, head_bias, unit_bias, dpn, nz):
    dp, z = lax.axis_index("dp"), lax.axis_index("tensor")
    rows = jnp.concatenate([norm_gains[0], row_shifts[0]], axis=0)
    w = rows.shape[1]
    rows = lax.dynamic_update_slice(jnp.zeros((6, D), BF), rows, (0, (dp * nz + z) * w)).reshape(1, 24, TILE)
    hw, uw = head_bias.shape[3], unit_bias.shape[2]
    head = jnp.zeros((4, 4, TILE), BF)
    head = lax.dynamic_update_slice(head, head_bias[0, 0][:, None], (0, z, dp * hw))
    head = lax.dynamic_update_slice(head, head_bias[0, 1][:, None], (0, z, 2 * HD + dp * hw))
    unit = lax.dynamic_update_slice(jnp.zeros((4, 4, TILE), BF), unit_bias[0][:, None], (0, z, dp * uw))
    return jnp.concatenate([jnp.broadcast_to(rows, (4, 24, TILE)), head, unit], axis=1)


def solution(mesh):
    dpn, nz = mesh.shape["dp"], mesh.shape["tensor"]

    def on_device(
        images_in, cotangent, w_qkv, w_out, w_up, w_down, norm_gains, row_shifts, head_bias, unit_bias
    ):
        R = w_up.shape[1]
        qkv = w_qkv[0].reshape(R, 3, 4, HD).transpose(2, 0, 1, 3).reshape(4, R, 3 * HD)
        wo = w_out[0].reshape(R, 4, HD).transpose(1, 0, 2)
        wa = jnp.concatenate([qkv, wo], axis=2)
        sp = small_pack(norm_gains, row_shifts, head_bias, unit_bias, dpn, nz)
        lo, ig, ga, gu, gd, gs = both_layers(dpn, nz, R)(images_in, cotangent, wa, w_up[0], w_down[0], sp)[:6]
        dp, z = lax.axis_index("dp"), lax.axis_index("tensor")
        g_qkv = ga[:, :, : 3 * HD].reshape(4, R, 3, HD).transpose(1, 2, 0, 3).reshape(w_qkv.shape)
        g_out = ga[:, :, 3 * HD :].transpose(1, 0, 2).reshape(w_out.shape)
        w, hw, uw = norm_gains.shape[2], head_bias.shape[3], unit_bias.shape[2]
        rows = lax.dynamic_slice(jnp.sum(gs[:, :24], axis=0).reshape(6, D), (0, (dp * nz + z) * w), (6, w))
        head = lax.dynamic_slice(gs, (0, 24 + z, 0), (4, 1, TILE))[:, 0]
        unit = lax.dynamic_slice(gs, (0, 28 + z, dp * uw), (4, 1, uw))[:, 0]
        g_head = jnp.stack([lax.dynamic_slice(head, (0, o + dp * hw), (4, hw)) for o in (0, 2 * HD)])
        return (
            lo[None], ig[None], g_qkv, g_out, gu[None], gd[None],
            rows[None, :2], rows[None, 2:], g_head[None], unit[None],
        )

    in_specs = (
        P(None, ("dp", "tensor"), None),
        P(None, ("dp", "tensor"), None),
        P("section", "dp", None, "tensor"),
        P("section", "dp", "tensor"),
        P("section", "dp", "tensor"),
        P("section", "dp", "tensor"),
        P("section", None, ("dp", "tensor")),
        P("section", None, ("dp", "tensor")),
        P("section", None, "tensor", "dp"),
        P("section", "tensor", "dp"),
    )
    out_specs = (
        P("section", None, ("dp", "tensor"), None),
        P("section", None, ("dp", "tensor"), None),
        P("section", "dp", None, "tensor"),
        P("section", "dp", "tensor"),
        P("section", "dp", "tensor"),
        P("section", "dp", "tensor"),
        P("section", None, ("dp", "tensor")),
        P("section", None, ("dp", "tensor")),
        P("section", None, "tensor", "dp"),
        P("section", "tensor", "dp"),
    )
    return jax.shard_map(
        on_device, mesh=mesh, in_specs=in_specs, out_specs=out_specs, check_vma=False
    )
```

```python
import math
import types

import jax
import jax.numpy as jnp
from jax import lax
from jax.experimental import pallas as pl
from jax.experimental.pallas import tpu as pltpu
from jax.sharding import PartitionSpec as P

D = 1024
HD = 64
SEQ = 197
RP = 208
RC = 16
TILE = 256
SCALE = 0.125
EPS = 1e-06
MESH = pl.DeviceIdType.MESH
BF = jnp.bfloat16
F32 = jnp.float32
NN = (((1,), (0,)), ((), ()))
NT = (((1,), (1,)), ((), ()))
TN = (((0,), (0,)), ((), ()))
VMEM_LIMIT = 62 * 2**20


def mm(a, b, dims):
    return lax.dot_general(a, b, dims, preferred_element_type=F32)


def blk(i, size):
    if isinstance(i, int):
        return pl.ds(i * size, size)
    return pl.ds(pl.multiple_of(i * size, size), size)


class Place:
    def __init__(self, dpn, nz):
        self.Y, self.nz = dpn // 2, nz
        self.x = lax.axis_index("section")
        dp = lax.axis_index("dp")
        self.z = lax.axis_index("tensor")
        self.y, self.c = dp // 2, lax.rem(dp, 2)
        self.j = 2 * self.x + self.c

    def dev(self, x=None, y=None, c=None, z=None):
        x = self.x if x is None else x
        y = self.y if y is None else y
        c = self.c if c is None else c
        z = self.z if z is None else z
        return (x, 2 * y + c, z)

    def cell(self, k):
        jp = lax.rem(self.j + k, 4)
        return jp, jp // 2, lax.rem(jp, 2)

    def yk(self, k):
        return lax.rem(self.y + k, self.Y)

    def zk(self, k):
        return lax.rem(self.z + k, self.nz)

    def barrier(self):
        bar = pltpu.get_barrier_semaphore()
        n = 0
        for k in range(1, 4):
            _, xp, cp = self.cell(k)
            pl.semaphore_signal(bar, inc=1, device_id=self.dev(x=xp, c=cp), device_id_type=MESH)
            n += 1
        for k in range(1, self.nz):
            pl.semaphore_signal(bar, inc=1, device_id=self.dev(z=self.zk(k)), device_id_type=MESH)
            n += 1
        for k in range(1, self.Y):
            pl.semaphore_signal(bar, inc=1, device_id=self.dev(y=self.yk(k)), device_id_type=MESH)
            n += 1
        pl.semaphore_wait(bar, n)


def rcopy(src, dst, ss, rs, dev):
    return pltpu.make_async_remote_copy(
        src_ref=src, dst_ref=dst, send_sem=ss, recv_sem=rs, device_id=dev, device_id_type=MESH
    )


def norm_row(v, g, b):
    cen = v - jnp.sum(v, axis=-1, keepdims=True) * (1.0 / D)
    var = jnp.sum(cen * cen, axis=-1, keepdims=True) * (1.0 / D)
    return cen * lax.rsqrt(var + EPS) * g + b


def norm_back(v, g, dy):
    cen = v - jnp.sum(v, axis=-1, keepdims=True) * (1.0 / D)
    rstd = lax.rsqrt(jnp.sum(cen * cen, axis=-1, keepdims=True) * (1.0 / D) + EPS)
    hat = cen * rstd
    dh = dy * g
    a = jnp.sum(dh, axis=-1, keepdims=True) * (1.0 / D)
    b = jnp.sum(dh * hat, axis=-1, keepdims=True) * (1.0 / D)
    return rstd * (dh - a - hat * b), dy * hat


def fold(v):
    return v[0:8] + v[8:16]


def half(g):
    return blk(g, 2 * RP)


def row(g, m):
    return blk(2 * g + m, RP)


def both_layers(dpn, nz, rows):
    Y, R = dpn // 2, rows
    R2 = 2 * R
    full = (4 * RP, D)
    dma = pltpu.SemaphoreType.DMA
    inputs = ["imgs", "wq", "wo", "wu", "wd", "sp"]
    outputs = {
        "lo": ((2, RP, D), BF), "ig": ((2, RP, D), BF), "cr": ((3, R, D), BF), "gs_out": ((4, 32, TILE), F32),
    }
    spilled = {"NF": full, "PR": full, "N2": full, "H": full, "GD": full, "PB": (16, RP, RP)}
    vmem = {
        "W": ((6, D, D), BF), "DX": ((D, D), BF), "WQ": ((R, 3 * TILE), BF), "WOS": ((R, TILE), BF), "WA": ((4, R, TILE), BF), "SPB": ((2, Y, nz, 2, 32, TILE), BF), "SPS": ((2, 32, TILE), F32),
        "G": ((2, 8, D), F32), "NF": (full, BF), "PR": (full, BF), "N2": (full, BF), "H": (full, BF), "GD": (full, BF),
        "PB": ((16, RP, RP), BF), "MX": (full, BF), "MXC": ((2, 4 * RP, TILE), BF), "GMC": ((4 * RP, TILE), BF), "WO": ((2, D, TILE), BF), "GT": (full, BF), "OP": (full, BF), "RB": ((2, 2, RP, D), BF),
        "CS": ((2, RP, D), BF), "XR": ((2, RP, D), BF), "XO": ((2, RP, D), BF), "MID": ((2, RP, D), F32),
        "OUT": ((2, RP, D), BF), "LOB": ((RP, D), BF), "GMID": ((RP, D), F32), "FIN": ((RP, D), F32), "IGB": ((2, RP, D), BF),
        "LGB": ((RP, D), BF), "YR": ((3, Y - 1, R2, D), BF), "ZR": ((6, 2, R2, TILE), BF), "ZC": ((6, 2, R2, TILE), BF),
        "RD": ((6, 2, R, TILE), BF), "CR": ((3, 4, R, TILE), BF), "SG": ((2, 32, TILE), F32),
        "SYR": ((2, Y - 1, 32, TILE), F32), "SZR": ((2, nz - 1, 32, TILE), F32), "SRD": ((4, 32, TILE), F32),
        "SCR": ((4, 32, TILE), F32),
    }
    sems = {
        "red_s": (3, 4), "red_r": (6, 2), "fz_s": (6, 4), "fz_r": (6, 4), "fy_s": (6, 4, Y), "fy_r": (6, 4, Y),
        "ps": (4 + 2 * nz + 2 * Y,), "pr": (6, max(nz, Y, 2)), "gs": (8, 3), "gr": (8, 3), "ss": (8, 3), "sr": (8, 3),
        "lo_s": (2,), "lo_r": (2,), "io": (9,), "cr_s": (3, 4), "keep": (2, 6), "y_s": (6, Y, nz), "y_r": (6, Y, nz), "z_s": (6, 4), "z_r": (6, 4),
        "c_s": (6, 2), "c_r": (3, 4), "sy_s": (2, Y), "sy_r": (2, Y), "sz_s": (2, nz), "sz_r": (2, nz), "sc_s": (2, 2),
        "sc_r": (4,),
    }
    names = inputs + list(outputs) + ["o_" + n for n in spilled] + list(vmem) + list(sems)

    def body(*refs):
        t = types.SimpleNamespace(**dict(zip(names, refs)))
        p = Place(dpn, nz)
        x, y, c, z, j = p.x, p.y, p.c, p.z, p.j
        near, far = x, 1 - x
        W, OP, RB, CS, XR = t.W, t.OP, t.RB, t.CS, t.XR

        def core_part(g, m, s):
            return rcopy(OP.at[row(g, m)], RB.at[int(s == 3), m], t.ss.at[s, m], t.sr.at[s, m], p.dev(c=1 - c))

        def chip_part(s):
            k = int(s == 3)
            return rcopy(CS.at[k], XR.at[k], t.ss.at[s, 2], t.sr.at[s, 2], p.dev(x=1 - x))

        def rs_out(g, s):
            @pl.when(c != g)
            def _():
                core_part(g, far, s).start()
                core_part(g, near, s).start()

            @pl.when(c == g)
            def _():
                core_part(g, far, s).wait_recv()
                k = int(s == 3)
                CS[k] = (OP[row(g, far), :].astype(F32) + RB[k, far].astype(F32)).astype(BF)
                chip_part(s).start()

        def rs_in(g, s, fn):
            @pl.when(c == g)
            def _():
                core_part(g, near, s).wait_recv()
                chip_part(s).wait_recv()
                fn()

        def rs_done(g, s):
            @pl.when(c != g)
            def _():
                for m in range(2):
                    core_part(g, m, s).wait_send()

            if s != 3:

                @pl.when(c == g)
                def _():
                    chip_part(s).wait_send()

        def sums(g, r):
            rs = blk(r, RC)
            own = OP[pl.ds(pl.multiple_of((2 * g + x) * RP + r * RC, RC), RC), :].astype(F32)
            return own + RB[0, x, rs, :].astype(F32) + XR[0, rs, :].astype(F32)

        def ag_part(buf, g, s, k):
            b = buf.at[row(g, far if k == 2 else near)]
            return rcopy(b, b, t.gs.at[s, k], t.gr.at[s, k], p.dev(x=1 - x) if k == 1 else p.dev(c=1 - c))

        def ag_send(buf, g, s):
            ag_part(buf, g, s, 1).start()
            ag_part(buf, g, s, 0).start()

        def ag_mid(buf, g, s):
            @pl.when(c == g)
            def _():
                ag_part(buf, g, s, 1).wait_recv()
                ag_part(buf, g, s, 2).start()

        def ag_in(buf, g, s):
            @pl.when(c != g)
            def _():
                ag_part(buf, g, s, 0).wait_recv()
                ag_part(buf, g, s, 2).wait_recv()

        def ag_done(buf, s):
            for g in range(2):

                @pl.when(c == g)
                def _():
                    for k in range(3):
                        ag_part(buf, g, s, k).wait_send()

        def ag_local(buf, s):
            return [
                rcopy(buf.at[row(c, m)], buf.at[row(c, m)], t.gs.at[s, m], t.gr.at[s, m], p.dev(c=1 - c))
                for m in range(2)
            ]

        def small_red(k):
            jp, xp, cp = p.cell(k)
            dst = t.SPB.at[x, y, z, c]
            if k == 0:
                return pltpu.make_async_copy(t.sp.at[jp], dst, t.pr.at[x, c])
            return rcopy(t.sp.at[jp], dst, t.ps.at[k], t.pr.at[x, c], p.dev(x=xp, c=cp))

        def small_z(l, k):
            b = t.SPB.at[l, y, z]
            return rcopy(b, b, t.ps.at[4 + l * nz + k], t.pr.at[2 + l, k], p.dev(z=p.zk(k)))

        def small_y(l, k):
            b = t.SPB.at[l, y]
            return rcopy(b, b, t.ps.at[4 + 2 * nz + l * Y + k], t.pr.at[4 + l, k], p.dev(y=p.yk(k)))

        src = (t.WA, t.wu, t.wd)
        inner = lax.rem((z + 1) // 2, 2)
        mate = z + 1 - 2 * lax.rem(z, 2)
        cross = 2 - z // 2
        other = 3 - 3 * (z // 2)
        sides = (z, mate, cross, other)
        holds = (z, mate + inner * (cross - mate), cross + inner * (other - cross), other + inner * (mate - other))

        def red(m, k):
            jp, xp, cp = p.cell(k)
            b = src[m].at[jp] if m == 0 else src[m].at[:, blk(jp, TILE)]
            dst = W.at[x * 3 + m, blk(2 * y + c, R), blk(z, TILE)]
            if k == 0:
                return pltpu.make_async_copy(b, dst, t.red_r.at[x * 3 + m, c])
            return rcopy(b, dst, t.red_s.at[m, k], t.red_r.at[x * 3 + m, c], p.dev(x=xp, c=cp))

        def chunk(lm, k):
            return W.at[lm, blk(y, R2), blk(holds[k], TILE)]

        def wz(lm, k):
            b = chunk(lm, 0)
            if k == 1:
                return rcopy(b, b, t.fz_s.at[lm, 0], t.fz_r.at[lm, 3 - 2 * inner], p.dev(z=mate))
            return rcopy(b, b, t.fz_s.at[lm, 1], t.fz_r.at[lm, 2 - inner], p.dev(z=cross))

        def wrelay(lm, k):
            b = chunk(lm, k)
            return rcopy(b, b, t.fz_s.at[lm, k + 1], t.fz_r.at[lm, k + 1], p.dev(z=mate))

        def wy(lm, k, ky):
            b = chunk(lm, k)
            return rcopy(b, b, t.fy_s.at[lm, k, ky], t.fy_r.at[lm, k, ky], p.dev(y=p.yk(ky)))

        def release(lm):
            for cs in range(2):
                b = W.at[lm, blk(2 * y + cs, R), blk(z, TILE)]
                pltpu.make_async_copy(b, b, t.red_r.at[lm, cs]).wait()
            wz(lm, 2).start()
            wz(lm, 1).start()
            for ky in range(1, Y):
                wy(lm, 0, ky).start()

        def hand_on(lm, k):
            pltpu.make_async_copy(chunk(lm, k), chunk(lm, k), t.fz_r.at[lm, k]).wait()
            if k < 3:

                @pl.when(inner == 1)
                def _():
                    wrelay(lm, k).start()

            for ky in range(1, Y):
                wy(lm, k, ky).start()
            if k == 3 and lm + 2 < 6:
                release(lm + 2)

        queue = [(lm, k) for lm in range(6) for k in (1, 2, 3)]
        handed = []

        def pump(n=1):
            for _ in range(n):
                if queue:
                    lm, k = queue.pop(0)
                    hand_on(lm, k)
                    handed.append((lm, k))

        def ready(lm, k):
            while k and (lm, k) not in handed:
                pump()
            for ky in range(1, Y):
                wy(lm, k, ky).wait_recv()

        def where(l, m):
            return t.DX if m == 2 else W.at[3 * l + m]

        def y_part(l, m, k, kz):
            cols = blk(sides[kz], TILE)
            return rcopy(
                where(l, m).at[blk(p.yk(k), R2), cols], t.YR.at[m, k - 1, :, cols],
                t.y_s.at[3 * l + m, k, kz], t.y_r.at[3 * l + m, k, kz], p.dev(y=p.yk(k)),
            )

        def z_part(l, m, k):
            n = 3 * l + m
            b = where(l, m).at[blk(y, R2), blk(sides[k], TILE)]
            if k == 1:
                return rcopy(b, t.ZR.at[n, 0], t.z_s.at[n, 1], t.z_r.at[n, 0], p.dev(z=mate))
            return rcopy(b, t.ZC.at[n, k - 2], t.z_s.at[n, k], t.z_r.at[n, k], p.dev(z=mate))

        def z_over(l, m, k):
            n = 3 * l + m
            b = where(l, m).at[blk(y, R2), blk(sides[k], TILE)]
            return rcopy(b, t.ZR.at[n, 1], t.z_s.at[n, k], t.z_r.at[n, 1], p.dev(z=sides[k]))

        order = (3, 2, 1, 0)

        def y_start(l, m):
            begun.add((l, m))
            for kz in order:
                for k in range(1, Y):
                    y_part(l, m, k, kz).start()

        begun = set()

        def y_sum(l, m, kz):
            cols = blk(sides[kz], TILE)
            buf = where(l, m)
            for k in range(1, Y):
                y_part(l, m, k, kz).wait_recv()
            v = buf[blk(y, R2), cols].astype(F32)
            for k in range(1, Y):
                v = v + t.YR[m, k - 1, :, cols].astype(F32)
            buf[blk(y, R2), cols] = v.astype(BF)
            if kz == 1:
                z_part(l, m, 1).start()
            elif kz:

                @pl.when(inner == 0)
                def _():
                    z_part(l, m, kz).start()

        def z_mid(l, m, k):
            @pl.when(inner == 1)
            def _():
                z_part(l, m, k).wait_recv()
                buf, cols = where(l, m), blk(sides[k], TILE)
                v = buf[blk(y, R2), cols].astype(F32) + t.ZC[3 * l + m, k - 2].astype(F32)
                buf[blk(y, R2), cols] = v.astype(BF)
                z_over(l, m, k).start()

        def z_sent(l, m):
            for k in (1, 2, 3):
                z_part(l, m, k).wait_send()

        def c_part(l, m, cp):
            lm = 3 * l + m
            return rcopy(t.RD.at[lm, cp], t.CR.at[m, j], t.c_s.at[lm, cp], t.c_r.at[m, j], p.dev(x=l, c=cp))

        def to_owner(l, remote, local):
            for cp in range(2):
                mine = jnp.logical_and(x == l, c == cp)

                @pl.when(mine)
                def _():
                    local(cp).start()

                @pl.when(jnp.logical_not(mine))
                def _():
                    remote(cp).start()

        def z_sum(l, m):
            lm = 3 * l + m
            z_part(l, m, 1).wait_recv()
            z_over(l, m, 2).wait_recv()
            v = where(l, m)[blk(y, R2), blk(z, TILE)].astype(F32)
            v = v + t.ZR[lm, 0].astype(F32) + t.ZR[lm, 1].astype(F32)
            t.RD[lm] = v.astype(BF).reshape(2, R, TILE)
            to_owner(
                l, lambda cp: c_part(l, m, cp),
                lambda cp: pltpu.make_async_copy(t.RD.at[lm, cp], t.CR.at[m, j], t.c_r.at[m, j]),
            )

        steps = []
        for n in range(6):
            l, m = 1 - n // 3, 2 - n % 3
            last = (1 - (n - 1) // 3, 2 - (n - 1) % 3)
            steps += [(y_sum, (l, m, k)) for k in order] + [(z_mid, (l, m, 3)), (z_mid, (l, m, 2))]
            if n:
                steps.append((z_sum, last))
        steps.append((z_sum, (0, 0)))

        def push(n=1):
            for _ in range(n):
                if steps and steps[0][1][:2] in begun:
                    f, a = steps.pop(0)
                    f(*a)

        def push_through(f, l, m):
            while any(g is f and a[:2] == (l, m) for g, a in steps):
                push()

        def s_y(l, k):
            return rcopy(t.SG.at[l], t.SYR.at[l, k - 1], t.sy_s.at[l, k], t.sy_r.at[l, k], p.dev(y=p.yk(k)))

        def s_z(l, k):
            return rcopy(t.SRD.at[l], t.SZR.at[l, k - 1], t.sz_s.at[l, k], t.sz_r.at[l, k], p.dev(z=p.zk(k)))

        def s_c(l, cp):
            return rcopy(t.SRD.at[2 + l], t.SCR.at[j], t.sc_s.at[l, cp], t.sc_r.at[j], p.dev(x=l, c=cp))

        def s_start(l):
            for k in range(1, Y):
                s_y(l, k).start()

        def s_mid(l):
            for k in range(1, Y):
                s_y(l, k).wait_recv()
            t.SRD[l] = t.SG[l] + jnp.sum(t.SYR[l], axis=0)
            for k in range(1, nz):
                s_z(l, k).start()

        def s_end(l):
            for k in range(1, nz):
                s_z(l, k).wait_recv()
            t.SRD[2 + l] = t.SRD[l] + jnp.sum(t.SZR[l], axis=0)
            to_owner(
                l, lambda cp: s_c(l, cp), lambda cp: pltpu.make_async_copy(t.SRD.at[2 + l], t.SCR.at[j], t.sc_r.at[j])
            )

        kept = list(spilled)

        def save(name):
            i = kept.index(name)
            return pltpu.make_async_copy(getattr(t, name), getattr(t, "o_" + name), t.keep.at[0, i])

        def fetch(name):
            i = kept.index(name)
            return pltpu.make_async_copy(getattr(t, "o_" + name), getattr(t, name), t.keep.at[1, i])

        def add_small(l, r, v):
            t.SG[l, pl.ds(r, 1), :] += v

        def put_small(l, r, acc):
            v = jnp.sum(acc, axis=0, keepdims=True)
            for q in range(4):
                add_small(l, 4 * r + q, v[:, q * TILE : (q + 1) * TILE])

        def own_rows(g, r):
            return pl.ds(pl.multiple_of((2 * g + x) * RP + r * RC, RC), RC)

        def attend(l, g, zz):
            rows_, cols = half(g), blk(zz, TILE)
            v = mm(t.NF[rows_, :], W[3 * l, :, cols], NN)
            t.PR[rows_, cols] = (v + t.SPS[l, pl.ds(24 + zz, 1), :]).astype(BF)
            live = lax.broadcasted_iota(jnp.int32, (RP, RP), 1) < SEQ
            for i in range(2):
                im = 2 * g + i
                b = t.PR[row(g, i), cols]
                q, k, v = b[:, 0:HD], b[:, HD : 2 * HD], b[:, 2 * HD : 3 * HD]
                s = jnp.where(live, mm(q, k, NT) * SCALE, -1e30)
                w = jnp.exp(s - jnp.max(s, axis=-1, keepdims=True))
                pb = (w * (1.0 / jnp.sum(w, axis=-1, keepdims=True))).astype(BF)
                t.PB[4 * im + zz] = pb
                put_mixed(l, row(g, i), zz, mm(pb, v, NN).astype(BF))

        def put_mixed(l, ri, zz, o):
            pair = t.MXC[l, ri, blk(zz // 2, 2 * HD)]
            up_half = lax.rem(zz, 2) == 1
            low, high = pair[:, :HD], pair[:, HD:]
            t.MXC[l, ri, blk(zz // 2, 2 * HD)] = jnp.concatenate(
                [jnp.where(up_half, low, o), jnp.where(up_half, o, high)], axis=1
            )

        def out_weights(l):
            for zz in range(4):
                t.WO[l, :, zz * HD : (zz + 1) * HD] = W[3 * l, :, zz * TILE + 3 * HD : (zz + 1) * TILE]

        def out_project(l, g):
            for n in range(4):
                cols = blk(n, TILE)
                OP[half(g), cols] = mm(t.MXC[l, half(g), :], t.WO[l, cols, :], NT).astype(BF)

        def project(lhs, lm, g):
            rows_ = half(g)

            def step(n):
                cols = blk(n, TILE)
                OP[rows_, cols] = mm(lhs[rows_, :], W[lm, cols, :], NT).astype(BF)

            for n in range(4):
                step(n)

        def up(l, g, zz):
            rows_, cols = half(g), blk(zz, TILE)
            u = mm(t.N2[rows_, :], W[3 * l + 1, :, cols], NN) + t.SPS[l, pl.ds(28 + zz, 1), :]
            cdf = 0.5 + 0.5 * lax.erf(u * (1.0 / math.sqrt(2.0)))
            t.H[rows_, cols] = (u * cdf).astype(BF)
            t.GD[rows_, cols] = (cdf + u * jnp.exp(-0.5 * u * u) * (1.0 / math.sqrt(2.0 * math.pi))).astype(BF)

        def pre(l, g):
            rows_ = half(g)

            def step(n):
                cols = blk(n, TILE)
                v = mm(t.GT[rows_, :], W[3 * l + 2, :, cols], NN) * t.GD[rows_, cols].astype(F32)
                gp = v.astype(BF)
                t.GD[rows_, cols] = gp
                add_small(l, 28 + n, jnp.sum(gp.astype(F32), axis=0, keepdims=True))

            for n in range(4):
                step(n)

        def weight_grad(buf, a, b):
            for r in range(4):
                cols = blk(r, TILE)
                buf[cols, :] = mm(a[:, cols], b[...], TN).astype(BF)

        def weight_grad_attn(l, buf):
            for r in range(4):
                cols = blk(r, TILE)
                v = mm(t.NF[:, cols], t.H[...], TN).astype(BF)
                o = mm(t.MX[:, cols], t.MXC[l], TN).astype(BF)
                for zz in range(4):
                    lo = zz * TILE
                    buf[cols, lo : lo + TILE] = jnp.concatenate(
                        [v[:, lo : lo + 3 * HD], o[:, zz * HD : (zz + 1) * HD]], axis=1
                    )

        def mixed_grad(l, g):
            t.GMC[half(g), :] = mm(t.MX[half(g), :], t.WO[l], NN).astype(BF)

        def attend_back(l, g):
            def step(i, _):
                im = 2 * g + i
                ri = blk(im, RP)
                for zz in range(4):
                    cols = blk(zz, TILE)
                    b = t.PR[ri, cols]
                    q, k, v = b[:, 0:HD], b[:, HD : 2 * HD], b[:, 2 * HD : 3 * HD]
                    gm = t.GMC[ri, zz * HD : (zz + 1) * HD]
                    pb = t.PB[4 * im + zz]
                    pf = pb.astype(F32)
                    gp = mm(gm, v, NT)
                    cen = jnp.sum(pf * gp, axis=-1, keepdims=True)
                    gsc = (pf * (gp - cen)).astype(BF)
                    gq = mm(gsc, k, NN) * SCALE
                    gk = mm(gsc, q, TN) * SCALE
                    gv = mm(pb, gm, TN)
                    out = jnp.concatenate([gq, gk, gv, jnp.zeros((RP, HD), F32)], axis=1).astype(BF)
                    t.H[ri, cols] = out
                    add_small(l, 24 + zz, jnp.sum(out.astype(F32), axis=0, keepdims=True))
                return 0

            lax.fori_loop(0, 2, step, 0)

        def swap(buf, got, i):
            return rcopy(buf.at[1 - x], got, t.lo_s.at[i], t.lo_r.at[i], p.dev(x=1 - x))

        def rows_loop(step, init=0):
            return lax.fori_loop(0, RP // RC, step, init)

        take = [
            pltpu.make_async_copy(t.wq, t.WQ, t.io.at[6]),
            pltpu.make_async_copy(t.wo, t.WOS, t.io.at[7]),
            pltpu.make_async_copy(t.imgs.at[0:2], t.XO, t.io.at[0]),
            pltpu.make_async_copy(t.imgs.at[2], t.GT.at[row(c, 0)], t.io.at[1]),
            pltpu.make_async_copy(t.imgs.at[3], t.GT.at[row(c, 1)], t.io.at[8]),
        ]
        for cp in take:
            cp.start()
        for cp in take[:2]:
            cp.wait()
        for jp in range(4):
            parts = [t.WQ[:, k * TILE + jp * HD : k * TILE + (jp + 1) * HD] for k in range(3)]
            t.WA[jp] = jnp.concatenate(parts + [t.WOS[:, jp * HD : (jp + 1) * HD]], axis=1)
        t.SG[...] = jnp.zeros((2, 32, TILE), F32)
        t.MXC[...] = jnp.zeros((2, 4 * RP, TILE), BF)
        p.barrier()
        for k in range(4):
            small_red(k).start()
        for m in range(3):
            for k in (1, 2, 3, 0):
                red(m, k).start()
        for l in range(2):
            for cs in range(2):
                b = t.SPB.at[l, y, z, cs]
                pltpu.make_async_copy(b, b, t.pr.at[l, cs]).wait()
            for k in range(1, nz):
                small_z(l, k).start()
        for cp in take[2:]:
            cp.wait()
        tops = ag_local(t.GT, 4)
        for cp in tops:
            cp.start()
        release(0)
        for l in range(2):
            for k in range(1, nz):
                small_z(l, k).wait_recv()
            for k in range(1, Y):
                small_y(l, k).start()
        for l in range(2):
            for k in range(1, Y):
                small_y(l, k).wait_recv()
            t.SPS[l] = jnp.sum(t.SPB[l].astype(F32).reshape(Y * nz * 2, 32, TILE), axis=0)
            for r in range(6):
                for q in range(4):
                    t.G[l, r : r + 1, q * TILE : (q + 1) * TILE] = t.SPS[l, 4 * r + q : 4 * r + q + 1, :]

        def ln(l, g, b, load, buf, at):
            gain, shift = t.G[l, g : g + 1, :], t.G[l, b : b + 1, :]

            def step(r, _):
                buf[at(r), :] = norm_row(load(r), gain, shift).astype(BF)
                return 0

            rows_loop(step)

        for m in range(2):
            ln(
                0, 0, 2, lambda r, m=m: t.XO[m, blk(r, RC), :].astype(F32), t.NF,
                lambda r, m=m: pl.ds(pl.multiple_of((2 * c + m) * RP + r * RC, RC), RC),
            )
        first = ag_local(t.NF, 0)
        for cp in first:
            cp.start()
        release(1)
        pump(1)
        for cp in first:
            cp.wait_recv()

        for l in range(2):
            A, U, DN = 3 * l, 3 * l + 1, 3 * l + 2
            s = 2 * l
            if l:
                ag_in(t.NF, 0, 2)
            for k in range(4):
                ready(A, k)
                attend(l, 0, holds[k])
                if l == 0 or k < 2:
                    pump()
            if l:
                rs_done(0, 1)
                rs_done(1, 1)
            out_weights(l)
            out_project(l, 0)
            rs_out(0, s)
            if l:
                ag_mid(t.NF, 1, 2)
                ag_in(t.NF, 1, 2)
            for k in range(4):
                attend(l, 1, holds[k])
                if k % 2:
                    pump()
            out_project(l, 1)
            rs_out(1, s)
            if l == 0:
                for cp in first:
                    cp.wait_send()
                for name in ("NF", "PR", "PB"):
                    save(name).start()
            else:
                ag_done(t.NF, 2)

            def second(g):
                gain, shift, bias = t.G[l, 1:2, :], t.G[l, 4:5, :], t.G[l, 3:4, :]

                def step(r, _):
                    rs = blk(r, RC)
                    v = t.XO[x, rs, :] if l == 0 else t.OUT[0, rs, :]
                    mid = v.astype(F32) + sums(g, r) + bias
                    t.MID[l, rs, :] = mid
                    t.N2[own_rows(g, r), :] = norm_row(mid, gain, shift).astype(BF)
                    return 0

                rows_loop(step)
                ag_send(t.N2, g, 1 + 2 * l)

            pump()
            for g in range(2):
                rs_in(g, s, lambda g=g: second(g))
            pump()
            ag_mid(t.N2, 0, 1 + 2 * l)
            ag_in(t.N2, 0, 1 + 2 * l)
            if l:
                save("H").wait()
                save("GD").wait()
            for k in range(4):
                ready(U, k)
                up(l, 0, holds[k])
            ag_mid(t.N2, 1, 1 + 2 * l)
            pump()
            ag_in(t.N2, 1, 1 + 2 * l)
            for k in range(4):
                up(l, 1, holds[k])
            pump()
            ag_done(t.N2, 1 + 2 * l)
            rs_done(0, s)
            rs_done(1, s)
            if l == 0:
                for name in ("N2", "H", "GD"):
                    save(name).start()
                for name in ("NF", "PR", "PB"):
                    save(name).wait()
            else:
                for cp in tops:
                    cp.wait_recv()
                weight_grad(t.DX, t.GT, t.H)
                y_start(1, 2)
            for k in range(4):
                ready(DN, k)
            s = 2 * l + 1
            project(t.H, DN, 0)
            rs_out(0, s)
            pump()
            project(t.H, DN, 1)
            rs_out(1, s)
            pump()
            if l == 0:
                save("N2").wait()

                def last(g):
                    gain, shift, bias = t.G[1, 0:1, :], t.G[1, 2:3, :], t.G[0, 5:6, :]

                    def step(r, _):
                        rs = blk(r, RC)
                        o = (t.MID[0, rs, :] + sums(g, r) + bias).astype(BF)
                        t.OUT[0, rs, :] = o
                        t.NF[own_rows(g, r), :] = norm_row(o.astype(F32), gain, shift).astype(BF)
                        return 0

                    rows_loop(step)
                    ag_send(t.NF, g, 2)

                for g in range(2):
                    rs_in(g, s, lambda g=g: last(g))
                pump()
                ag_mid(t.NF, 0, 2)

            else:
                for g in range(2):

                    @pl.when(c == g)
                    def _():
                        def step(r, _):
                            rs = blk(r, RC)
                            t.FIN[rs, :] = t.MID[1, rs, :] + OP[own_rows(g, r), :].astype(F32) + t.G[1, 5:6, :]
                            return 0

                        rows_loop(step)

        for k in range(1, 4):
            small_red(k).wait_send()
        for l in range(2):
            for k in range(1, nz):
                small_z(l, k).wait_send()
            for k in range(1, Y):
                small_y(l, k).wait_send()
        for m in range(3):
            for k in range(1, 4):
                red(m, k).wait_send()
        for lm in range(6):
            wz(lm, 1).wait_send()
            wz(lm, 2).wait_send()
            for k in (1, 2):

                @pl.when(inner == 1)
                def _():
                    wrelay(lm, k).wait_send()

            for k in range(4):
                for ky in range(1, Y):
                    wy(lm, k, ky).wait_send()

        def final_out(g):
            def step(r, _):
                rs = blk(r, RC)
                v = t.FIN[rs, :] + RB[1, x, rs, :].astype(F32) + XR[1, rs, :].astype(F32)
                t.OUT[1, rs, :] = v.astype(BF)
                return 0

            rows_loop(step)

        zero8 = jnp.zeros((8, D), F32)
        for l in (1, 0):
            A, U, DN = 3 * l, 3 * l + 1, 3 * l + 2
            s = 4 + 2 * (1 - l)
            if l == 0:
                ag_in(t.GT, 0, 6)
                fetch("GD").wait()
            rs_done(0, s - 1)
            rs_done(1, s - 1)
            pre(l, 0)
            project(t.GD, U, 0)
            rs_out(0, s)
            push()
            if l == 0:
                ag_mid(t.GT, 1, 6)
                ag_in(t.GT, 1, 6)
                fetch("H").wait()
                push_through(z_sum, 1, 2)
                for kz in range(nz):
                    for k in range(1, Y):
                        y_part(1, 2, k, kz).wait_send()
                z_sent(1, 2)
                weight_grad(t.DX, t.GT, t.H)
                push_through(y_sum, 1, 0)
                y_start(0, 2)
            pre(l, 1)
            project(t.GD, U, 1)
            rs_out(1, s)
            push()
            if l == 1:
                for cp in tops:
                    cp.wait_send()
            else:
                ag_done(t.GT, 6)

            def fill_up():
                if l == 0:
                    fetch("N2").wait()
                weight_grad(W.at[U], t.N2, t.GD)
                y_start(l, 1)
                if l == 1:
                    fetch("N2").start()
                    fetch("GD").start()

            def mid_back(g):
                def step(r, acc):
                    rs = blk(r, RC)
                    dy = sums(g, r)
                    top = t.GT[own_rows(g, r), :].astype(F32)
                    dx, dg = norm_back(t.MID[l, rs, :], t.G[l, 1:2, :], dy)
                    gmid = top + dx
                    t.GMID[rs, :] = gmid
                    t.MX[own_rows(g, r), :] = gmid.astype(BF)
                    return acc[0] + fold(dg), acc[1] + fold(dy), acc[2] + fold(gmid), acc[3] + fold(top)

                acc = rows_loop(step, (zero8,) * 4)
                put_small(l, 1, acc[0])
                put_small(l, 4, acc[1])
                put_small(l, 3, acc[2])
                put_small(l, 5, acc[3])
                ag_send(t.MX, g, s + 1)

            rs_in(0, s, lambda: mid_back(0))
            fill_up()
            rs_in(1, s, lambda: mid_back(1))
            push()
            if l == 0:
                for name in ("PR", "PB"):
                    fetch(name).wait()
            ag_mid(t.MX, 0, s + 1)
            ag_in(t.MX, 0, s + 1)
            push()
            mixed_grad(l, 0)
            attend_back(l, 0)
            push()
            rs_done(0, s)
            rs_done(1, s)
            project(t.H, A, 0)
            rs_out(0, s + 1)
            push()
            ag_mid(t.MX, 1, s + 1)
            ag_in(t.MX, 1, s + 1)
            mixed_grad(l, 1)
            attend_back(l, 1)
            push()
            project(t.H, A, 1)
            rs_out(1, s + 1)
            ag_done(t.MX, s + 1)
            if l == 1:
                push_through(y_sum, 1, 1)
            else:
                fetch("NF").wait()
                s_mid(1)
                push_through(y_sum, 0, 2)
            def first_back(g):
                def step(r, acc):
                    rs = blk(r, RC)
                    dy = sums(g, r)
                    v = (t.XO[x, rs, :] if l == 0 else t.OUT[0, rs, :]).astype(F32)
                    dx, dg = norm_back(v, t.G[l, 0:1, :], dy)
                    gx = (t.GMID[rs, :] + dx).astype(BF)
                    t.IGB[l, rs, :] = gx
                    if l == 1:
                        t.GT[own_rows(g, r), :] = gx
                    return acc[0] + fold(dg), acc[1] + fold(dy)

                acc = rows_loop(step, (zero8,) * 2)
                put_small(l, 0, acc[0])
                put_small(l, 2, acc[1])
                if l == 1:
                    ag_send(t.GT, g, 6)

            if l == 0:
                swap(t.OUT, t.LOB, 0).start()

            def fill_attn():
                weight_grad_attn(l, W.at[A])
                y_start(l, 0)
                if l == 1:
                    for name in ("H", "PR", "PB", "NF"):
                        fetch(name).start()

            if l == 0:
                fill_attn()
            rs_in(0, s + 1, lambda: first_back(0))
            if l == 1:
                fill_attn()
            rs_in(1, s + 1, lambda: first_back(1))
            if l == 1:
                for g in range(2):
                    rs_in(g, 3, lambda g=g: final_out(g))
            s_start(l)

            if l == 1:
                ag_mid(t.GT, 0, 6)

        swap(t.IGB, t.LGB, 1).start()
        s_end(1)
        push(100)
        s_mid(0)
        s_end(0)
        give = []
        for i, (buf, got, out) in enumerate(((t.OUT, t.LOB, t.lo), (t.IGB, t.LGB, t.ig))):
            cp = swap(buf, got, i)
            cp.wait_recv()
            cp.wait_send()
            give.append(pltpu.make_async_copy(buf.at[x], out.at[x], t.io.at[2 + 2 * i]))
            give.append(pltpu.make_async_copy(got, out.at[1 - x], t.io.at[3 + 2 * i]))
            for cp in give[-2:]:
                cp.start()
        for m in (2, 1, 0):
            for jj in range(4):
                b = t.CR.at[m, jj]
                pltpu.make_async_copy(b, b, t.c_r.at[m, jj]).wait()
                give.append(pltpu.make_async_copy(b, t.cr.at[m, :, blk(jj, TILE)], t.cr_s.at[m, jj]))
                give[-1].start()
        for jj in range(4):
            b = t.SCR.at[jj]
            pltpu.make_async_copy(b, b, t.sc_r.at[jj]).wait()
            t.gs_out[jj] = t.SCR[jj]
        for cp in give:
            cp.wait()
        for g in range(2):
            rs_done(g, 7)
        chip_part(3).wait_send()
        for l in range(2):
            for m in range(3 if l == 0 else 2):
                for kz in range(nz):
                    for k in range(1, Y):
                        y_part(l, m, k, kz).wait_send()
                z_sent(l, m)
            for k in range(1, Y):
                s_y(l, k).wait_send()
            for k in range(1, nz):
                s_z(l, k).wait_send()
            for cp in range(2):

                @pl.when(jnp.logical_not(jnp.logical_and(x == l, c == cp)))
                def _():
                    s_c(l, cp).wait_send()
                    for m in range(3):
                        c_part(l, m, cp).wait_send()

    vm = pl.BlockSpec(memory_space=pltpu.VMEM)
    hbm = pl.BlockSpec(memory_space=pl.ANY)
    return pl.pallas_call(
        body,
        out_shape=[jax.ShapeDtypeStruct(*a) for a in outputs.values()]
        + [jax.ShapeDtypeStruct(a, BF) for a in spilled.values()],
        in_specs=[hbm] * 6,
        out_specs=[hbm] * (len(outputs) - 1) + [vm] + [hbm] * len(spilled),
        scratch_shapes=[pltpu.VMEM(*a) for a in vmem.values()] + [dma(a) for a in sems.values()],
        compiler_params=pltpu.CompilerParams(
            collective_id=0, has_side_effects=True, vmem_limit_bytes=VMEM_LIMIT
        ),
    )


def small_pack(norm_gains, row_shifts, head_bias, unit_bias, dpn, nz):
    dp, z = lax.axis_index("dp"), lax.axis_index("tensor")
    rows = jnp.concatenate([norm_gains[0], row_shifts[0]], axis=0)
    w = rows.shape[1]
    rows = lax.dynamic_update_slice(jnp.zeros((6, D), BF), rows, (0, (dp * nz + z) * w)).reshape(1, 24, TILE)
    hw, uw = head_bias.shape[3], unit_bias.shape[2]
    head = jnp.zeros((4, 4, TILE), BF)
    head = lax.dynamic_update_slice(head, head_bias[0, 0][:, None], (0, z, dp * hw))
    head = lax.dynamic_update_slice(head, head_bias[0, 1][:, None], (0, z, 2 * HD + dp * hw))
    unit = lax.dynamic_update_slice(jnp.zeros((4, 4, TILE), BF), unit_bias[0][:, None], (0, z, dp * uw))
    return jnp.concatenate([jnp.broadcast_to(rows, (4, 24, TILE)), head, unit], axis=1)


def solution(mesh):
    dpn, nz = mesh.shape["dp"], mesh.shape["tensor"]

    def on_device(
        images_in, cotangent, w_qkv, w_out, w_up, w_down, norm_gains, row_shifts, head_bias, unit_bias
    ):
        R = w_up.shape[1]
        sp = small_pack(norm_gains, row_shifts, head_bias, unit_bias, dpn, nz)
        imgs = jnp.pad(jnp.concatenate([images_in, cotangent]), ((0, 0), (0, RP - SEQ), (0, 0)))
        lo, ig, cr, gs = both_layers(dpn, nz, R)(
            imgs, w_qkv[0].reshape(R, 3 * TILE), w_out[0], w_up[0], w_down[0], sp
        )[:4]
        lo, ig = lo[:, :SEQ], ig[:, :SEQ]
        gu, gd = cr[1].astype(F32), cr[2].astype(F32)
        dp, z = lax.axis_index("dp"), lax.axis_index("tensor")
        ga = cr[0].astype(F32).reshape(R, 4, TILE)
        g_qkv = ga[:, :, : 3 * HD].reshape(R, 4, 3, HD).transpose(0, 2, 1, 3).reshape(w_qkv.shape)
        g_out = ga[:, :, 3 * HD :].reshape(w_out.shape)
        w, hw, uw = norm_gains.shape[2], head_bias.shape[3], unit_bias.shape[2]
        rows = lax.dynamic_slice(jnp.sum(gs[:, :24], axis=0).reshape(6, D), (0, (dp * nz + z) * w), (6, w))
        head = lax.dynamic_slice(gs, (0, 24 + z, 0), (4, 1, TILE))[:, 0]
        unit = lax.dynamic_slice(gs, (0, 28 + z, dp * uw), (4, 1, uw))[:, 0]
        g_head = jnp.stack([lax.dynamic_slice(head, (0, o + dp * hw), (4, hw)) for o in (0, 2 * HD)])
        return (
            lo[None], ig[None], g_qkv, g_out, gu[None], gd[None],
            rows[None, :2], rows[None, 2:], g_head[None], unit[None],
        )

    in_specs = (
        P(None, ("dp", "tensor"), None),
        P(None, ("dp", "tensor"), None),
        P("section", "dp", None, "tensor"),
        P("section", "dp", "tensor"),
        P("section", "dp", "tensor"),
        P("section", "dp", "tensor"),
        P("section", None, ("dp", "tensor")),
        P("section", None, ("dp", "tensor")),
        P("section", None, "tensor", "dp"),
        P("section", "tensor", "dp"),
    )
    out_specs = (
        P("section", None, ("dp", "tensor"), None),
        P("section", None, ("dp", "tensor"), None),
        P("section", "dp", None, "tensor"),
        P("section", "dp", "tensor"),
        P("section", "dp", "tensor"),
        P("section", "dp", "tensor"),
        P("section", None, ("dp", "tensor")),
        P("section", None, ("dp", "tensor")),
        P("section", None, "tensor", "dp"),
        P("section", "tensor", "dp"),
    )
    return jax.shard_map(
        on_device, mesh=mesh, in_specs=in_specs, out_specs=out_specs, check_vma=False
    )
```

```python
import math
import types

import jax
import jax.numpy as jnp
from jax import lax
from jax.experimental import pallas as pl
from jax.experimental.pallas import tpu as pltpu
from jax.sharding import PartitionSpec as P

D = 1024
HD = 64
SEQ = 197
RP = 208
RC = 16
PARTS = ((0, 7), (7, 13))
TILE = 256
SCALE = 0.125
EPS = 1e-06
MESH = pl.DeviceIdType.MESH
BF = jnp.bfloat16
F32 = jnp.float32
NN = (((1,), (0,)), ((), ()))
NT = (((1,), (1,)), ((), ()))
TN = (((0,), (0,)), ((), ()))
VMEM_LIMIT = 62 * 2**20


def mm(a, b, dims):
    return lax.dot_general(a, b, dims, preferred_element_type=F32)


def blk(i, size):
    if isinstance(i, int):
        return pl.ds(i * size, size)
    return pl.ds(pl.multiple_of(i * size, size), size)


class Place:
    def __init__(self, dpn, nz):
        self.Y, self.nz = dpn // 2, nz
        self.x = lax.axis_index("section")
        dp = lax.axis_index("dp")
        self.z = lax.axis_index("tensor")
        self.y, self.c = dp // 2, lax.rem(dp, 2)
        self.j = 2 * self.x + self.c

    def dev(self, x=None, y=None, c=None, z=None):
        x = self.x if x is None else x
        y = self.y if y is None else y
        c = self.c if c is None else c
        z = self.z if z is None else z
        return (x, 2 * y + c, z)

    def cell(self, k):
        jp = lax.rem(self.j + k, 4)
        return jp, jp // 2, lax.rem(jp, 2)

    def yk(self, k):
        return lax.rem(self.y + k, self.Y)

    def zk(self, k):
        return lax.rem(self.z + k, self.nz)

    def barrier(self):
        bar = pltpu.get_barrier_semaphore()
        n = 0
        for k in range(1, 4):
            _, xp, cp = self.cell(k)
            pl.semaphore_signal(bar, inc=1, device_id=self.dev(x=xp, c=cp), device_id_type=MESH)
            n += 1
        for k in range(1, self.nz):
            pl.semaphore_signal(bar, inc=1, device_id=self.dev(z=self.zk(k)), device_id_type=MESH)
            n += 1
        for k in range(1, self.Y):
            pl.semaphore_signal(bar, inc=1, device_id=self.dev(y=self.yk(k)), device_id_type=MESH)
            n += 1
        pl.semaphore_wait(bar, n)


def rcopy(src, dst, ss, rs, dev):
    return pltpu.make_async_remote_copy(
        src_ref=src, dst_ref=dst, send_sem=ss, recv_sem=rs, device_id=dev, device_id_type=MESH
    )


def norm_row(v, g, b):
    cen = v - jnp.sum(v, axis=-1, keepdims=True) * (1.0 / D)
    var = jnp.sum(cen * cen, axis=-1, keepdims=True) * (1.0 / D)
    return cen * lax.rsqrt(var + EPS) * g + b


def norm_back(v, g, dy):
    cen = v - jnp.sum(v, axis=-1, keepdims=True) * (1.0 / D)
    rstd = lax.rsqrt(jnp.sum(cen * cen, axis=-1, keepdims=True) * (1.0 / D) + EPS)
    hat = cen * rstd
    dh = dy * g
    a = jnp.sum(dh, axis=-1, keepdims=True) * (1.0 / D)
    b = jnp.sum(dh * hat, axis=-1, keepdims=True) * (1.0 / D)
    return rstd * (dh - a - hat * b), dy * hat


def fold(v):
    return v[0:8] + v[8:16]


def half(g):
    return blk(g, 2 * RP)


def row(g, m):
    return blk(2 * g + m, RP)


def both_layers(dpn, nz, rows):
    Y, R = dpn // 2, rows
    R2 = 2 * R
    full = (4 * RP, D)
    dma = pltpu.SemaphoreType.DMA
    inputs = ["imgs", "wq", "wo", "wu", "wd", "sp"]
    outputs = {
        "lo": ((2, RP, D), BF), "ig": ((2, RP, D), BF), "cr": ((3, R, D), BF), "gs_out": ((4, 32, TILE), F32),
    }
    spilled = {"NF": full, "PR": full, "N2": full, "H": full, "GD": full, "PB": (16, RP, RP)}
    vmem = {
        "W": ((6, D, D), BF), "DX": ((D, D), BF), "WQ": ((R, 3 * TILE), BF), "WOS": ((R, TILE), BF), "WA": ((4, R, TILE), BF), "SPB": ((2, Y, nz, 2, 32, TILE), BF), "SPS": ((2, 32, TILE), F32),
        "G": ((2, 8, D), F32), "NF": (full, BF), "PR": (full, BF), "N2": (full, BF), "H": (full, BF), "GD": (full, BF),
        "PB": ((16, RP, RP), BF), "MX": (full, BF), "MXC": ((2, 4 * RP, TILE), BF), "GMC": ((4 * RP, TILE), BF), "WO": ((2, D, TILE), BF), "GT": (full, BF), "OP": (full, BF), "RB": ((2, 2, RP, D), BF),
        "CS": ((2, RP, D), BF), "XR": ((2, RP, D), BF), "XO": ((2, RP, D), BF), "MID": ((2, RP, D), F32),
        "OUT": ((2, RP, D), BF), "LOB": ((RP, D), BF), "GMID": ((RP, D), F32), "FIN": ((RP, D), F32), "IGB": ((2, RP, D), BF),
        "LGB": ((RP, D), BF), "YR": ((3, Y - 1, R2, D), BF), "ZR": ((6, 2, R2, TILE), BF), "ZC": ((6, 2, R2, TILE), BF),
        "RD": ((6, 2, R, TILE), BF), "CR": ((3, 4, R, TILE), BF), "SG": ((2, 32, TILE), F32),
        "SYR": ((2, Y - 1, 32, TILE), F32), "SZR": ((2, nz - 1, 32, TILE), F32), "SRD": ((4, 32, TILE), F32),
        "SCR": ((4, 32, TILE), F32),
    }
    sems = {
        "red_s": (3, 4), "red_r": (6, 2), "fz_s": (6, 4), "fz_r": (6, 4), "fy_s": (6, 4, Y), "fy_r": (6, 4, Y),
        "ps": (4 + 2 * nz + 2 * Y,), "pr": (6, max(nz, Y, 2)), "gs": (8, 6), "gr": (8, 6), "ss": (8, 4), "sr": (8, 4),
        "lo_s": (2,), "lo_r": (2,), "io": (9,), "cr_s": (3, 4), "keep": (2, 6), "y_s": (6, Y, nz), "y_r": (6, Y, nz), "z_s": (6, 4), "z_r": (6, 4),
        "c_s": (6, 2), "c_r": (3, 4), "sy_s": (2, Y), "sy_r": (2, Y), "sz_s": (2, nz), "sz_r": (2, nz), "sc_s": (2, 2),
        "sc_r": (4,),
    }
    names = inputs + list(outputs) + ["o_" + n for n in spilled] + list(vmem) + list(sems)

    def body(*refs):
        t = types.SimpleNamespace(**dict(zip(names, refs)))
        p = Place(dpn, nz)
        x, y, c, z, j = p.x, p.y, p.c, p.z, p.j
        near, far = x, 1 - x
        W, OP, RB, CS, XR = t.W, t.OP, t.RB, t.CS, t.XR

        def core_part(g, m, s):
            return rcopy(OP.at[row(g, m)], RB.at[int(s == 3), m], t.ss.at[s, m], t.sr.at[s, m], p.dev(c=1 - c))

        def chip_part(s, h):
            k, rs = int(s == 3), pl.ds(PARTS[h][0] * RC, (PARTS[h][1] - PARTS[h][0]) * RC)
            return rcopy(CS.at[k, rs], XR.at[k, rs], t.ss.at[s, 2 + h], t.sr.at[s, 2 + h], p.dev(x=1 - x))

        def rs_out(g, s):
            @pl.when(c != g)
            def _():
                core_part(g, far, s).start()
                core_part(g, near, s).start()

            @pl.when(c == g)
            def _():
                core_part(g, far, s).wait_recv()
                k = int(s == 3)
                for h, (lo, hi) in enumerate(PARTS):
                    rs = pl.ds(lo * RC, (hi - lo) * RC)
                    src_rows = pl.ds(pl.multiple_of((2 * g + far) * RP + lo * RC, RC), (hi - lo) * RC)
                    CS[k, rs, :] = (OP[src_rows, :].astype(F32) + RB[k, far, rs, :].astype(F32)).astype(BF)
                    chip_part(s, h).start()

        def rs_in(g, s, fn, init=0, end=None):
            @pl.when(c == g)
            def _():
                core_part(g, near, s).wait_recv()
                acc = init
                for h in range(2):
                    chip_part(s, h).wait_recv()
                    acc = fn(h, acc)
                if end is not None:
                    end(acc)

        def rs_done(g, s):
            @pl.when(c != g)
            def _():
                for m in range(2):
                    core_part(g, m, s).wait_send()

            if s != 3:

                @pl.when(c == g)
                def _():
                    for h in range(2):
                        chip_part(s, h).wait_send()

        def sums(g, r):
            rs = blk(r, RC)
            own = OP[pl.ds(pl.multiple_of((2 * g + x) * RP + r * RC, RC), RC), :].astype(F32)
            return own + RB[0, x, rs, :].astype(F32) + XR[0, rs, :].astype(F32)

        def ag_part(buf, g, s, k, h):
            lo, hi = PARTS[h]
            m = far if k == 2 else near
            b = buf.at[pl.ds(pl.multiple_of((2 * g + m) * RP + lo * RC, RC), (hi - lo) * RC)]
            i = 2 * k + h
            return rcopy(b, b, t.gs.at[s, i], t.gr.at[s, i], p.dev(x=1 - x) if k == 1 else p.dev(c=1 - c))

        def ag_send(buf, g, s, h):
            ag_part(buf, g, s, 1, h).start()
            ag_part(buf, g, s, 0, h).start()

        def ag_mid(buf, g, s):
            @pl.when(c == g)
            def _():
                for h in range(2):
                    ag_part(buf, g, s, 1, h).wait_recv()
                    ag_part(buf, g, s, 2, h).start()

        def ag_in(buf, g, s):
            @pl.when(c != g)
            def _():
                for h in range(2):
                    ag_part(buf, g, s, 0, h).wait_recv()
                    ag_part(buf, g, s, 2, h).wait_recv()

        def ag_done(buf, s):
            for g in range(2):

                @pl.when(c == g)
                def _():
                    for h in range(2):
                        for k in range(3):
                            ag_part(buf, g, s, k, h).wait_send()

        def ag_local(buf, s):
            return [
                rcopy(buf.at[row(c, m)], buf.at[row(c, m)], t.gs.at[s, m], t.gr.at[s, m], p.dev(c=1 - c))
                for m in range(2)
            ]

        def small_red(k):
            jp, xp, cp = p.cell(k)
            dst = t.SPB.at[x, y, z, c]
            if k == 0:
                return pltpu.make_async_copy(t.sp.at[jp], dst, t.pr.at[x, c])
            return rcopy(t.sp.at[jp], dst, t.ps.at[k], t.pr.at[x, c], p.dev(x=xp, c=cp))

        def small_z(l, k):
            b = t.SPB.at[l, y, z]
            return rcopy(b, b, t.ps.at[4 + l * nz + k], t.pr.at[2 + l, k], p.dev(z=p.zk(k)))

        def small_y(l, k):
            b = t.SPB.at[l, y]
            return rcopy(b, b, t.ps.at[4 + 2 * nz + l * Y + k], t.pr.at[4 + l, k], p.dev(y=p.yk(k)))

        src = (t.WA, t.wu, t.wd)
        inner = lax.rem((z + 1) // 2, 2)
        mate = z + 1 - 2 * lax.rem(z, 2)
        cross = 2 - z // 2
        other = 3 - 3 * (z // 2)
        sides = (z, mate, cross, other)
        holds = (z, mate + inner * (cross - mate), cross + inner * (other - cross), other + inner * (mate - other))

        def red(m, k):
            jp, xp, cp = p.cell(k)
            b = src[m].at[jp] if m == 0 else src[m].at[:, blk(jp, TILE)]
            dst = W.at[x * 3 + m, blk(2 * y + c, R), blk(z, TILE)]
            if k == 0:
                return pltpu.make_async_copy(b, dst, t.red_r.at[x * 3 + m, c])
            return rcopy(b, dst, t.red_s.at[m, k], t.red_r.at[x * 3 + m, c], p.dev(x=xp, c=cp))

        def chunk(lm, k):
            return W.at[lm, blk(y, R2), blk(holds[k], TILE)]

        def wz(lm, k):
            b = chunk(lm, 0)
            if k == 1:
                return rcopy(b, b, t.fz_s.at[lm, 0], t.fz_r.at[lm, 3 - 2 * inner], p.dev(z=mate))
            return rcopy(b, b, t.fz_s.at[lm, 1], t.fz_r.at[lm, 2 - inner], p.dev(z=cross))

        def wrelay(lm, k):
            b = chunk(lm, k)
            return rcopy(b, b, t.fz_s.at[lm, k + 1], t.fz_r.at[lm, k + 1], p.dev(z=mate))

        def wy(lm, k, ky):
            b = chunk(lm, k)
            return rcopy(b, b, t.fy_s.at[lm, k, ky], t.fy_r.at[lm, k, ky], p.dev(y=p.yk(ky)))

        def release(lm):
            for cs in range(2):
                b = W.at[lm, blk(2 * y + cs, R), blk(z, TILE)]
                pltpu.make_async_copy(b, b, t.red_r.at[lm, cs]).wait()
            wz(lm, 2).start()
            wz(lm, 1).start()
            for ky in range(1, Y):
                wy(lm, 0, ky).start()

        def hand_on(lm, k):
            pltpu.make_async_copy(chunk(lm, k), chunk(lm, k), t.fz_r.at[lm, k]).wait()
            if k < 3:

                @pl.when(inner == 1)
                def _():
                    wrelay(lm, k).start()

            for ky in range(1, Y):
                wy(lm, k, ky).start()
            if k == 3 and lm + 2 < 6:
                release(lm + 2)

        queue = [(lm, k) for lm in range(6) for k in (1, 2, 3)]
        handed = []

        def pump(n=1):
            for _ in range(n):
                if queue:
                    lm, k = queue.pop(0)
                    hand_on(lm, k)
                    handed.append((lm, k))

        def ready(lm, k):
            while k and (lm, k) not in handed:
                pump()
            for ky in range(1, Y):
                wy(lm, k, ky).wait_recv()

        def where(l, m):
            return t.DX if m == 2 else W.at[3 * l + m]

        def y_part(l, m, k, kz):
            cols = blk(sides[kz], TILE)
            return rcopy(
                where(l, m).at[blk(p.yk(k), R2), cols], t.YR.at[m, k - 1, :, cols],
                t.y_s.at[3 * l + m, k, kz], t.y_r.at[3 * l + m, k, kz], p.dev(y=p.yk(k)),
            )

        def z_part(l, m, k):
            n = 3 * l + m
            b = where(l, m).at[blk(y, R2), blk(sides[k], TILE)]
            if k == 1:
                return rcopy(b, t.ZR.at[n, 0], t.z_s.at[n, 1], t.z_r.at[n, 0], p.dev(z=mate))
            return rcopy(b, t.ZC.at[n, k - 2], t.z_s.at[n, k], t.z_r.at[n, k], p.dev(z=mate))

        def z_over(l, m, k):
            n = 3 * l + m
            b = where(l, m).at[blk(y, R2), blk(sides[k], TILE)]
            return rcopy(b, t.ZR.at[n, 1], t.z_s.at[n, k], t.z_r.at[n, 1], p.dev(z=sides[k]))

        order = (3, 2, 1, 0)

        def y_start(l, m):
            begun.add((l, m))
            for kz in order:
                for k in range(1, Y):
                    y_part(l, m, k, kz).start()

        begun = set()

        def y_sum(l, m, kz):
            cols = blk(sides[kz], TILE)
            buf = where(l, m)
            for k in range(1, Y):
                y_part(l, m, k, kz).wait_recv()
            v = buf[blk(y, R2), cols].astype(F32)
            for k in range(1, Y):
                v = v + t.YR[m, k - 1, :, cols].astype(F32)
            buf[blk(y, R2), cols] = v.astype(BF)
            if kz == 1:
                z_part(l, m, 1).start()
            elif kz:

                @pl.when(inner == 0)
                def _():
                    z_part(l, m, kz).start()

        def z_mid(l, m, k):
            @pl.when(inner == 1)
            def _():
                z_part(l, m, k).wait_recv()
                buf, cols = where(l, m), blk(sides[k], TILE)
                v = buf[blk(y, R2), cols].astype(F32) + t.ZC[3 * l + m, k - 2].astype(F32)
                buf[blk(y, R2), cols] = v.astype(BF)
                z_over(l, m, k).start()

        def z_sent(l, m):
            for k in (1, 2, 3):
                z_part(l, m, k).wait_send()

        def c_part(l, m, cp):
            lm = 3 * l + m
            return rcopy(t.RD.at[lm, cp], t.CR.at[m, j], t.c_s.at[lm, cp], t.c_r.at[m, j], p.dev(x=l, c=cp))

        def to_owner(l, remote, local):
            for cp in range(2):
                mine = jnp.logical_and(x == l, c == cp)

                @pl.when(mine)
                def _():
                    local(cp).start()

                @pl.when(jnp.logical_not(mine))
                def _():
                    remote(cp).start()

        def z_sum(l, m):
            lm = 3 * l + m
            z_part(l, m, 1).wait_recv()
            z_over(l, m, 2).wait_recv()
            v = where(l, m)[blk(y, R2), blk(z, TILE)].astype(F32)
            v = v + t.ZR[lm, 0].astype(F32) + t.ZR[lm, 1].astype(F32)
            t.RD[lm] = v.astype(BF).reshape(2, R, TILE)
            to_owner(
                l, lambda cp: c_part(l, m, cp),
                lambda cp: pltpu.make_async_copy(t.RD.at[lm, cp], t.CR.at[m, j], t.c_r.at[m, j]),
            )

        steps = []
        for n in range(6):
            l, m = 1 - n // 3, 2 - n % 3
            last = (1 - (n - 1) // 3, 2 - (n - 1) % 3)
            steps += [(y_sum, (l, m, k)) for k in order] + [(z_mid, (l, m, 3)), (z_mid, (l, m, 2))]
            if n:
                steps.append((z_sum, last))
        steps.append((z_sum, (0, 0)))

        def push(n=1):
            for _ in range(n):
                if steps and steps[0][1][:2] in begun:
                    f, a = steps.pop(0)
                    f(*a)

        def push_through(f, l, m):
            while any(g is f and a[:2] == (l, m) for g, a in steps):
                push()

        def s_y(l, k):
            return rcopy(t.SG.at[l], t.SYR.at[l, k - 1], t.sy_s.at[l, k], t.sy_r.at[l, k], p.dev(y=p.yk(k)))

        def s_z(l, k):
            return rcopy(t.SRD.at[l], t.SZR.at[l, k - 1], t.sz_s.at[l, k], t.sz_r.at[l, k], p.dev(z=p.zk(k)))

        def s_c(l, cp):
            return rcopy(t.SRD.at[2 + l], t.SCR.at[j], t.sc_s.at[l, cp], t.sc_r.at[j], p.dev(x=l, c=cp))

        def s_start(l):
            for k in range(1, Y):
                s_y(l, k).start()

        def s_mid(l):
            for k in range(1, Y):
                s_y(l, k).wait_recv()
            t.SRD[l] = t.SG[l] + jnp.sum(t.SYR[l], axis=0)
            for k in range(1, nz):
                s_z(l, k).start()

        def s_end(l):
            for k in range(1, nz):
                s_z(l, k).wait_recv()
            t.SRD[2 + l] = t.SRD[l] + jnp.sum(t.SZR[l], axis=0)
            to_owner(
                l, lambda cp: s_c(l, cp), lambda cp: pltpu.make_async_copy(t.SRD.at[2 + l], t.SCR.at[j], t.sc_r.at[j])
            )

        kept = list(spilled)

        def save(name):
            i = kept.index(name)
            return pltpu.make_async_copy(getattr(t, name), getattr(t, "o_" + name), t.keep.at[0, i])

        def fetch(name):
            i = kept.index(name)
            return pltpu.make_async_copy(getattr(t, "o_" + name), getattr(t, name), t.keep.at[1, i])

        def add_small(l, r, v):
            t.SG[l, pl.ds(r, 1), :] += v

        def put_small(l, r, acc):
            v = jnp.sum(acc, axis=0, keepdims=True)
            for q in range(4):
                add_small(l, 4 * r + q, v[:, q * TILE : (q + 1) * TILE])

        def own_rows(g, r):
            return pl.ds(pl.multiple_of((2 * g + x) * RP + r * RC, RC), RC)

        def attend(l, g, zz):
            rows_, cols = half(g), blk(zz, TILE)
            v = mm(t.NF[rows_, :], W[3 * l, :, cols], NN)
            t.PR[rows_, cols] = (v + t.SPS[l, pl.ds(24 + zz, 1), :]).astype(BF)
            live = lax.broadcasted_iota(jnp.int32, (RP, RP), 1) < SEQ
            for i in range(2):
                im = 2 * g + i
                b = t.PR[row(g, i), cols]
                q, k, v = b[:, 0:HD], b[:, HD : 2 * HD], b[:, 2 * HD : 3 * HD]
                s = jnp.where(live, mm(q, k, NT) * SCALE, -1e30)
                w = jnp.exp(s - jnp.max(s, axis=-1, keepdims=True))
                pb = (w * (1.0 / jnp.sum(w, axis=-1, keepdims=True))).astype(BF)
                t.PB[4 * im + zz] = pb
                put_mixed(l, row(g, i), zz, mm(pb, v, NN).astype(BF))

        def put_mixed(l, ri, zz, o):
            pair = t.MXC[l, ri, blk(zz // 2, 2 * HD)]
            up_half = lax.rem(zz, 2) == 1
            low, high = pair[:, :HD], pair[:, HD:]
            t.MXC[l, ri, blk(zz // 2, 2 * HD)] = jnp.concatenate(
                [jnp.where(up_half, low, o), jnp.where(up_half, o, high)], axis=1
            )

        def out_weights(l):
            for zz in range(4):
                t.WO[l, :, zz * HD : (zz + 1) * HD] = W[3 * l, :, zz * TILE + 3 * HD : (zz + 1) * TILE]

        def out_project(l, g):
            for n in range(4):
                cols = blk(n, TILE)
                OP[half(g), cols] = mm(t.MXC[l, half(g), :], t.WO[l, cols, :], NT).astype(BF)

        def project(lhs, lm, g):
            rows_ = half(g)

            def step(n):
                cols = blk(n, TILE)
                OP[rows_, cols] = mm(lhs[rows_, :], W[lm, cols, :], NT).astype(BF)

            for n in range(4):
                step(n)

        def up(l, g, zz):
            rows_, cols = half(g), blk(zz, TILE)
            u = mm(t.N2[rows_, :], W[3 * l + 1, :, cols], NN) + t.SPS[l, pl.ds(28 + zz, 1), :]
            cdf = 0.5 + 0.5 * lax.erf(u * (1.0 / math.sqrt(2.0)))
            t.H[rows_, cols] = (u * cdf).astype(BF)
            t.GD[rows_, cols] = (cdf + u * jnp.exp(-0.5 * u * u) * (1.0 / math.sqrt(2.0 * math.pi))).astype(BF)

        def pre(l, g):
            rows_ = half(g)

            def step(n):
                cols = blk(n, TILE)
                v = mm(t.GT[rows_, :], W[3 * l + 2, :, cols], NN) * t.GD[rows_, cols].astype(F32)
                gp = v.astype(BF)
                t.GD[rows_, cols] = gp
                add_small(l, 28 + n, jnp.sum(gp.astype(F32), axis=0, keepdims=True))

            for n in range(4):
                step(n)

        def weight_grad(buf, a, b):
            for r in range(4):
                cols = blk(r, TILE)
                buf[cols, :] = mm(a[:, cols], b[...], TN).astype(BF)

        def weight_grad_attn(l, buf):
            for r in range(4):
                cols = blk(r, TILE)
                v = mm(t.NF[:, cols], t.H[...], TN).astype(BF)
                o = mm(t.MX[:, cols], t.MXC[l], TN).astype(BF)
                for zz in range(4):
                    lo = zz * TILE
                    buf[cols, lo : lo + TILE] = jnp.concatenate(
                        [v[:, lo : lo + 3 * HD], o[:, zz * HD : (zz + 1) * HD]], axis=1
                    )

        def mixed_grad(l, g):
            t.GMC[half(g), :] = mm(t.MX[half(g), :], t.WO[l], NN).astype(BF)

        def attend_back(l, g):
            def step(i, _):
                im = 2 * g + i
                ri = blk(im, RP)
                for zz in range(4):
                    cols = blk(zz, TILE)
                    b = t.PR[ri, cols]
                    q, k, v = b[:, 0:HD], b[:, HD : 2 * HD], b[:, 2 * HD : 3 * HD]
                    gm = t.GMC[ri, zz * HD : (zz + 1) * HD]
                    pb = t.PB[4 * im + zz]
                    pf = pb.astype(F32)
                    gp = mm(gm, v, NT)
                    cen = jnp.sum(pf * gp, axis=-1, keepdims=True)
                    gsc = (pf * (gp - cen)).astype(BF)
                    gq = mm(gsc, k, NN) * SCALE
                    gk = mm(gsc, q, TN) * SCALE
                    gv = mm(pb, gm, TN)
                    out = jnp.concatenate([gq, gk, gv, jnp.zeros((RP, HD), F32)], axis=1).astype(BF)
                    t.H[ri, cols] = out
                    add_small(l, 24 + zz, jnp.sum(out.astype(F32), axis=0, keepdims=True))
                return 0

            lax.fori_loop(0, 2, step, 0)

        def swap(buf, got, i):
            return rcopy(buf.at[1 - x], got, t.lo_s.at[i], t.lo_r.at[i], p.dev(x=1 - x))

        def rows_loop(step, init=0, h=None):
            lo, hi = (0, RP // RC) if h is None else PARTS[h]
            return lax.fori_loop(lo, hi, step, init)

        take = [
            pltpu.make_async_copy(t.wq, t.WQ, t.io.at[6]),
            pltpu.make_async_copy(t.wo, t.WOS, t.io.at[7]),
            pltpu.make_async_copy(t.imgs.at[0:2], t.XO, t.io.at[0]),
            pltpu.make_async_copy(t.imgs.at[2], t.GT.at[row(c, 0)], t.io.at[1]),
            pltpu.make_async_copy(t.imgs.at[3], t.GT.at[row(c, 1)], t.io.at[8]),
        ]
        for cp in take:
            cp.start()
        for cp in take[:2]:
            cp.wait()
        for jp in range(4):
            parts = [t.WQ[:, k * TILE + jp * HD : k * TILE + (jp + 1) * HD] for k in range(3)]
            t.WA[jp] = jnp.concatenate(parts + [t.WOS[:, jp * HD : (jp + 1) * HD]], axis=1)
        t.SG[...] = jnp.zeros((2, 32, TILE), F32)
        t.MXC[...] = jnp.zeros((2, 4 * RP, TILE), BF)
        p.barrier()
        for k in range(4):
            small_red(k).start()
        for m in range(3):
            for k in (1, 2, 3, 0):
                red(m, k).start()
        for l in range(2):
            for cs in range(2):
                b = t.SPB.at[l, y, z, cs]
                pltpu.make_async_copy(b, b, t.pr.at[l, cs]).wait()
            for k in range(1, nz):
                small_z(l, k).start()
        for cp in take[2:]:
            cp.wait()
        tops = ag_local(t.GT, 4)
        for cp in tops:
            cp.start()
        release(0)
        for l in range(2):
            for k in range(1, nz):
                small_z(l, k).wait_recv()
            for k in range(1, Y):
                small_y(l, k).start()
        for l in range(2):
            for k in range(1, Y):
                small_y(l, k).wait_recv()
            t.SPS[l] = jnp.sum(t.SPB[l].astype(F32).reshape(Y * nz * 2, 32, TILE), axis=0)
            for r in range(6):
                for q in range(4):
                    t.G[l, r : r + 1, q * TILE : (q + 1) * TILE] = t.SPS[l, 4 * r + q : 4 * r + q + 1, :]

        def ln(l, g, b, load, buf, at):
            gain, shift = t.G[l, g : g + 1, :], t.G[l, b : b + 1, :]

            def step(r, _):
                buf[at(r), :] = norm_row(load(r), gain, shift).astype(BF)
                return 0

            rows_loop(step)

        for m in range(2):
            ln(
                0, 0, 2, lambda r, m=m: t.XO[m, blk(r, RC), :].astype(F32), t.NF,
                lambda r, m=m: pl.ds(pl.multiple_of((2 * c + m) * RP + r * RC, RC), RC),
            )
        first = ag_local(t.NF, 0)
        for cp in first:
            cp.start()
        release(1)
        pump(1)
        for cp in first:
            cp.wait_recv()

        for l in range(2):
            A, U, DN = 3 * l, 3 * l + 1, 3 * l + 2
            s = 2 * l
            if l:
                ag_in(t.NF, 0, 2)
            for k in range(4):
                ready(A, k)
                attend(l, 0, holds[k])
                if l == 0 or k < 2:
                    pump()
            if l:
                rs_done(0, 1)
                rs_done(1, 1)
            out_weights(l)
            out_project(l, 0)
            rs_out(0, s)
            if l:
                ag_mid(t.NF, 1, 2)
                ag_in(t.NF, 1, 2)
            for k in range(4):
                attend(l, 1, holds[k])
                if k % 2:
                    pump()
            out_project(l, 1)
            rs_out(1, s)
            if l == 0:
                for cp in first:
                    cp.wait_send()
                for name in ("NF", "PR", "PB"):
                    save(name).start()
            else:
                ag_done(t.NF, 2)

            def second(g, h):
                gain, shift, bias = t.G[l, 1:2, :], t.G[l, 4:5, :], t.G[l, 3:4, :]

                def step(r, _):
                    rs = blk(r, RC)
                    v = t.XO[x, rs, :] if l == 0 else t.OUT[0, rs, :]
                    mid = v.astype(F32) + sums(g, r) + bias
                    t.MID[l, rs, :] = mid
                    t.N2[own_rows(g, r), :] = norm_row(mid, gain, shift).astype(BF)
                    return 0

                rows_loop(step, 0, h)
                ag_send(t.N2, g, 1 + 2 * l, h)
                return 0

            pump()
            for g in range(2):
                rs_in(g, s, lambda h, _, g=g: second(g, h))
            pump()
            ag_mid(t.N2, 0, 1 + 2 * l)
            ag_in(t.N2, 0, 1 + 2 * l)
            if l:
                save("H").wait()
                save("GD").wait()
            for k in range(4):
                ready(U, k)
                up(l, 0, holds[k])
            ag_mid(t.N2, 1, 1 + 2 * l)
            pump()
            ag_in(t.N2, 1, 1 + 2 * l)
            for k in range(4):
                up(l, 1, holds[k])
            pump()
            ag_done(t.N2, 1 + 2 * l)
            rs_done(0, s)
            rs_done(1, s)
            if l == 0:
                for name in ("N2", "H", "GD"):
                    save(name).start()
                for name in ("NF", "PR", "PB"):
                    save(name).wait()
            else:
                for cp in tops:
                    cp.wait_recv()
                weight_grad(t.DX, t.GT, t.H)
                y_start(1, 2)
            for k in range(4):
                ready(DN, k)
            s = 2 * l + 1
            project(t.H, DN, 0)
            rs_out(0, s)
            pump()
            project(t.H, DN, 1)
            rs_out(1, s)
            pump()
            if l == 0:
                save("N2").wait()

                def last(g, h):
                    gain, shift, bias = t.G[1, 0:1, :], t.G[1, 2:3, :], t.G[0, 5:6, :]

                    def step(r, _):
                        rs = blk(r, RC)
                        o = (t.MID[0, rs, :] + sums(g, r) + bias).astype(BF)
                        t.OUT[0, rs, :] = o
                        t.NF[own_rows(g, r), :] = norm_row(o.astype(F32), gain, shift).astype(BF)
                        return 0

                    rows_loop(step, 0, h)
                    ag_send(t.NF, g, 2, h)
                    return 0

                for g in range(2):
                    rs_in(g, s, lambda h, _, g=g: last(g, h))
                pump()
                ag_mid(t.NF, 0, 2)

            else:
                for g in range(2):

                    @pl.when(c == g)
                    def _():
                        def step(r, _):
                            rs = blk(r, RC)
                            t.FIN[rs, :] = t.MID[1, rs, :] + OP[own_rows(g, r), :].astype(F32) + t.G[1, 5:6, :]
                            return 0

                        rows_loop(step)

        for k in range(1, 4):
            small_red(k).wait_send()
        for l in range(2):
            for k in range(1, nz):
                small_z(l, k).wait_send()
            for k in range(1, Y):
                small_y(l, k).wait_send()
        for m in range(3):
            for k in range(1, 4):
                red(m, k).wait_send()
        for lm in range(6):
            wz(lm, 1).wait_send()
            wz(lm, 2).wait_send()
            for k in (1, 2):

                @pl.when(inner == 1)
                def _():
                    wrelay(lm, k).wait_send()

            for k in range(4):
                for ky in range(1, Y):
                    wy(lm, k, ky).wait_send()

        def final_out(h):
            def step(r, _):
                rs = blk(r, RC)
                v = t.FIN[rs, :] + RB[1, x, rs, :].astype(F32) + XR[1, rs, :].astype(F32)
                t.OUT[1, rs, :] = v.astype(BF)
                return 0

            return rows_loop(step, 0, h)

        zero8 = jnp.zeros((8, D), F32)
        for l in (1, 0):
            A, U, DN = 3 * l, 3 * l + 1, 3 * l + 2
            s = 4 + 2 * (1 - l)
            if l == 0:
                ag_in(t.GT, 0, 6)
                fetch("GD").wait()
            rs_done(0, s - 1)
            rs_done(1, s - 1)
            pre(l, 0)
            project(t.GD, U, 0)
            rs_out(0, s)
            push()
            if l == 0:
                ag_mid(t.GT, 1, 6)
                ag_in(t.GT, 1, 6)
                fetch("H").wait()
                push_through(z_sum, 1, 2)
                for kz in range(nz):
                    for k in range(1, Y):
                        y_part(1, 2, k, kz).wait_send()
                z_sent(1, 2)
                weight_grad(t.DX, t.GT, t.H)
                push_through(y_sum, 1, 0)
                y_start(0, 2)
            pre(l, 1)
            project(t.GD, U, 1)
            rs_out(1, s)
            push()
            if l == 1:
                for cp in tops:
                    cp.wait_send()
            else:
                ag_done(t.GT, 6)

            def fill_up():
                if l == 0:
                    fetch("N2").wait()
                weight_grad(W.at[U], t.N2, t.GD)
                y_start(l, 1)
                if l == 1:
                    fetch("N2").start()
                    fetch("GD").start()

            def mid_back(g, h, init):
                def step(r, acc):
                    rs = blk(r, RC)
                    dy = sums(g, r)
                    top = t.GT[own_rows(g, r), :].astype(F32)
                    dx, dg = norm_back(t.MID[l, rs, :], t.G[l, 1:2, :], dy)
                    gmid = top + dx
                    t.GMID[rs, :] = gmid
                    t.MX[own_rows(g, r), :] = gmid.astype(BF)
                    return acc[0] + fold(dg), acc[1] + fold(dy), acc[2] + fold(gmid), acc[3] + fold(top)

                acc = rows_loop(step, init, h)
                ag_send(t.MX, g, s + 1, h)
                return acc

            def mid_end(acc):
                for i, r in enumerate((1, 4, 3, 5)):
                    put_small(l, r, acc[i])

            rs_in(0, s, lambda h, acc: mid_back(0, h, acc), (zero8,) * 4, mid_end)
            fill_up()
            rs_in(1, s, lambda h, acc: mid_back(1, h, acc), (zero8,) * 4, mid_end)
            push()
            if l == 0:
                for name in ("PR", "PB"):
                    fetch(name).wait()
            ag_mid(t.MX, 0, s + 1)
            ag_in(t.MX, 0, s + 1)
            push()
            mixed_grad(l, 0)
            attend_back(l, 0)
            push()
            rs_done(0, s)
            rs_done(1, s)
            project(t.H, A, 0)
            rs_out(0, s + 1)
            push()
            ag_mid(t.MX, 1, s + 1)
            ag_in(t.MX, 1, s + 1)
            mixed_grad(l, 1)
            attend_back(l, 1)
            push()
            project(t.H, A, 1)
            rs_out(1, s + 1)
            ag_done(t.MX, s + 1)
            if l == 1:
                push_through(y_sum, 1, 1)
            else:
                fetch("NF").wait()
                s_mid(1)
                push_through(y_sum, 0, 2)
            def first_back(g, h, init):
                def step(r, acc):
                    rs = blk(r, RC)
                    dy = sums(g, r)
                    v = (t.XO[x, rs, :] if l == 0 else t.OUT[0, rs, :]).astype(F32)
                    dx, dg = norm_back(v, t.G[l, 0:1, :], dy)
                    gx = (t.GMID[rs, :] + dx).astype(BF)
                    t.IGB[l, rs, :] = gx
                    if l == 1:
                        t.GT[own_rows(g, r), :] = gx
                    return acc[0] + fold(dg), acc[1] + fold(dy)

                acc = rows_loop(step, init, h)
                if l == 1:
                    ag_send(t.GT, g, 6, h)
                return acc

            def first_end(acc):
                put_small(l, 0, acc[0])
                put_small(l, 2, acc[1])

            if l == 0:
                swap(t.OUT, t.LOB, 0).start()

            def fill_attn():
                weight_grad_attn(l, W.at[A])
                y_start(l, 0)
                if l == 1:
                    for name in ("H", "PR", "PB", "NF"):
                        fetch(name).start()

            if l == 0:
                fill_attn()
            rs_in(0, s + 1, lambda h, acc: first_back(0, h, acc), (zero8,) * 2, first_end)
            if l == 1:
                fill_attn()
            rs_in(1, s + 1, lambda h, acc: first_back(1, h, acc), (zero8,) * 2, first_end)
            if l == 1:
                for g in range(2):
                    rs_in(g, 3, lambda h, _: final_out(h))
            s_start(l)

            if l == 1:
                ag_mid(t.GT, 0, 6)

        swap(t.IGB, t.LGB, 1).start()
        s_end(1)
        push(100)
        s_mid(0)
        s_end(0)
        give = []
        for i, (buf, got, out) in enumerate(((t.OUT, t.LOB, t.lo), (t.IGB, t.LGB, t.ig))):
            cp = swap(buf, got, i)
            cp.wait_recv()
            cp.wait_send()
            give.append(pltpu.make_async_copy(buf.at[x], out.at[x], t.io.at[2 + 2 * i]))
            give.append(pltpu.make_async_copy(got, out.at[1 - x], t.io.at[3 + 2 * i]))
            for cp in give[-2:]:
                cp.start()
        for m in (2, 1, 0):
            for jj in range(4):
                b = t.CR.at[m, jj]
                pltpu.make_async_copy(b, b, t.c_r.at[m, jj]).wait()
                give.append(pltpu.make_async_copy(b, t.cr.at[m, :, blk(jj, TILE)], t.cr_s.at[m, jj]))
                give[-1].start()
        for jj in range(4):
            b = t.SCR.at[jj]
            pltpu.make_async_copy(b, b, t.sc_r.at[jj]).wait()
            t.gs_out[jj] = t.SCR[jj]
        for cp in give:
            cp.wait()
        for g in range(2):
            rs_done(g, 7)
        for h in range(2):
            chip_part(3, h).wait_send()
        for l in range(2):
            for m in range(3 if l == 0 else 2):
                for kz in range(nz):
                    for k in range(1, Y):
                        y_part(l, m, k, kz).wait_send()
                z_sent(l, m)
            for k in range(1, Y):
                s_y(l, k).wait_send()
            for k in range(1, nz):
                s_z(l, k).wait_send()
            for cp in range(2):

                @pl.when(jnp.logical_not(jnp.logical_and(x == l, c == cp)))
                def _():
                    s_c(l, cp).wait_send()
                    for m in range(3):
                        c_part(l, m, cp).wait_send()

    vm = pl.BlockSpec(memory_space=pltpu.VMEM)
    hbm = pl.BlockSpec(memory_space=pl.ANY)
    return pl.pallas_call(
        body,
        out_shape=[jax.ShapeDtypeStruct(*a) for a in outputs.values()]
        + [jax.ShapeDtypeStruct(a, BF) for a in spilled.values()],
        in_specs=[hbm] * 6,
        out_specs=[hbm] * (len(outputs) - 1) + [vm] + [hbm] * len(spilled),
        scratch_shapes=[pltpu.VMEM(*a) for a in vmem.values()] + [dma(a) for a in sems.values()],
        compiler_params=pltpu.CompilerParams(
            collective_id=0, has_side_effects=True, vmem_limit_bytes=VMEM_LIMIT
        ),
    )


def small_pack(norm_gains, row_shifts, head_bias, unit_bias, dpn, nz):
    dp, z = lax.axis_index("dp"), lax.axis_index("tensor")
    rows = jnp.concatenate([norm_gains[0], row_shifts[0]], axis=0)
    w = rows.shape[1]
    rows = lax.dynamic_update_slice(jnp.zeros((6, D), BF), rows, (0, (dp * nz + z) * w)).reshape(1, 24, TILE)
    hw, uw = head_bias.shape[3], unit_bias.shape[2]
    head = jnp.zeros((4, 4, TILE), BF)
    head = lax.dynamic_update_slice(head, head_bias[0, 0][:, None], (0, z, dp * hw))
    head = lax.dynamic_update_slice(head, head_bias[0, 1][:, None], (0, z, 2 * HD + dp * hw))
    unit = lax.dynamic_update_slice(jnp.zeros((4, 4, TILE), BF), unit_bias[0][:, None], (0, z, dp * uw))
    return jnp.concatenate([jnp.broadcast_to(rows, (4, 24, TILE)), head, unit], axis=1)


def solution(mesh):
    dpn, nz = mesh.shape["dp"], mesh.shape["tensor"]

    def on_device(
        images_in, cotangent, w_qkv, w_out, w_up, w_down, norm_gains, row_shifts, head_bias, unit_bias
    ):
        R = w_up.shape[1]
        sp = small_pack(norm_gains, row_shifts, head_bias, unit_bias, dpn, nz)
        imgs = jnp.pad(jnp.concatenate([images_in, cotangent]), ((0, 0), (0, RP - SEQ), (0, 0)))
        lo, ig, cr, gs = both_layers(dpn, nz, R)(
            imgs, w_qkv[0].reshape(R, 3 * TILE), w_out[0], w_up[0], w_down[0], sp
        )[:4]
        lo, ig = lo[:, :SEQ], ig[:, :SEQ]
        gu, gd = cr[1].astype(F32), cr[2].astype(F32)
        dp, z = lax.axis_index("dp"), lax.axis_index("tensor")
        ga = cr[0].astype(F32).reshape(R, 4, TILE)
        g_qkv = ga[:, :, : 3 * HD].reshape(R, 4, 3, HD).transpose(0, 2, 1, 3).reshape(w_qkv.shape)
        g_out = ga[:, :, 3 * HD :].reshape(w_out.shape)
        w, hw, uw = norm_gains.shape[2], head_bias.shape[3], unit_bias.shape[2]
        rows = lax.dynamic_slice(jnp.sum(gs[:, :24], axis=0).reshape(6, D), (0, (dp * nz + z) * w), (6, w))
        head = lax.dynamic_slice(gs, (0, 24 + z, 0), (4, 1, TILE))[:, 0]
        unit = lax.dynamic_slice(gs, (0, 28 + z, dp * uw), (4, 1, uw))[:, 0]
        g_head = jnp.stack([lax.dynamic_slice(head, (0, o + dp * hw), (4, hw)) for o in (0, 2 * HD)])
        return (
            lo[None], ig[None], g_qkv, g_out, gu[None], gd[None],
            rows[None, :2], rows[None, 2:], g_head[None], unit[None],
        )

    in_specs = (
        P(None, ("dp", "tensor"), None),
        P(None, ("dp", "tensor"), None),
        P("section", "dp", None, "tensor"),
        P("section", "dp", "tensor"),
        P("section", "dp", "tensor"),
        P("section", "dp", "tensor"),
        P("section", None, ("dp", "tensor")),
        P("section", None, ("dp", "tensor")),
        P("section", None, "tensor", "dp"),
        P("section", "tensor", "dp"),
    )
    out_specs = (
        P("section", None, ("dp", "tensor"), None),
        P("section", None, ("dp", "tensor"), None),
        P("section", "dp", None, "tensor"),
        P("section", "dp", "tensor"),
        P("section", "dp", "tensor"),
        P("section", "dp", "tensor"),
        P("section", None, ("dp", "tensor")),
        P("section", None, ("dp", "tensor")),
        P("section", None, "tensor", "dp"),
        P("section", "tensor", "dp"),
    )
    return jax.shard_map(
        on_device, mesh=mesh, in_specs=in_specs, out_specs=out_specs, check_vma=False
    )
```

```python
import math
import types

import jax
import jax.numpy as jnp
from jax import lax
from jax.experimental import pallas as pl
from jax.experimental.pallas import tpu as pltpu
from jax.sharding import PartitionSpec as P

D = 1024
HD = 64
SEQ = 197
RP = 208
RC = 16
PARTS = ((0, 7), (7, 13))
TILE = 256
SCALE = 0.125
EPS = 1e-06
MESH = pl.DeviceIdType.MESH
BF = jnp.bfloat16
F32 = jnp.float32
NN = (((1,), (0,)), ((), ()))
NT = (((1,), (1,)), ((), ()))
TN = (((0,), (0,)), ((), ()))
VMEM_LIMIT = 62 * 2**20


def mm(a, b, dims):
    return lax.dot_general(a, b, dims, preferred_element_type=F32)


def blk(i, size):
    if isinstance(i, int):
        return pl.ds(i * size, size)
    return pl.ds(pl.multiple_of(i * size, size), size)


class Place:
    def __init__(self, dpn, nz):
        self.Y, self.nz = dpn // 2, nz
        self.x = lax.axis_index("section")
        dp = lax.axis_index("dp")
        self.z = lax.axis_index("tensor")
        self.y, self.c = dp // 2, lax.rem(dp, 2)
        self.j = 2 * self.x + self.c

    def dev(self, x=None, y=None, c=None, z=None):
        x = self.x if x is None else x
        y = self.y if y is None else y
        c = self.c if c is None else c
        z = self.z if z is None else z
        return (x, 2 * y + c, z)

    def cell(self, k):
        jp = lax.rem(self.j + k, 4)
        return jp, jp // 2, lax.rem(jp, 2)

    def yk(self, k):
        return lax.rem(self.y + k, self.Y)

    def zk(self, k):
        return lax.rem(self.z + k, self.nz)

    def barrier(self):
        bar = pltpu.get_barrier_semaphore()
        n = 0
        for k in range(1, 4):
            _, xp, cp = self.cell(k)
            pl.semaphore_signal(bar, inc=1, device_id=self.dev(x=xp, c=cp), device_id_type=MESH)
            n += 1
        for k in range(1, self.nz):
            pl.semaphore_signal(bar, inc=1, device_id=self.dev(z=self.zk(k)), device_id_type=MESH)
            n += 1
        for k in range(1, self.Y):
            pl.semaphore_signal(bar, inc=1, device_id=self.dev(y=self.yk(k)), device_id_type=MESH)
            n += 1
        pl.semaphore_wait(bar, n)


def rcopy(src, dst, ss, rs, dev):
    return pltpu.make_async_remote_copy(
        src_ref=src, dst_ref=dst, send_sem=ss, recv_sem=rs, device_id=dev, device_id_type=MESH
    )


def norm_row(v, g, b):
    cen = v - jnp.sum(v, axis=-1, keepdims=True) * (1.0 / D)
    var = jnp.sum(cen * cen, axis=-1, keepdims=True) * (1.0 / D)
    return cen * lax.rsqrt(var + EPS) * g + b


def norm_back(v, g, dy):
    cen = v - jnp.sum(v, axis=-1, keepdims=True) * (1.0 / D)
    rstd = lax.rsqrt(jnp.sum(cen * cen, axis=-1, keepdims=True) * (1.0 / D) + EPS)
    hat = cen * rstd
    dh = dy * g
    a = jnp.sum(dh, axis=-1, keepdims=True) * (1.0 / D)
    b = jnp.sum(dh * hat, axis=-1, keepdims=True) * (1.0 / D)
    return rstd * (dh - a - hat * b), dy * hat


def fold(v):
    return v[0:8] + v[8:16]


def half(g):
    return blk(g, 2 * RP)


def row(g, m):
    return blk(2 * g + m, RP)


def both_layers(dpn, nz, rows):
    Y, R = dpn // 2, rows
    R2 = 2 * R
    full = (4 * RP, D)
    dma = pltpu.SemaphoreType.DMA
    inputs = ["imgs", "wq", "wo", "wu", "wd", "sp"]
    outputs = {
        "lo": ((2, RP, D), BF), "ig": ((2, RP, D), BF), "cr": ((3, R, D), BF), "gs_out": ((4, 32, TILE), F32),
    }
    spilled = {"NF": full, "PR": full, "N2": full, "H": full, "GD": full, "PB": (16, RP, RP)}
    vmem = {
        "W": ((6, D, D), BF), "DX": ((D, D), BF), "WQ": ((R, 3 * TILE), BF), "WOS": ((R, TILE), BF), "WA": ((4, R, TILE), BF), "SPB": ((2, Y, nz, 2, 32, TILE), BF), "SPS": ((2, 32, TILE), F32),
        "G": ((2, 8, D), F32), "NF": (full, BF), "PR": (full, BF), "N2": (full, BF), "H": (full, BF), "GD": (full, BF),
        "PB": ((16, RP, RP), BF), "MX": (full, BF), "MXC": ((2, 4 * RP, TILE), BF), "GMC": ((4 * RP, TILE), BF), "WO": ((2, D, TILE), BF), "GT": (full, BF), "OP": (full, BF), "RB": ((2, 2, RP, D), BF),
        "CS": ((2, RP, D), BF), "XR": ((2, RP, D), BF), "XO": ((2, RP, D), BF), "MID": ((2, RP, D), F32),
        "OUT": ((2, RP, D), BF), "LOB": ((RP, D), BF), "GMID": ((RP, D), F32), "FIN": ((RP, D), F32), "IGB": ((2, RP, D), BF),
        "LGB": ((RP, D), BF), "YR": ((3, Y - 1, R2, D), BF), "ZR": ((6, 2, R2, TILE), BF), "ZC": ((6, 2, R2, TILE), BF), "ZF": ((2, D, TILE // 2), BF), "ZFC": ((2, D, TILE // 2), BF),
        "RD": ((6, 2, R, TILE), BF), "CR": ((3, 4, R, TILE), BF), "SG": ((2, 32, TILE), F32),
        "SYR": ((2, Y - 1, 32, TILE), F32), "SZR": ((2, nz - 1, 32, TILE), F32), "SRD": ((4, 32, TILE), F32),
        "SCR": ((4, 32, TILE), F32),
    }
    sems = {
        "red_s": (3, 4), "red_r": (6, 2), "fz_s": (6, 4), "fz_r": (6, 4), "fy_s": (6, 4, Y), "fy_r": (6, 4, Y),
        "ps": (4 + 2 * nz + 2 * Y,), "pr": (6, max(nz, Y, 2)), "gs": (8, 6), "gr": (8, 6), "ss": (8, 4), "sr": (8, 4),
        "lo_s": (2,), "lo_r": (2,), "io": (9,), "cr_s": (3, 4), "keep": (2, 6), "y_s": (6, Y, nz), "y_r": (6, Y, nz), "z_s": (6, 4), "z_r": (6, 4), "zf_s": (4,), "zf_r": (4,), "zy_s": (Y,), "zy_r": (Y,),
        "c_s": (6, 2), "c_r": (3, 4), "sy_s": (2, Y), "sy_r": (2, Y), "sz_s": (2, nz), "sz_r": (2, nz), "sc_s": (2, 2),
        "sc_r": (4,),
    }
    names = inputs + list(outputs) + ["o_" + n for n in spilled] + list(vmem) + list(sems)

    def body(*refs):
        t = types.SimpleNamespace(**dict(zip(names, refs)))
        p = Place(dpn, nz)
        x, y, c, z, j = p.x, p.y, p.c, p.z, p.j
        near, far = x, 1 - x
        W, OP, RB, CS, XR = t.W, t.OP, t.RB, t.CS, t.XR

        def core_part(g, m, s):
            return rcopy(OP.at[row(g, m)], RB.at[int(s == 3), m], t.ss.at[s, m], t.sr.at[s, m], p.dev(c=1 - c))

        def chip_part(s, h):
            k, rs = int(s == 3), pl.ds(PARTS[h][0] * RC, (PARTS[h][1] - PARTS[h][0]) * RC)
            return rcopy(CS.at[k, rs], XR.at[k, rs], t.ss.at[s, 2 + h], t.sr.at[s, 2 + h], p.dev(x=1 - x))

        def rs_out(g, s):
            @pl.when(c != g)
            def _():
                core_part(g, far, s).start()
                core_part(g, near, s).start()

            @pl.when(c == g)
            def _():
                core_part(g, far, s).wait_recv()
                k = int(s == 3)
                for h, (lo, hi) in enumerate(PARTS):
                    rs = pl.ds(lo * RC, (hi - lo) * RC)
                    src_rows = pl.ds(pl.multiple_of((2 * g + far) * RP + lo * RC, RC), (hi - lo) * RC)
                    CS[k, rs, :] = (OP[src_rows, :].astype(F32) + RB[k, far, rs, :].astype(F32)).astype(BF)
                    chip_part(s, h).start()

        def rs_in(g, s, fn, init=0, end=None):
            @pl.when(c == g)
            def _():
                core_part(g, near, s).wait_recv()
                acc = init
                for h in range(2):
                    chip_part(s, h).wait_recv()
                    acc = fn(h, acc)
                if end is not None:
                    end(acc)

        def rs_done(g, s):
            @pl.when(c != g)
            def _():
                for m in range(2):
                    core_part(g, m, s).wait_send()

            if s != 3:

                @pl.when(c == g)
                def _():
                    for h in range(2):
                        chip_part(s, h).wait_send()

        def sums(g, r):
            rs = blk(r, RC)
            own = OP[pl.ds(pl.multiple_of((2 * g + x) * RP + r * RC, RC), RC), :].astype(F32)
            return own + RB[0, x, rs, :].astype(F32) + XR[0, rs, :].astype(F32)

        def ag_part(buf, g, s, k, h):
            lo, hi = PARTS[h]
            m = far if k == 2 else near
            b = buf.at[pl.ds(pl.multiple_of((2 * g + m) * RP + lo * RC, RC), (hi - lo) * RC)]
            i = 2 * k + h
            return rcopy(b, b, t.gs.at[s, i], t.gr.at[s, i], p.dev(x=1 - x) if k == 1 else p.dev(c=1 - c))

        def ag_send(buf, g, s, h):
            ag_part(buf, g, s, 1, h).start()
            ag_part(buf, g, s, 0, h).start()

        def ag_mid(buf, g, s):
            @pl.when(c == g)
            def _():
                for h in range(2):
                    ag_part(buf, g, s, 1, h).wait_recv()
                    ag_part(buf, g, s, 2, h).start()

        def ag_in(buf, g, s):
            @pl.when(c != g)
            def _():
                for h in range(2):
                    ag_part(buf, g, s, 0, h).wait_recv()
                    ag_part(buf, g, s, 2, h).wait_recv()

        def ag_done(buf, s):
            for g in range(2):

                @pl.when(c == g)
                def _():
                    for h in range(2):
                        for k in range(3):
                            ag_part(buf, g, s, k, h).wait_send()

        def ag_local(buf, s):
            return [
                rcopy(buf.at[row(c, m)], buf.at[row(c, m)], t.gs.at[s, m], t.gr.at[s, m], p.dev(c=1 - c))
                for m in range(2)
            ]

        def small_red(k):
            jp, xp, cp = p.cell(k)
            dst = t.SPB.at[x, y, z, c]
            if k == 0:
                return pltpu.make_async_copy(t.sp.at[jp], dst, t.pr.at[x, c])
            return rcopy(t.sp.at[jp], dst, t.ps.at[k], t.pr.at[x, c], p.dev(x=xp, c=cp))

        def small_z(l, k):
            b = t.SPB.at[l, y, z]
            return rcopy(b, b, t.ps.at[4 + l * nz + k], t.pr.at[2 + l, k], p.dev(z=p.zk(k)))

        def small_y(l, k):
            b = t.SPB.at[l, y]
            return rcopy(b, b, t.ps.at[4 + 2 * nz + l * Y + k], t.pr.at[4 + l, k], p.dev(y=p.yk(k)))

        src = (t.WA, t.wu, t.wd)
        inner = lax.rem((z + 1) // 2, 2)
        mate = z + 1 - 2 * lax.rem(z, 2)
        cross = 2 - z // 2
        other = 3 - 3 * (z // 2)
        sides = (z, mate, cross, other)
        holds = (z, mate + inner * (cross - mate), cross + inner * (other - cross), other + inner * (mate - other))

        def red(m, k):
            jp, xp, cp = p.cell(k)
            b = src[m].at[jp] if m == 0 else src[m].at[:, blk(jp, TILE)]
            dst = W.at[x * 3 + m, blk(2 * y + c, R), blk(z, TILE)]
            if k == 0:
                return pltpu.make_async_copy(b, dst, t.red_r.at[x * 3 + m, c])
            return rcopy(b, dst, t.red_s.at[m, k], t.red_r.at[x * 3 + m, c], p.dev(x=xp, c=cp))

        def chunk(lm, k):
            return W.at[lm, blk(y, R2), blk(holds[k], TILE)]

        def wz(lm, k):
            b = chunk(lm, 0)
            if k == 1:
                return rcopy(b, b, t.fz_s.at[lm, 0], t.fz_r.at[lm, 3 - 2 * inner], p.dev(z=mate))
            return rcopy(b, b, t.fz_s.at[lm, 1], t.fz_r.at[lm, 2 - inner], p.dev(z=cross))

        def wrelay(lm, k):
            b = chunk(lm, k)
            return rcopy(b, b, t.fz_s.at[lm, k + 1], t.fz_r.at[lm, k + 1], p.dev(z=mate))

        def wy(lm, k, ky):
            b = chunk(lm, k)
            return rcopy(b, b, t.fy_s.at[lm, k, ky], t.fy_r.at[lm, k, ky], p.dev(y=p.yk(ky)))

        def release(lm):
            for cs in range(2):
                b = W.at[lm, blk(2 * y + cs, R), blk(z, TILE)]
                pltpu.make_async_copy(b, b, t.red_r.at[lm, cs]).wait()
            wz(lm, 2).start()
            wz(lm, 1).start()
            for ky in range(1, Y):
                wy(lm, 0, ky).start()

        def hand_on(lm, k):
            pltpu.make_async_copy(chunk(lm, k), chunk(lm, k), t.fz_r.at[lm, k]).wait()
            if k < 3:

                @pl.when(inner == 1)
                def _():
                    wrelay(lm, k).start()

            for ky in range(1, Y):
                wy(lm, k, ky).start()
            if k == 3 and lm + 2 < 6:
                release(lm + 2)

        queue = [(lm, k) for lm in range(6) for k in (1, 2, 3)]
        handed = []

        def pump(n=1):
            for _ in range(n):
                if queue:
                    lm, k = queue.pop(0)
                    hand_on(lm, k)
                    handed.append((lm, k))

        def ready(lm, k):
            while k and (lm, k) not in handed:
                pump()
            for ky in range(1, Y):
                wy(lm, k, ky).wait_recv()

        def where(l, m):
            return t.DX if m == 2 else W.at[3 * l + m]

        def usual(l, m, zz):
            if (l, m) == (0, 2):
                return pl.ds(pl.multiple_of(zz * TILE + TILE // 2, TILE // 2), TILE // 2)
            return blk(zz, TILE)

        def take(l, m):
            return slice(0, TILE // 2) if (l, m) == (0, 2) else slice(0, TILE)

        def y_part(l, m, k, kz):
            cols = usual(l, m, sides[kz])
            return rcopy(
                where(l, m).at[blk(p.yk(k), R2), cols], t.YR.at[m, k - 1, :, cols],
                t.y_s.at[3 * l + m, k, kz], t.y_r.at[3 * l + m, k, kz], p.dev(y=p.yk(k)),
            )

        def z_part(l, m, k):
            n = 3 * l + m
            b = where(l, m).at[blk(y, R2), usual(l, m, sides[k])]
            if k == 1:
                return rcopy(b, t.ZR.at[n, 0, :, take(l, m)], t.z_s.at[n, 1], t.z_r.at[n, 0], p.dev(z=mate))
            return rcopy(b, t.ZC.at[n, k - 2, :, take(l, m)], t.z_s.at[n, k], t.z_r.at[n, k], p.dev(z=mate))

        def z_over(l, m, k):
            n = 3 * l + m
            b = where(l, m).at[blk(y, R2), usual(l, m, sides[k])]
            return rcopy(b, t.ZR.at[n, 1, :, take(l, m)], t.z_s.at[n, k], t.z_r.at[n, 1], p.dev(z=sides[k]))

        order = (3, 2, 1, 0)

        def y_start(l, m):
            begun.add((l, m))
            for kz in order:
                for k in range(1, Y):
                    y_part(l, m, k, kz).start()

        begun = set()

        def y_sum(l, m, kz):
            cols = usual(l, m, sides[kz])
            buf = where(l, m)
            for k in range(1, Y):
                y_part(l, m, k, kz).wait_recv()
            v = buf[blk(y, R2), cols].astype(F32)
            for k in range(1, Y):
                v = v + t.YR[m, k - 1, :, cols].astype(F32)
            buf[blk(y, R2), cols] = v.astype(BF)
            if kz == 1:
                z_part(l, m, 1).start()
            elif kz:

                @pl.when(inner == 0)
                def _():
                    z_part(l, m, kz).start()

        def z_mid(l, m, k):
            @pl.when(inner == 1)
            def _():
                z_part(l, m, k).wait_recv()
                buf, cols = where(l, m), usual(l, m, sides[k])
                v = buf[blk(y, R2), cols].astype(F32) + t.ZC[3 * l + m, k - 2, :, take(l, m)].astype(F32)
                buf[blk(y, R2), cols] = v.astype(BF)
                z_over(l, m, k).start()

        def z_sent(l, m):
            for k in (1, 2, 3):
                z_part(l, m, k).wait_send()

        def zf_cols(zz):
            return pl.ds(pl.multiple_of(zz * TILE, TILE), TILE // 2)

        def zf_part(k):
            b = t.DX.at[:, zf_cols(sides[k])]
            dst = t.ZF.at[0] if k == 1 else t.ZFC.at[k - 2]
            return rcopy(b, dst, t.zf_s.at[k], t.zf_r.at[0 if k == 1 else k], p.dev(z=mate))

        def zf_over(k):
            return rcopy(t.DX.at[:, zf_cols(sides[k])], t.ZF.at[1], t.zf_s.at[k], t.zf_r.at[1], p.dev(z=sides[k]))

        def zf_start():
            @pl.when(inner == 0)
            def _():
                zf_part(3).start()
                zf_part(2).start()

            zf_part(1).start()

        def zf_mid(l, m, k):
            @pl.when(inner == 1)
            def _():
                zf_part(k).wait_recv()
                cols = zf_cols(sides[k])
                t.DX[:, cols] = (t.DX[:, cols].astype(F32) + t.ZFC[k - 2].astype(F32)).astype(BF)
                zf_over(k).start()

        def zf_y(k):
            b = t.DX.at[blk(p.yk(k), R2), zf_cols(z)]
            dst = t.YR.at[2, k - 1, :, zf_cols(z)]
            return rcopy(b, dst, t.zy_s.at[k], t.zy_r.at[k], p.dev(y=p.yk(k)))

        def zf_sum(l, m):
            zf_part(1).wait_recv()
            zf_over(2).wait_recv()
            cols = zf_cols(z)
            v = t.DX[:, cols].astype(F32) + t.ZF[0].astype(F32) + t.ZF[1].astype(F32)
            t.DX[:, cols] = v.astype(BF)
            for k in range(1, Y):
                zf_y(k).start()

        def zf_end(l, m):
            for k in range(1, Y):
                zf_y(k).wait_recv()
            v = t.DX[blk(y, R2), zf_cols(z)].astype(F32)
            for k in range(1, Y):
                v = v + t.YR[2, k - 1, :, zf_cols(z)].astype(F32)
            t.RD[2, :, :, 0 : TILE // 2] = v.astype(BF).reshape(2, R, TILE // 2)

        def c_part(l, m, cp):
            lm = 3 * l + m
            return rcopy(t.RD.at[lm, cp], t.CR.at[m, j], t.c_s.at[lm, cp], t.c_r.at[m, j], p.dev(x=l, c=cp))

        def to_owner(l, remote, local):
            for cp in range(2):
                mine = jnp.logical_and(x == l, c == cp)

                @pl.when(mine)
                def _():
                    local(cp).start()

                @pl.when(jnp.logical_not(mine))
                def _():
                    remote(cp).start()

        def z_sum(l, m):
            lm = 3 * l + m
            z_part(l, m, 1).wait_recv()
            z_over(l, m, 2).wait_recv()
            v = where(l, m)[blk(y, R2), usual(l, m, z)].astype(F32)
            v = v + t.ZR[lm, 0, :, take(l, m)].astype(F32) + t.ZR[lm, 1, :, take(l, m)].astype(F32)
            if (l, m) == (0, 2):
                t.RD[lm, :, :, TILE // 2 :] = v.astype(BF).reshape(2, R, TILE // 2)
            else:
                t.RD[lm] = v.astype(BF).reshape(2, R, TILE)
            to_owner(
                l, lambda cp: c_part(l, m, cp),
                lambda cp: pltpu.make_async_copy(t.RD.at[lm, cp], t.CR.at[m, j], t.c_r.at[m, j]),
            )

        def s_y(l, k):
            return rcopy(t.SG.at[l], t.SYR.at[l, k - 1], t.sy_s.at[l, k], t.sy_r.at[l, k], p.dev(y=p.yk(k)))

        def s_z(l, k):
            return rcopy(t.SRD.at[l], t.SZR.at[l, k - 1], t.sz_s.at[l, k], t.sz_r.at[l, k], p.dev(z=p.zk(k)))

        def s_c(l, cp):
            return rcopy(t.SRD.at[2 + l], t.SCR.at[j], t.sc_s.at[l, cp], t.sc_r.at[j], p.dev(x=l, c=cp))

        def s_start(l):
            begun.add((l,))
            for k in range(1, Y):
                s_y(l, k).start()

        def s_mid(l):
            for k in range(1, Y):
                s_y(l, k).wait_recv()
            t.SRD[l] = t.SG[l] + jnp.sum(t.SYR[l], axis=0)
            for k in range(1, nz):
                s_z(l, k).start()

        def s_end(l):
            for k in range(1, nz):
                s_z(l, k).wait_recv()
            t.SRD[2 + l] = t.SRD[l] + jnp.sum(t.SZR[l], axis=0)
            to_owner(
                l, lambda cp: s_c(l, cp), lambda cp: pltpu.make_async_copy(t.SRD.at[2 + l], t.SCR.at[j], t.sc_r.at[j])
            )

        steps = []
        for n in range(6):
            l, m = 1 - n // 3, 2 - n % 3
            ys = [(y_sum, (l, m, k)) for k in order]
            zs = [(z_mid, (l, m, 3)), (z_mid, (l, m, 2))]
            last = [(z_sum, (1 - (n - 1) // 3, 2 - (n - 1) % 3))] if n else []
            if n == 3:
                steps += ys[:2] + [(zf_mid, (0, 2, 3))] + ys[2:] + [(zf_mid, (0, 2, 2))] + zs + last
            elif n == 4:
                steps += ys[:2] + [(zf_sum, (0, 2))] + ys[2:] + zs
            elif n == 5:
                steps += ys + [(s_mid, (0,))] + zs + last + [(zf_end, (0, 2)), (z_sum, (0, 2)), (s_end, (0,))]
            else:
                steps += ys + zs + last
        steps.append((z_sum, (0, 0)))

        def push(n=1):
            for _ in range(n):
                if steps and steps[0][1][:2] in begun:
                    f, a = steps.pop(0)
                    f(*a)

        def push_through(f, l, m):
            while any(g is f and a[:2] == (l, m) for g, a in steps):
                push()

        kept = list(spilled)

        def save(name):
            i = kept.index(name)
            return pltpu.make_async_copy(getattr(t, name), getattr(t, "o_" + name), t.keep.at[0, i])

        def fetch(name):
            i = kept.index(name)
            return pltpu.make_async_copy(getattr(t, "o_" + name), getattr(t, name), t.keep.at[1, i])

        def add_small(l, r, v):
            t.SG[l, pl.ds(r, 1), :] += v

        def put_small(l, r, acc):
            v = jnp.sum(acc, axis=0, keepdims=True)
            for q in range(4):
                add_small(l, 4 * r + q, v[:, q * TILE : (q + 1) * TILE])

        def own_rows(g, r):
            return pl.ds(pl.multiple_of((2 * g + x) * RP + r * RC, RC), RC)

        def attend(l, g, zz):
            rows_, cols = half(g), blk(zz, TILE)
            v = mm(t.NF[rows_, :], W[3 * l, :, cols], NN)
            t.PR[rows_, cols] = (v + t.SPS[l, pl.ds(24 + zz, 1), :]).astype(BF)
            live = lax.broadcasted_iota(jnp.int32, (RP, RP), 1) < SEQ
            for i in range(2):
                im = 2 * g + i
                b = t.PR[row(g, i), cols]
                q, k, v = b[:, 0:HD], b[:, HD : 2 * HD], b[:, 2 * HD : 3 * HD]
                s = jnp.where(live, mm(q, k, NT) * SCALE, -1e30)
                w = jnp.exp(s - jnp.max(s, axis=-1, keepdims=True))
                pb = (w * (1.0 / jnp.sum(w, axis=-1, keepdims=True))).astype(BF)
                t.PB[4 * im + zz] = pb
                put_mixed(l, row(g, i), zz, mm(pb, v, NN).astype(BF))

        def put_mixed(l, ri, zz, o):
            pair = t.MXC[l, ri, blk(zz // 2, 2 * HD)]
            up_half = lax.rem(zz, 2) == 1
            low, high = pair[:, :HD], pair[:, HD:]
            t.MXC[l, ri, blk(zz // 2, 2 * HD)] = jnp.concatenate(
                [jnp.where(up_half, low, o), jnp.where(up_half, o, high)], axis=1
            )

        def out_weights(l):
            for zz in range(4):
                t.WO[l, :, zz * HD : (zz + 1) * HD] = W[3 * l, :, zz * TILE + 3 * HD : (zz + 1) * TILE]

        def out_project(l, g):
            for n in range(4):
                cols = blk(n, TILE)
                OP[half(g), cols] = mm(t.MXC[l, half(g), :], t.WO[l, cols, :], NT).astype(BF)

        def project(lhs, lm, g):
            rows_ = half(g)

            def step(n):
                cols = blk(n, TILE)
                OP[rows_, cols] = mm(lhs[rows_, :], W[lm, cols, :], NT).astype(BF)

            for n in range(4):
                step(n)

        def up(l, g, zz):
            rows_, cols = half(g), blk(zz, TILE)
            u = mm(t.N2[rows_, :], W[3 * l + 1, :, cols], NN) + t.SPS[l, pl.ds(28 + zz, 1), :]
            cdf = 0.5 + 0.5 * lax.erf(u * (1.0 / math.sqrt(2.0)))
            t.H[rows_, cols] = (u * cdf).astype(BF)
            t.GD[rows_, cols] = (cdf + u * jnp.exp(-0.5 * u * u) * (1.0 / math.sqrt(2.0 * math.pi))).astype(BF)

        def pre(l, g):
            rows_ = half(g)

            def step(n):
                cols = blk(n, TILE)
                v = mm(t.GT[rows_, :], W[3 * l + 2, :, cols], NN) * t.GD[rows_, cols].astype(F32)
                gp = v.astype(BF)
                t.GD[rows_, cols] = gp
                add_small(l, 28 + n, jnp.sum(gp.astype(F32), axis=0, keepdims=True))

            for n in range(4):
                step(n)

        def weight_grad(buf, a, b):
            for r in range(4):
                cols = blk(r, TILE)
                buf[cols, :] = mm(a[:, cols], b[...], TN).astype(BF)

        def weight_grad_attn(l, buf):
            for r in range(4):
                cols = blk(r, TILE)
                v = mm(t.NF[:, cols], t.H[...], TN).astype(BF)
                o = mm(t.MX[:, cols], t.MXC[l], TN).astype(BF)
                for zz in range(4):
                    lo = zz * TILE
                    buf[cols, lo : lo + TILE] = jnp.concatenate(
                        [v[:, lo : lo + 3 * HD], o[:, zz * HD : (zz + 1) * HD]], axis=1
                    )

        def mixed_grad(l, g):
            t.GMC[half(g), :] = mm(t.MX[half(g), :], t.WO[l], NN).astype(BF)

        def attend_back(l, g):
            def step(i, _):
                im = 2 * g + i
                ri = blk(im, RP)
                for zz in range(4):
                    cols = blk(zz, TILE)
                    b = t.PR[ri, cols]
                    q, k, v = b[:, 0:HD], b[:, HD : 2 * HD], b[:, 2 * HD : 3 * HD]
                    gm = t.GMC[ri, zz * HD : (zz + 1) * HD]
                    pb = t.PB[4 * im + zz]
                    pf = pb.astype(F32)
                    gp = mm(gm, v, NT)
                    cen = jnp.sum(pf * gp, axis=-1, keepdims=True)
                    gsc = (pf * (gp - cen)).astype(BF)
                    gq = mm(gsc, k, NN) * SCALE
                    gk = mm(gsc, q, TN) * SCALE
                    gv = mm(pb, gm, TN)
                    out = jnp.concatenate([gq, gk, gv, jnp.zeros((RP, HD), F32)], axis=1).astype(BF)
                    t.H[ri, cols] = out
                    add_small(l, 24 + zz, jnp.sum(out.astype(F32), axis=0, keepdims=True))
                return 0

            lax.fori_loop(0, 2, step, 0)

        def swap(buf, got, i):
            return rcopy(buf.at[1 - x], got, t.lo_s.at[i], t.lo_r.at[i], p.dev(x=1 - x))

        def rows_loop(step, init=0, h=None):
            lo, hi = (0, RP // RC) if h is None else PARTS[h]
            return lax.fori_loop(lo, hi, step, init)

        firsts = [
            pltpu.make_async_copy(t.wq, t.WQ, t.io.at[6]),
            pltpu.make_async_copy(t.wo, t.WOS, t.io.at[7]),
            pltpu.make_async_copy(t.imgs.at[0:2], t.XO, t.io.at[0]),
            pltpu.make_async_copy(t.imgs.at[2], t.GT.at[row(c, 0)], t.io.at[1]),
            pltpu.make_async_copy(t.imgs.at[3], t.GT.at[row(c, 1)], t.io.at[8]),
        ]
        for cp in firsts:
            cp.start()
        for cp in firsts[:2]:
            cp.wait()
        for jp in range(4):
            parts = [t.WQ[:, k * TILE + jp * HD : k * TILE + (jp + 1) * HD] for k in range(3)]
            t.WA[jp] = jnp.concatenate(parts + [t.WOS[:, jp * HD : (jp + 1) * HD]], axis=1)
        t.SG[...] = jnp.zeros((2, 32, TILE), F32)
        t.MXC[...] = jnp.zeros((2, 4 * RP, TILE), BF)
        p.barrier()
        for k in range(4):
            small_red(k).start()
        for m in range(3):
            for k in (1, 2, 3, 0):
                red(m, k).start()
        for l in range(2):
            for cs in range(2):
                b = t.SPB.at[l, y, z, cs]
                pltpu.make_async_copy(b, b, t.pr.at[l, cs]).wait()
            for k in range(1, nz):
                small_z(l, k).start()
        for cp in firsts[2:]:
            cp.wait()
        tops = ag_local(t.GT, 4)
        for cp in tops:
            cp.start()
        release(0)
        for l in range(2):
            for k in range(1, nz):
                small_z(l, k).wait_recv()
            for k in range(1, Y):
                small_y(l, k).start()
        for l in range(2):
            for k in range(1, Y):
                small_y(l, k).wait_recv()
            t.SPS[l] = jnp.sum(t.SPB[l].astype(F32).reshape(Y * nz * 2, 32, TILE), axis=0)
            for r in range(6):
                for q in range(4):
                    t.G[l, r : r + 1, q * TILE : (q + 1) * TILE] = t.SPS[l, 4 * r + q : 4 * r + q + 1, :]

        def ln(l, g, b, load, buf, at):
            gain, shift = t.G[l, g : g + 1, :], t.G[l, b : b + 1, :]

            def step(r, _):
                buf[at(r), :] = norm_row(load(r), gain, shift).astype(BF)
                return 0

            rows_loop(step)

        for m in range(2):
            ln(
                0, 0, 2, lambda r, m=m: t.XO[m, blk(r, RC), :].astype(F32), t.NF,
                lambda r, m=m: pl.ds(pl.multiple_of((2 * c + m) * RP + r * RC, RC), RC),
            )
        first = ag_local(t.NF, 0)
        for cp in first:
            cp.start()
        release(1)
        pump(1)
        for cp in first:
            cp.wait_recv()

        for l in range(2):
            A, U, DN = 3 * l, 3 * l + 1, 3 * l + 2
            s = 2 * l
            if l:
                ag_in(t.NF, 0, 2)
            for k in range(4):
                ready(A, k)
                attend(l, 0, holds[k])
                if l == 0 or k < 2:
                    pump()
            if l:
                rs_done(0, 1)
                rs_done(1, 1)
            out_weights(l)
            out_project(l, 0)
            rs_out(0, s)
            if l:
                ag_mid(t.NF, 1, 2)
                ag_in(t.NF, 1, 2)
            for k in range(4):
                attend(l, 1, holds[k])
                if k % 2:
                    pump()
            out_project(l, 1)
            rs_out(1, s)
            if l == 0:
                for cp in first:
                    cp.wait_send()
                for name in ("NF", "PR", "PB"):
                    save(name).start()
            else:
                ag_done(t.NF, 2)

            def second(g, h):
                gain, shift, bias = t.G[l, 1:2, :], t.G[l, 4:5, :], t.G[l, 3:4, :]

                def step(r, _):
                    rs = blk(r, RC)
                    v = t.XO[x, rs, :] if l == 0 else t.OUT[0, rs, :]
                    mid = v.astype(F32) + sums(g, r) + bias
                    t.MID[l, rs, :] = mid
                    t.N2[own_rows(g, r), :] = norm_row(mid, gain, shift).astype(BF)
                    return 0

                rows_loop(step, 0, h)
                ag_send(t.N2, g, 1 + 2 * l, h)
                return 0

            pump()
            for g in range(2):
                rs_in(g, s, lambda h, _, g=g: second(g, h))
            pump()
            ag_mid(t.N2, 0, 1 + 2 * l)
            ag_in(t.N2, 0, 1 + 2 * l)
            if l:
                save("H").wait()
                save("GD").wait()
            for k in range(4):
                ready(U, k)
                up(l, 0, holds[k])
            ag_mid(t.N2, 1, 1 + 2 * l)
            pump()
            ag_in(t.N2, 1, 1 + 2 * l)
            for k in range(4):
                up(l, 1, holds[k])
            pump()
            ag_done(t.N2, 1 + 2 * l)
            rs_done(0, s)
            rs_done(1, s)
            if l == 0:
                for name in ("N2", "H", "GD"):
                    save(name).start()
                for name in ("NF", "PR", "PB"):
                    save(name).wait()
            else:
                for cp in tops:
                    cp.wait_recv()
                weight_grad(t.DX, t.GT, t.H)
                y_start(1, 2)
            for k in range(4):
                ready(DN, k)
            s = 2 * l + 1
            project(t.H, DN, 0)
            rs_out(0, s)
            pump()
            project(t.H, DN, 1)
            rs_out(1, s)
            pump()
            if l == 0:
                save("N2").wait()

                def last(g, h):
                    gain, shift, bias = t.G[1, 0:1, :], t.G[1, 2:3, :], t.G[0, 5:6, :]

                    def step(r, _):
                        rs = blk(r, RC)
                        o = (t.MID[0, rs, :] + sums(g, r) + bias).astype(BF)
                        t.OUT[0, rs, :] = o
                        t.NF[own_rows(g, r), :] = norm_row(o.astype(F32), gain, shift).astype(BF)
                        return 0

                    rows_loop(step, 0, h)
                    ag_send(t.NF, g, 2, h)
                    return 0

                for g in range(2):
                    rs_in(g, s, lambda h, _, g=g: last(g, h))
                pump()
                ag_mid(t.NF, 0, 2)

            else:
                for g in range(2):

                    @pl.when(c == g)
                    def _():
                        def step(r, _):
                            rs = blk(r, RC)
                            t.FIN[rs, :] = t.MID[1, rs, :] + OP[own_rows(g, r), :].astype(F32) + t.G[1, 5:6, :]
                            return 0

                        rows_loop(step)

        for k in range(1, 4):
            small_red(k).wait_send()
        for l in range(2):
            for k in range(1, nz):
                small_z(l, k).wait_send()
            for k in range(1, Y):
                small_y(l, k).wait_send()
        for m in range(3):
            for k in range(1, 4):
                red(m, k).wait_send()
        for lm in range(6):
            wz(lm, 1).wait_send()
            wz(lm, 2).wait_send()
            for k in (1, 2):

                @pl.when(inner == 1)
                def _():
                    wrelay(lm, k).wait_send()

            for k in range(4):
                for ky in range(1, Y):
                    wy(lm, k, ky).wait_send()

        def final_out(h):
            def step(r, _):
                rs = blk(r, RC)
                v = t.FIN[rs, :] + RB[1, x, rs, :].astype(F32) + XR[1, rs, :].astype(F32)
                t.OUT[1, rs, :] = v.astype(BF)
                return 0

            return rows_loop(step, 0, h)

        zero8 = jnp.zeros((8, D), F32)
        for l in (1, 0):
            A, U, DN = 3 * l, 3 * l + 1, 3 * l + 2
            s = 4 + 2 * (1 - l)
            if l == 0:
                ag_in(t.GT, 0, 6)
                fetch("GD").wait()
            rs_done(0, s - 1)
            rs_done(1, s - 1)
            pre(l, 0)
            project(t.GD, U, 0)
            rs_out(0, s)
            push()
            if l == 0:
                ag_mid(t.GT, 1, 6)
                ag_in(t.GT, 1, 6)
                fetch("H").wait()
                push_through(z_sum, 1, 2)
                for kz in range(nz):
                    for k in range(1, Y):
                        y_part(1, 2, k, kz).wait_send()
                z_sent(1, 2)
                weight_grad(t.DX, t.GT, t.H)
                push_through(y_sum, 1, 0)
                y_start(0, 2)
                zf_start()
            pre(l, 1)
            project(t.GD, U, 1)
            rs_out(1, s)
            push()
            if l == 1:
                for cp in tops:
                    cp.wait_send()
            else:
                ag_done(t.GT, 6)

            def fill_up():
                if l == 0:
                    fetch("N2").wait()
                weight_grad(W.at[U], t.N2, t.GD)
                y_start(l, 1)
                if l == 1:
                    fetch("N2").start()
                    fetch("GD").start()

            def mid_back(g, h, init):
                def step(r, acc):
                    rs = blk(r, RC)
                    dy = sums(g, r)
                    top = t.GT[own_rows(g, r), :].astype(F32)
                    dx, dg = norm_back(t.MID[l, rs, :], t.G[l, 1:2, :], dy)
                    gmid = top + dx
                    t.GMID[rs, :] = gmid
                    t.MX[own_rows(g, r), :] = gmid.astype(BF)
                    return acc[0] + fold(dg), acc[1] + fold(dy), acc[2] + fold(gmid), acc[3] + fold(top)

                acc = rows_loop(step, init, h)
                ag_send(t.MX, g, s + 1, h)
                return acc

            def mid_end(acc):
                for i, r in enumerate((1, 4, 3, 5)):
                    put_small(l, r, acc[i])

            rs_in(0, s, lambda h, acc: mid_back(0, h, acc), (zero8,) * 4, mid_end)
            fill_up()
            rs_in(1, s, lambda h, acc: mid_back(1, h, acc), (zero8,) * 4, mid_end)
            push()
            if l == 0:
                s_mid(1)
                for name in ("PR", "PB"):
                    fetch(name).wait()
            ag_mid(t.MX, 0, s + 1)
            ag_in(t.MX, 0, s + 1)
            push()
            mixed_grad(l, 0)
            attend_back(l, 0)
            push()
            rs_done(0, s)
            rs_done(1, s)
            project(t.H, A, 0)
            rs_out(0, s + 1)
            push()
            ag_mid(t.MX, 1, s + 1)
            ag_in(t.MX, 1, s + 1)
            mixed_grad(l, 1)
            attend_back(l, 1)
            push()
            project(t.H, A, 1)
            rs_out(1, s + 1)
            ag_done(t.MX, s + 1)
            if l == 1:
                push_through(y_sum, 1, 1)
            else:
                fetch("NF").wait()
                push_through(y_sum, 0, 2)
            def first_back(g, h, init):
                def step(r, acc):
                    rs = blk(r, RC)
                    dy = sums(g, r)
                    v = (t.XO[x, rs, :] if l == 0 else t.OUT[0, rs, :]).astype(F32)
                    dx, dg = norm_back(v, t.G[l, 0:1, :], dy)
                    gx = (t.GMID[rs, :] + dx).astype(BF)
                    t.IGB[l, rs, :] = gx
                    if l == 1:
                        t.GT[own_rows(g, r), :] = gx
                    return acc[0] + fold(dg), acc[1] + fold(dy)

                acc = rows_loop(step, init, h)
                if l == 1:
                    ag_send(t.GT, g, 6, h)
                return acc

            def first_end(acc):
                put_small(l, 0, acc[0])
                put_small(l, 2, acc[1])

            if l == 0:
                swap(t.OUT, t.LOB, 0).start()

            def fill_attn():
                weight_grad_attn(l, W.at[A])
                y_start(l, 0)
                if l == 1:
                    for name in ("H", "PR", "PB", "NF"):
                        fetch(name).start()

            if l == 0:
                fill_attn()
            rs_in(0, s + 1, lambda h, acc: first_back(0, h, acc), (zero8,) * 2, first_end)
            if l == 1:
                fill_attn()
            rs_in(1, s + 1, lambda h, acc: first_back(1, h, acc), (zero8,) * 2, first_end)
            if l == 1:
                for g in range(2):
                    rs_in(g, 3, lambda h, _: final_out(h))
            s_start(l)

            if l == 1:
                ag_mid(t.GT, 0, 6)

        swap(t.IGB, t.LGB, 1).start()
        push(100)
        s_end(1)
        give = []
        for i, (buf, got, out) in enumerate(((t.OUT, t.LOB, t.lo), (t.IGB, t.LGB, t.ig))):
            cp = swap(buf, got, i)
            cp.wait_recv()
            cp.wait_send()
            give.append(pltpu.make_async_copy(buf.at[x], out.at[x], t.io.at[2 + 2 * i]))
            give.append(pltpu.make_async_copy(got, out.at[1 - x], t.io.at[3 + 2 * i]))
            for cp in give[-2:]:
                cp.start()
        for m in (2, 1, 0):
            for jj in range(4):
                b = t.CR.at[m, jj]
                pltpu.make_async_copy(b, b, t.c_r.at[m, jj]).wait()
                give.append(pltpu.make_async_copy(b, t.cr.at[m, :, blk(jj, TILE)], t.cr_s.at[m, jj]))
                give[-1].start()
        for jj in range(4):
            b = t.SCR.at[jj]
            pltpu.make_async_copy(b, b, t.sc_r.at[jj]).wait()
            t.gs_out[jj] = t.SCR[jj]
        for cp in give:
            cp.wait()
        for g in range(2):
            rs_done(g, 7)
        for h in range(2):
            chip_part(3, h).wait_send()
        for k in (1, 2, 3):
            zf_part(k).wait_send()
        for k in range(1, Y):
            zf_y(k).wait_send()
        for l in range(2):
            for m in range(3 if l == 0 else 2):
                for kz in range(nz):
                    for k in range(1, Y):
                        y_part(l, m, k, kz).wait_send()
                z_sent(l, m)
            for k in range(1, Y):
                s_y(l, k).wait_send()
            for k in range(1, nz):
                s_z(l, k).wait_send()
            for cp in range(2):

                @pl.when(jnp.logical_not(jnp.logical_and(x == l, c == cp)))
                def _():
                    s_c(l, cp).wait_send()
                    for m in range(3):
                        c_part(l, m, cp).wait_send()

    vm = pl.BlockSpec(memory_space=pltpu.VMEM)
    hbm = pl.BlockSpec(memory_space=pl.ANY)
    return pl.pallas_call(
        body,
        out_shape=[jax.ShapeDtypeStruct(*a) for a in outputs.values()]
        + [jax.ShapeDtypeStruct(a, BF) for a in spilled.values()],
        in_specs=[hbm] * 6,
        out_specs=[hbm] * (len(outputs) - 1) + [vm] + [hbm] * len(spilled),
        scratch_shapes=[pltpu.VMEM(*a) for a in vmem.values()] + [dma(a) for a in sems.values()],
        compiler_params=pltpu.CompilerParams(
            collective_id=0, has_side_effects=True, vmem_limit_bytes=VMEM_LIMIT
        ),
    )


def small_pack(norm_gains, row_shifts, head_bias, unit_bias, dpn, nz):
    dp, z = lax.axis_index("dp"), lax.axis_index("tensor")
    rows = jnp.concatenate([norm_gains[0], row_shifts[0]], axis=0)
    w = rows.shape[1]
    rows = lax.dynamic_update_slice(jnp.zeros((6, D), BF), rows, (0, (dp * nz + z) * w)).reshape(1, 24, TILE)
    hw, uw = head_bias.shape[3], unit_bias.shape[2]
    head = jnp.zeros((4, 4, TILE), BF)
    head = lax.dynamic_update_slice(head, head_bias[0, 0][:, None], (0, z, dp * hw))
    head = lax.dynamic_update_slice(head, head_bias[0, 1][:, None], (0, z, 2 * HD + dp * hw))
    unit = lax.dynamic_update_slice(jnp.zeros((4, 4, TILE), BF), unit_bias[0][:, None], (0, z, dp * uw))
    return jnp.concatenate([jnp.broadcast_to(rows, (4, 24, TILE)), head, unit], axis=1)


def solution(mesh):
    dpn, nz = mesh.shape["dp"], mesh.shape["tensor"]

    def on_device(
        images_in, cotangent, w_qkv, w_out, w_up, w_down, norm_gains, row_shifts, head_bias, unit_bias
    ):
        R = w_up.shape[1]
        sp = small_pack(norm_gains, row_shifts, head_bias, unit_bias, dpn, nz)
        imgs = jnp.pad(jnp.concatenate([images_in, cotangent]), ((0, 0), (0, RP - SEQ), (0, 0)))
        lo, ig, cr, gs = both_layers(dpn, nz, R)(
            imgs, w_qkv[0].reshape(R, 3 * TILE), w_out[0], w_up[0], w_down[0], sp
        )[:4]
        lo, ig = lo[:, :SEQ], ig[:, :SEQ]
        gu, gd = cr[1].astype(F32), cr[2].astype(F32)
        dp, z = lax.axis_index("dp"), lax.axis_index("tensor")
        ga = cr[0].astype(F32).reshape(R, 4, TILE)
        g_qkv = ga[:, :, : 3 * HD].reshape(R, 4, 3, HD).transpose(0, 2, 1, 3).reshape(w_qkv.shape)
        g_out = ga[:, :, 3 * HD :].reshape(w_out.shape)
        w, hw, uw = norm_gains.shape[2], head_bias.shape[3], unit_bias.shape[2]
        rows = lax.dynamic_slice(jnp.sum(gs[:, :24], axis=0).reshape(6, D), (0, (dp * nz + z) * w), (6, w))
        head = lax.dynamic_slice(gs, (0, 24 + z, 0), (4, 1, TILE))[:, 0]
        unit = lax.dynamic_slice(gs, (0, 28 + z, dp * uw), (4, 1, uw))[:, 0]
        g_head = jnp.stack([lax.dynamic_slice(head, (0, o + dp * hw), (4, hw)) for o in (0, 2 * HD)])
        return (
            lo[None], ig[None], g_qkv, g_out, gu[None], gd[None],
            rows[None, :2], rows[None, 2:], g_head[None], unit[None],
        )

    in_specs = (
        P(None, ("dp", "tensor"), None),
        P(None, ("dp", "tensor"), None),
        P("section", "dp", None, "tensor"),
        P("section", "dp", "tensor"),
        P("section", "dp", "tensor"),
        P("section", "dp", "tensor"),
        P("section", None, ("dp", "tensor")),
        P("section", None, ("dp", "tensor")),
        P("section", None, "tensor", "dp"),
        P("section", "tensor", "dp"),
    )
    out_specs = (
        P("section", None, ("dp", "tensor"), None),
        P("section", None, ("dp", "tensor"), None),
        P("section", "dp", None, "tensor"),
        P("section", "dp", "tensor"),
        P("section", "dp", "tensor"),
        P("section", "dp", "tensor"),
        P("section", None, ("dp", "tensor")),
        P("section", None, ("dp", "tensor")),
        P("section", None, "tensor", "dp"),
        P("section", "tensor", "dp"),
    )
    return jax.shard_map(
        on_device, mesh=mesh, in_specs=in_specs, out_specs=out_specs, check_vma=False
    )
```

```python
import math
import types

import jax
import jax.numpy as jnp
from jax import lax
from jax.experimental import pallas as pl
from jax.experimental.pallas import tpu as pltpu
from jax.sharding import PartitionSpec as P

D = 1024
HD = 64
SEQ = 197
RP = 208
RC = 16
PARTS = ((0, 7), (7, 13))
TILE = 256
SCALE = 0.125
EPS = 1e-06
MESH = pl.DeviceIdType.MESH
BF = jnp.bfloat16
F32 = jnp.float32
NN = (((1,), (0,)), ((), ()))
NT = (((1,), (1,)), ((), ()))
TN = (((0,), (0,)), ((), ()))
VMEM_LIMIT = 62 * 2**20


def mm(a, b, dims):
    return lax.dot_general(a, b, dims, preferred_element_type=F32)


def blk(i, size):
    if isinstance(i, int):
        return pl.ds(i * size, size)
    return pl.ds(pl.multiple_of(i * size, size), size)


class Place:
    def __init__(self, dpn, nz):
        self.Y, self.nz = dpn // 2, nz
        self.x = lax.axis_index("section")
        dp = lax.axis_index("dp")
        self.z = lax.axis_index("tensor")
        self.y, self.c = dp // 2, lax.rem(dp, 2)
        self.j = 2 * self.x + self.c

    def dev(self, x=None, y=None, c=None, z=None):
        x = self.x if x is None else x
        y = self.y if y is None else y
        c = self.c if c is None else c
        z = self.z if z is None else z
        return (x, 2 * y + c, z)

    def cell(self, k):
        jp = lax.rem(self.j + k, 4)
        return jp, jp // 2, lax.rem(jp, 2)

    def yk(self, k):
        return lax.rem(self.y + k, self.Y)

    def zk(self, k):
        return lax.rem(self.z + k, self.nz)

    def barrier(self):
        bar = pltpu.get_barrier_semaphore()
        n = 0
        for k in range(1, 4):
            _, xp, cp = self.cell(k)
            pl.semaphore_signal(bar, inc=1, device_id=self.dev(x=xp, c=cp), device_id_type=MESH)
            n += 1
        for k in range(1, self.nz):
            pl.semaphore_signal(bar, inc=1, device_id=self.dev(z=self.zk(k)), device_id_type=MESH)
            n += 1
        for k in range(1, self.Y):
            pl.semaphore_signal(bar, inc=1, device_id=self.dev(y=self.yk(k)), device_id_type=MESH)
            n += 1
        pl.semaphore_wait(bar, n)


def rcopy(src, dst, ss, rs, dev):
    return pltpu.make_async_remote_copy(
        src_ref=src, dst_ref=dst, send_sem=ss, recv_sem=rs, device_id=dev, device_id_type=MESH
    )


def norm_row(v, g, b):
    cen = v - jnp.sum(v, axis=-1, keepdims=True) * (1.0 / D)
    var = jnp.sum(cen * cen, axis=-1, keepdims=True) * (1.0 / D)
    return cen * lax.rsqrt(var + EPS) * g + b


def norm_back(v, g, dy):
    cen = v - jnp.sum(v, axis=-1, keepdims=True) * (1.0 / D)
    rstd = lax.rsqrt(jnp.sum(cen * cen, axis=-1, keepdims=True) * (1.0 / D) + EPS)
    hat = cen * rstd
    dh = dy * g
    a = jnp.sum(dh, axis=-1, keepdims=True) * (1.0 / D)
    b = jnp.sum(dh * hat, axis=-1, keepdims=True) * (1.0 / D)
    return rstd * (dh - a - hat * b), dy * hat


def fold(v):
    return v[0:8] + v[8:16]


def half(g):
    return blk(g, 2 * RP)


def row(g, m):
    return blk(2 * g + m, RP)


def both_layers(dpn, nz, rows):
    Y, R = dpn // 2, rows
    R2 = 2 * R
    full = (4 * RP, D)
    dma = pltpu.SemaphoreType.DMA
    inputs = ["imgs", "wq", "wo", "wu", "wd", "sp"]
    outputs = {
        "lo": ((2, RP, D), BF), "ig": ((2, RP, D), BF), "cr": ((3, R, D), BF), "gs_out": ((4, 32, TILE), F32),
    }
    spilled = {"NF": full, "PR": full, "N2": full, "H": full, "GD": full, "PB": (16, RP, RP)}
    vmem = {
        "W": ((6, D, D), BF), "DX": ((D, D), BF), "WQ": ((R, 3 * TILE), BF), "WOS": ((R, TILE), BF), "WA": ((4, R, TILE), BF), "SPB": ((2, Y, nz, 2, 32, TILE), BF), "SPS": ((2, 32, TILE), F32),
        "G": ((2, 8, D), F32), "NF": (full, BF), "PR": (full, BF), "N2": (full, BF), "H": (full, BF), "GD": (full, BF),
        "PB": ((16, RP, RP), BF), "MX": (full, BF), "MXC": ((2, 4 * RP, TILE), BF), "GMC": ((4 * RP, TILE), BF), "WO": ((2, D, TILE), BF), "GT": (full, BF), "OP": (full, BF), "RB": ((2, 2, RP, D), BF),
        "CS": ((2, RP, D), BF), "XR": ((2, RP, D), BF), "XO": ((2, RP, D), BF), "MID": ((2, RP, D), F32),
        "OUT": ((2, RP, D), BF), "LOB": ((RP, D), BF), "GMID": ((RP, D), F32), "FIN": ((RP, D), F32), "IGB": ((2, RP, D), BF),
        "LGB": ((RP, D), BF), "YR": ((3, Y - 1, R2, D), BF), "ZR": ((6, 2, R2, TILE), BF), "ZC": ((6, 2, R2, TILE), BF), "ZF": ((2, D, TILE // 2), BF), "ZFC": ((2, D, TILE // 2), BF),
        "RD": ((6, 2, R, TILE), BF), "CR": ((3, 4, R, TILE), BF), "SG": ((2, 32, TILE), F32),
        "SYR": ((2, Y - 1, 32, TILE), F32), "SZR": ((2, nz - 1, 32, TILE), F32), "SRD": ((4, 32, TILE), F32),
        "SCR": ((4, 32, TILE), F32),
    }
    sems = {
        "red_s": (3, 4), "red_r": (6, 2), "fz_s": (6, 4), "fz_r": (6, 4), "fy_s": (6, 4, Y), "fy_r": (6, 4, Y),
        "ps": (4 + 2 * nz + 2 * Y,), "pr": (6, max(nz, Y, 2)), "gs": (8, 6), "gr": (8, 6), "ss": (8, 4), "sr": (8, 4),
        "lo_s": (2,), "lo_r": (2,), "io": (9,), "cr_s": (3, 4), "keep": (2, 6), "y_s": (6, Y, nz), "y_r": (6, Y, nz), "z_s": (6, 4), "z_r": (6, 4), "zf_s": (4,), "zf_r": (4,), "zy_s": (Y,), "zy_r": (Y,),
        "c_s": (6, 2), "c_r": (3, 4), "sy_s": (2, Y), "sy_r": (2, Y), "sz_s": (2, nz), "sz_r": (2, nz), "sc_s": (2, 2),
        "sc_r": (4,),
    }
    names = inputs + list(outputs) + ["o_" + n for n in spilled] + list(vmem) + list(sems)

    def body(*refs):
        t = types.SimpleNamespace(**dict(zip(names, refs)))
        p = Place(dpn, nz)
        x, y, c, z, j = p.x, p.y, p.c, p.z, p.j
        near, far = x, 1 - x
        W, OP, RB, CS, XR = t.W, t.OP, t.RB, t.CS, t.XR

        def core_part(g, m, s):
            return rcopy(OP.at[row(g, m)], RB.at[int(s == 3), m], t.ss.at[s, m], t.sr.at[s, m], p.dev(c=1 - c))

        def chip_part(s, h):
            k, rs = int(s == 3), pl.ds(PARTS[h][0] * RC, (PARTS[h][1] - PARTS[h][0]) * RC)
            return rcopy(CS.at[k, rs], XR.at[k, rs], t.ss.at[s, 2 + h], t.sr.at[s, 2 + h], p.dev(x=1 - x))

        def rs_help(g, s):
            @pl.when(c != g)
            def _():
                core_part(g, far, s).start()
                core_part(g, near, s).start()

        def rs_own(g, s):
            @pl.when(c == g)
            def _():
                core_part(g, far, s).wait_recv()
                k = int(s == 3)
                for h, (lo, hi) in enumerate(PARTS):
                    rs = pl.ds(lo * RC, (hi - lo) * RC)
                    src_rows = pl.ds(pl.multiple_of((2 * g + far) * RP + lo * RC, RC), (hi - lo) * RC)
                    CS[k, rs, :] = (OP[src_rows, :].astype(F32) + RB[k, far, rs, :].astype(F32)).astype(BF)
                    chip_part(s, h).start()

        def rs_out(g, s):
            rs_help(g, s)
            rs_own(g, s)

        def rs_in(g, s, fn, init=0, end=None):
            @pl.when(c == g)
            def _():
                core_part(g, near, s).wait_recv()
                acc = init
                for h in range(2):
                    chip_part(s, h).wait_recv()
                    acc = fn(h, acc)
                if end is not None:
                    end(acc)

        def rs_done(g, s):
            @pl.when(c != g)
            def _():
                for m in range(2):
                    core_part(g, m, s).wait_send()

            if s != 3:

                @pl.when(c == g)
                def _():
                    for h in range(2):
                        chip_part(s, h).wait_send()

        def sums(g, r):
            rs = blk(r, RC)
            own = OP[pl.ds(pl.multiple_of((2 * g + x) * RP + r * RC, RC), RC), :].astype(F32)
            return own + RB[0, x, rs, :].astype(F32) + XR[0, rs, :].astype(F32)

        def ag_part(buf, g, s, k, h):
            lo, hi = PARTS[h]
            m = far if k == 2 else near
            b = buf.at[pl.ds(pl.multiple_of((2 * g + m) * RP + lo * RC, RC), (hi - lo) * RC)]
            i = 2 * k + h
            return rcopy(b, b, t.gs.at[s, i], t.gr.at[s, i], p.dev(x=1 - x) if k == 1 else p.dev(c=1 - c))

        def ag_send(buf, g, s, h):
            ag_part(buf, g, s, 1, h).start()
            ag_part(buf, g, s, 0, h).start()

        def ag_mid(buf, g, s):
            @pl.when(c == g)
            def _():
                for h in range(2):
                    ag_part(buf, g, s, 1, h).wait_recv()
                    ag_part(buf, g, s, 2, h).start()

        def ag_in(buf, g, s):
            @pl.when(c != g)
            def _():
                for h in range(2):
                    ag_part(buf, g, s, 0, h).wait_recv()
                    ag_part(buf, g, s, 2, h).wait_recv()

        def ag_done(buf, s):
            for g in range(2):

                @pl.when(c == g)
                def _():
                    for h in range(2):
                        for k in range(3):
                            ag_part(buf, g, s, k, h).wait_send()

        def ag_local(buf, s):
            return [
                rcopy(buf.at[row(c, m)], buf.at[row(c, m)], t.gs.at[s, m], t.gr.at[s, m], p.dev(c=1 - c))
                for m in range(2)
            ]

        def small_red(k):
            jp, xp, cp = p.cell(k)
            dst = t.SPB.at[x, y, z, c]
            if k == 0:
                return pltpu.make_async_copy(t.sp.at[jp], dst, t.pr.at[x, c])
            return rcopy(t.sp.at[jp], dst, t.ps.at[k], t.pr.at[x, c], p.dev(x=xp, c=cp))

        def small_z(l, k):
            b = t.SPB.at[l, y, z]
            return rcopy(b, b, t.ps.at[4 + l * nz + k], t.pr.at[2 + l, k], p.dev(z=p.zk(k)))

        def small_y(l, k):
            b = t.SPB.at[l, y]
            return rcopy(b, b, t.ps.at[4 + 2 * nz + l * Y + k], t.pr.at[4 + l, k], p.dev(y=p.yk(k)))

        src = (t.WA, t.wu, t.wd)
        inner = lax.rem((z + 1) // 2, 2)
        mate = z + 1 - 2 * lax.rem(z, 2)
        cross = 2 - z // 2
        other = 3 - 3 * (z // 2)
        sides = (z, mate, cross, other)
        holds = (z, mate + inner * (cross - mate), cross + inner * (other - cross), other + inner * (mate - other))

        def red(m, k):
            jp, xp, cp = p.cell(k)
            b = src[m].at[jp] if m == 0 else src[m].at[:, blk(jp, TILE)]
            dst = W.at[x * 3 + m, blk(2 * y + c, R), blk(z, TILE)]
            if k == 0:
                return pltpu.make_async_copy(b, dst, t.red_r.at[x * 3 + m, c])
            return rcopy(b, dst, t.red_s.at[m, k], t.red_r.at[x * 3 + m, c], p.dev(x=xp, c=cp))

        def chunk(lm, k):
            return W.at[lm, blk(y, R2), blk(holds[k], TILE)]

        def wz(lm, k):
            b = chunk(lm, 0)
            if k == 1:
                return rcopy(b, b, t.fz_s.at[lm, 0], t.fz_r.at[lm, 3 - 2 * inner], p.dev(z=mate))
            return rcopy(b, b, t.fz_s.at[lm, 1], t.fz_r.at[lm, 2 - inner], p.dev(z=cross))

        def wrelay(lm, k):
            b = chunk(lm, k)
            return rcopy(b, b, t.fz_s.at[lm, k + 1], t.fz_r.at[lm, k + 1], p.dev(z=mate))

        def wy(lm, k, ky):
            b = chunk(lm, k)
            return rcopy(b, b, t.fy_s.at[lm, k, ky], t.fy_r.at[lm, k, ky], p.dev(y=p.yk(ky)))

        def release(lm):
            for cs in range(2):
                b = W.at[lm, blk(2 * y + cs, R), blk(z, TILE)]
                pltpu.make_async_copy(b, b, t.red_r.at[lm, cs]).wait()
            wz(lm, 2).start()
            wz(lm, 1).start()
            for ky in range(1, Y):
                wy(lm, 0, ky).start()

        def hand_on(lm, k):
            pltpu.make_async_copy(chunk(lm, k), chunk(lm, k), t.fz_r.at[lm, k]).wait()
            if k < 3:

                @pl.when(inner == 1)
                def _():
                    wrelay(lm, k).start()

            for ky in range(1, Y):
                wy(lm, k, ky).start()
            if k == 3 and lm + 2 < 6:
                release(lm + 2)

        queue = [(lm, k) for lm in range(6) for k in (1, 2, 3)]
        handed = []

        def pump(n=1):
            for _ in range(n):
                if queue:
                    lm, k = queue.pop(0)
                    hand_on(lm, k)
                    handed.append((lm, k))

        def ready(lm, k):
            while k and (lm, k) not in handed:
                pump()
            for ky in range(1, Y):
                wy(lm, k, ky).wait_recv()

        def where(l, m):
            return t.DX if m == 2 else W.at[3 * l + m]

        def usual(l, m, zz):
            if (l, m) == (0, 2):
                return pl.ds(pl.multiple_of(zz * TILE + TILE // 2, TILE // 2), TILE // 2)
            return blk(zz, TILE)

        def take(l, m):
            return slice(0, TILE // 2) if (l, m) == (0, 2) else slice(0, TILE)

        def y_part(l, m, k, kz):
            cols = usual(l, m, sides[kz])
            return rcopy(
                where(l, m).at[blk(p.yk(k), R2), cols], t.YR.at[m, k - 1, :, cols],
                t.y_s.at[3 * l + m, k, kz], t.y_r.at[3 * l + m, k, kz], p.dev(y=p.yk(k)),
            )

        def z_part(l, m, k):
            n = 3 * l + m
            b = where(l, m).at[blk(y, R2), usual(l, m, sides[k])]
            if k == 1:
                return rcopy(b, t.ZR.at[n, 0, :, take(l, m)], t.z_s.at[n, 1], t.z_r.at[n, 0], p.dev(z=mate))
            return rcopy(b, t.ZC.at[n, k - 2, :, take(l, m)], t.z_s.at[n, k], t.z_r.at[n, k], p.dev(z=mate))

        def z_over(l, m, k):
            n = 3 * l + m
            b = where(l, m).at[blk(y, R2), usual(l, m, sides[k])]
            return rcopy(b, t.ZR.at[n, 1, :, take(l, m)], t.z_s.at[n, k], t.z_r.at[n, 1], p.dev(z=sides[k]))

        order = (3, 2, 1, 0)

        def y_start(l, m):
            begun.add((l, m))
            for kz in order:
                for k in range(1, Y):
                    y_part(l, m, k, kz).start()

        begun = set()

        def y_sum(l, m, kz):
            cols = usual(l, m, sides[kz])
            buf = where(l, m)
            for k in range(1, Y):
                y_part(l, m, k, kz).wait_recv()
            v = buf[blk(y, R2), cols].astype(F32)
            for k in range(1, Y):
                v = v + t.YR[m, k - 1, :, cols].astype(F32)
            buf[blk(y, R2), cols] = v.astype(BF)
            if kz == 1:
                z_part(l, m, 1).start()
            elif kz:

                @pl.when(inner == 0)
                def _():
                    z_part(l, m, kz).start()

        def z_mid(l, m, k):
            @pl.when(inner == 1)
            def _():
                z_part(l, m, k).wait_recv()
                buf, cols = where(l, m), usual(l, m, sides[k])
                v = buf[blk(y, R2), cols].astype(F32) + t.ZC[3 * l + m, k - 2, :, take(l, m)].astype(F32)
                buf[blk(y, R2), cols] = v.astype(BF)
                z_over(l, m, k).start()

        def z_sent(l, m):
            for k in (1, 2, 3):
                z_part(l, m, k).wait_send()

        def zf_cols(zz):
            return pl.ds(pl.multiple_of(zz * TILE, TILE), TILE // 2)

        def zf_part(k):
            b = t.DX.at[:, zf_cols(sides[k])]
            dst = t.ZF.at[0] if k == 1 else t.ZFC.at[k - 2]
            return rcopy(b, dst, t.zf_s.at[k], t.zf_r.at[0 if k == 1 else k], p.dev(z=mate))

        def zf_over(k):
            return rcopy(t.DX.at[:, zf_cols(sides[k])], t.ZF.at[1], t.zf_s.at[k], t.zf_r.at[1], p.dev(z=sides[k]))

        def zf_start():
            @pl.when(inner == 0)
            def _():
                zf_part(3).start()
                zf_part(2).start()

            zf_part(1).start()

        def zf_mid(l, m, k):
            @pl.when(inner == 1)
            def _():
                zf_part(k).wait_recv()
                cols = zf_cols(sides[k])
                t.DX[:, cols] = (t.DX[:, cols].astype(F32) + t.ZFC[k - 2].astype(F32)).astype(BF)
                zf_over(k).start()

        def zf_y(k):
            b = t.DX.at[blk(p.yk(k), R2), zf_cols(z)]
            dst = t.YR.at[2, k - 1, :, zf_cols(z)]
            return rcopy(b, dst, t.zy_s.at[k], t.zy_r.at[k], p.dev(y=p.yk(k)))

        def zf_sum(l, m):
            zf_part(1).wait_recv()
            zf_over(2).wait_recv()
            cols = zf_cols(z)
            v = t.DX[:, cols].astype(F32) + t.ZF[0].astype(F32) + t.ZF[1].astype(F32)
            t.DX[:, cols] = v.astype(BF)
            for k in range(1, Y):
                zf_y(k).start()

        def zf_end(l, m):
            for k in range(1, Y):
                zf_y(k).wait_recv()
            v = t.DX[blk(y, R2), zf_cols(z)].astype(F32)
            for k in range(1, Y):
                v = v + t.YR[2, k - 1, :, zf_cols(z)].astype(F32)
            t.RD[2, :, :, 0 : TILE // 2] = v.astype(BF).reshape(2, R, TILE // 2)

        def c_part(l, m, cp):
            lm = 3 * l + m
            return rcopy(t.RD.at[lm, cp], t.CR.at[m, j], t.c_s.at[lm, cp], t.c_r.at[m, j], p.dev(x=l, c=cp))

        def to_owner(l, remote, local):
            for cp in range(2):
                mine = jnp.logical_and(x == l, c == cp)

                @pl.when(mine)
                def _():
                    local(cp).start()

                @pl.when(jnp.logical_not(mine))
                def _():
                    remote(cp).start()

        def z_sum(l, m):
            lm = 3 * l + m
            z_part(l, m, 1).wait_recv()
            z_over(l, m, 2).wait_recv()
            v = where(l, m)[blk(y, R2), usual(l, m, z)].astype(F32)
            v = v + t.ZR[lm, 0, :, take(l, m)].astype(F32) + t.ZR[lm, 1, :, take(l, m)].astype(F32)
            if (l, m) == (0, 2):
                t.RD[lm, :, :, TILE // 2 :] = v.astype(BF).reshape(2, R, TILE // 2)
            else:
                t.RD[lm] = v.astype(BF).reshape(2, R, TILE)
            to_owner(
                l, lambda cp: c_part(l, m, cp),
                lambda cp: pltpu.make_async_copy(t.RD.at[lm, cp], t.CR.at[m, j], t.c_r.at[m, j]),
            )

        def s_y(l, k):
            return rcopy(t.SG.at[l], t.SYR.at[l, k - 1], t.sy_s.at[l, k], t.sy_r.at[l, k], p.dev(y=p.yk(k)))

        def s_z(l, k):
            return rcopy(t.SRD.at[l], t.SZR.at[l, k - 1], t.sz_s.at[l, k], t.sz_r.at[l, k], p.dev(z=p.zk(k)))

        def s_c(l, cp):
            return rcopy(t.SRD.at[2 + l], t.SCR.at[j], t.sc_s.at[l, cp], t.sc_r.at[j], p.dev(x=l, c=cp))

        def s_start(l):
            begun.add((l,))
            for k in range(1, Y):
                s_y(l, k).start()

        def s_mid(l):
            for k in range(1, Y):
                s_y(l, k).wait_recv()
            t.SRD[l] = t.SG[l] + jnp.sum(t.SYR[l], axis=0)
            for k in range(1, nz):
                s_z(l, k).start()

        def s_end(l):
            for k in range(1, nz):
                s_z(l, k).wait_recv()
            t.SRD[2 + l] = t.SRD[l] + jnp.sum(t.SZR[l], axis=0)
            to_owner(
                l, lambda cp: s_c(l, cp), lambda cp: pltpu.make_async_copy(t.SRD.at[2 + l], t.SCR.at[j], t.sc_r.at[j])
            )

        steps = []
        for n in range(6):
            l, m = 1 - n // 3, 2 - n % 3
            ys = [(y_sum, (l, m, k)) for k in order]
            zs = [(z_mid, (l, m, 3)), (z_mid, (l, m, 2))]
            last = [(z_sum, (1 - (n - 1) // 3, 2 - (n - 1) % 3))] if n else []
            if n == 3:
                steps += ys[:2] + [(zf_mid, (0, 2, 3))] + ys[2:] + [(zf_mid, (0, 2, 2))] + zs + last
            elif n == 4:
                steps += ys[:2] + [(zf_sum, (0, 2))] + ys[2:] + zs
            elif n == 5:
                steps += ys + [(s_mid, (0,))] + zs + last + [(zf_end, (0, 2)), (z_sum, (0, 2)), (s_end, (0,))]
            else:
                steps += ys + zs + last
        steps.append((z_sum, (0, 0)))

        def push(n=1):
            for _ in range(n):
                if steps and steps[0][1][:2] in begun:
                    f, a = steps.pop(0)
                    f(*a)

        def push_through(f, l, m):
            while any(g is f and a[:2] == (l, m) for g, a in steps):
                push()

        kept = list(spilled)

        def save(name):
            i = kept.index(name)
            return pltpu.make_async_copy(getattr(t, name), getattr(t, "o_" + name), t.keep.at[0, i])

        def fetch(name):
            i = kept.index(name)
            return pltpu.make_async_copy(getattr(t, "o_" + name), getattr(t, name), t.keep.at[1, i])

        def add_small(l, r, v):
            t.SG[l, pl.ds(r, 1), :] += v

        def put_small(l, r, acc):
            v = jnp.sum(acc, axis=0, keepdims=True)
            for q in range(4):
                add_small(l, 4 * r + q, v[:, q * TILE : (q + 1) * TILE])

        def own_rows(g, r):
            return pl.ds(pl.multiple_of((2 * g + x) * RP + r * RC, RC), RC)

        def attend(l, g, zz):
            rows_, cols = half(g), blk(zz, TILE)
            v = mm(t.NF[rows_, :], W[3 * l, :, cols], NN)
            t.PR[rows_, cols] = (v + t.SPS[l, pl.ds(24 + zz, 1), :]).astype(BF)
            live = lax.broadcasted_iota(jnp.int32, (RP, RP), 1) < SEQ
            for i in range(2):
                im = 2 * g + i
                b = t.PR[row(g, i), cols]
                q, k, v = b[:, 0:HD], b[:, HD : 2 * HD], b[:, 2 * HD : 3 * HD]
                s = jnp.where(live, mm(q, k, NT) * SCALE, -1e30)
                w = jnp.exp(s - jnp.max(s, axis=-1, keepdims=True))
                pb = (w * (1.0 / jnp.sum(w, axis=-1, keepdims=True))).astype(BF)
                t.PB[4 * im + zz] = pb
                put_mixed(l, row(g, i), zz, mm(pb, v, NN).astype(BF))

        def put_mixed(l, ri, zz, o):
            pair = t.MXC[l, ri, blk(zz // 2, 2 * HD)]
            up_half = lax.rem(zz, 2) == 1
            low, high = pair[:, :HD], pair[:, HD:]
            t.MXC[l, ri, blk(zz // 2, 2 * HD)] = jnp.concatenate(
                [jnp.where(up_half, low, o), jnp.where(up_half, o, high)], axis=1
            )

        def out_weights(l):
            for zz in range(4):
                t.WO[l, :, zz * HD : (zz + 1) * HD] = W[3 * l, :, zz * TILE + 3 * HD : (zz + 1) * TILE]

        def out_project(l, g):
            for n in range(4):
                cols = blk(n, TILE)
                OP[half(g), cols] = mm(t.MXC[l, half(g), :], t.WO[l, cols, :], NT).astype(BF)

        def project(lhs, lm, g):
            rows_ = half(g)

            def step(n):
                cols = blk(n, TILE)
                OP[rows_, cols] = mm(lhs[rows_, :], W[lm, cols, :], NT).astype(BF)

            for n in range(4):
                step(n)

        def up(l, g, zz):
            rows_, cols = half(g), blk(zz, TILE)
            u = mm(t.N2[rows_, :], W[3 * l + 1, :, cols], NN) + t.SPS[l, pl.ds(28 + zz, 1), :]
            cdf = 0.5 + 0.5 * lax.erf(u * (1.0 / math.sqrt(2.0)))
            t.H[rows_, cols] = (u * cdf).astype(BF)
            t.GD[rows_, cols] = (cdf + u * jnp.exp(-0.5 * u * u) * (1.0 / math.sqrt(2.0 * math.pi))).astype(BF)

        def pre(l, g):
            rows_ = half(g)

            def step(n):
                cols = blk(n, TILE)
                v = mm(t.GT[rows_, :], W[3 * l + 2, :, cols], NN) * t.GD[rows_, cols].astype(F32)
                gp = v.astype(BF)
                t.GD[rows_, cols] = gp
                add_small(l, 28 + n, jnp.sum(gp.astype(F32), axis=0, keepdims=True))

            for n in range(4):
                step(n)

        def weight_grad(buf, a, b):
            for r in range(4):
                cols = blk(r, TILE)
                buf[cols, :] = mm(a[:, cols], b[...], TN).astype(BF)

        def weight_grad_attn(l, buf):
            for r in range(4):
                cols = blk(r, TILE)
                v = mm(t.NF[:, cols], t.H[...], TN).astype(BF)
                o = mm(t.MX[:, cols], t.MXC[l], TN).astype(BF)
                for zz in range(4):
                    lo = zz * TILE
                    buf[cols, lo : lo + TILE] = jnp.concatenate(
                        [v[:, lo : lo + 3 * HD], o[:, zz * HD : (zz + 1) * HD]], axis=1
                    )

        def mixed_grad(l, g):
            t.GMC[half(g), :] = mm(t.MX[half(g), :], t.WO[l], NN).astype(BF)

        def attend_back(l, g):
            def step(i, _):
                im = 2 * g + i
                ri = blk(im, RP)
                for zz in range(4):
                    cols = blk(zz, TILE)
                    b = t.PR[ri, cols]
                    q, k, v = b[:, 0:HD], b[:, HD : 2 * HD], b[:, 2 * HD : 3 * HD]
                    gm = t.GMC[ri, zz * HD : (zz + 1) * HD]
                    pb = t.PB[4 * im + zz]
                    pf = pb.astype(F32)
                    gp = mm(gm, v, NT)
                    cen = jnp.sum(pf * gp, axis=-1, keepdims=True)
                    gsc = (pf * (gp - cen)).astype(BF)
                    gq = mm(gsc, k, NN) * SCALE
                    gk = mm(gsc, q, TN) * SCALE
                    gv = mm(pb, gm, TN)
                    out = jnp.concatenate([gq, gk, gv, jnp.zeros((RP, HD), F32)], axis=1).astype(BF)
                    t.H[ri, cols] = out
                    add_small(l, 24 + zz, jnp.sum(out.astype(F32), axis=0, keepdims=True))
                return 0

            lax.fori_loop(0, 2, step, 0)

        def swap(buf, got, i):
            return rcopy(buf.at[1 - x], got, t.lo_s.at[i], t.lo_r.at[i], p.dev(x=1 - x))

        def rows_loop(step, init=0, h=None):
            lo, hi = (0, RP // RC) if h is None else PARTS[h]
            return lax.fori_loop(lo, hi, step, init)

        firsts = [
            pltpu.make_async_copy(t.wq, t.WQ, t.io.at[6]),
            pltpu.make_async_copy(t.wo, t.WOS, t.io.at[7]),
            pltpu.make_async_copy(t.imgs.at[0:2], t.XO, t.io.at[0]),
            pltpu.make_async_copy(t.imgs.at[2], t.GT.at[row(c, 0)], t.io.at[1]),
            pltpu.make_async_copy(t.imgs.at[3], t.GT.at[row(c, 1)], t.io.at[8]),
        ]
        for cp in firsts:
            cp.start()
        for cp in firsts[:2]:
            cp.wait()
        for jp in range(4):
            parts = [t.WQ[:, k * TILE + jp * HD : k * TILE + (jp + 1) * HD] for k in range(3)]
            t.WA[jp] = jnp.concatenate(parts + [t.WOS[:, jp * HD : (jp + 1) * HD]], axis=1)
        t.SG[...] = jnp.zeros((2, 32, TILE), F32)
        t.MXC[...] = jnp.zeros((2, 4 * RP, TILE), BF)
        p.barrier()
        for k in range(4):
            small_red(k).start()
        for m in range(3):
            for k in (1, 2, 3, 0):
                red(m, k).start()
        for l in range(2):
            for cs in range(2):
                b = t.SPB.at[l, y, z, cs]
                pltpu.make_async_copy(b, b, t.pr.at[l, cs]).wait()
            for k in range(1, nz):
                small_z(l, k).start()
        for cp in firsts[2:]:
            cp.wait()
        tops = ag_local(t.GT, 4)
        for cp in tops:
            cp.start()
        release(0)
        for l in range(2):
            for k in range(1, nz):
                small_z(l, k).wait_recv()
            for k in range(1, Y):
                small_y(l, k).start()
        for l in range(2):
            for k in range(1, Y):
                small_y(l, k).wait_recv()
            t.SPS[l] = jnp.sum(t.SPB[l].astype(F32).reshape(Y * nz * 2, 32, TILE), axis=0)
            for r in range(6):
                for q in range(4):
                    t.G[l, r : r + 1, q * TILE : (q + 1) * TILE] = t.SPS[l, 4 * r + q : 4 * r + q + 1, :]

        def ln(l, g, b, load, buf, at):
            gain, shift = t.G[l, g : g + 1, :], t.G[l, b : b + 1, :]

            def step(r, _):
                buf[at(r), :] = norm_row(load(r), gain, shift).astype(BF)
                return 0

            rows_loop(step)

        for m in range(2):
            ln(
                0, 0, 2, lambda r, m=m: t.XO[m, blk(r, RC), :].astype(F32), t.NF,
                lambda r, m=m: pl.ds(pl.multiple_of((2 * c + m) * RP + r * RC, RC), RC),
            )
        first = ag_local(t.NF, 0)
        for cp in first:
            cp.start()
        release(1)
        pump(1)
        for cp in first:
            cp.wait_recv()

        for l in range(2):
            A, U, DN = 3 * l, 3 * l + 1, 3 * l + 2
            s = 2 * l
            if l:
                ag_in(t.NF, 0, 2)
            for k in range(4):
                ready(A, k)
                attend(l, 0, holds[k])
                if l == 0 or k < 2:
                    pump()
            if l:
                rs_done(0, 1)
                rs_done(1, 1)
            out_weights(l)
            out_project(l, 0)
            rs_out(0, s)
            if l:
                ag_mid(t.NF, 1, 2)
                ag_in(t.NF, 1, 2)
            for k in range(4):
                attend(l, 1, holds[k])
                if k % 2:
                    pump()
            out_project(l, 1)
            rs_out(1, s)
            if l == 0:
                for cp in first:
                    cp.wait_send()
                for name in ("NF", "PR", "PB"):
                    save(name).start()
            else:
                ag_done(t.NF, 2)

            def second(g, h):
                gain, shift, bias = t.G[l, 1:2, :], t.G[l, 4:5, :], t.G[l, 3:4, :]

                def step(r, _):
                    rs = blk(r, RC)
                    v = t.XO[x, rs, :] if l == 0 else t.OUT[0, rs, :]
                    mid = v.astype(F32) + sums(g, r) + bias
                    t.MID[l, rs, :] = mid
                    t.N2[own_rows(g, r), :] = norm_row(mid, gain, shift).astype(BF)
                    return 0

                rows_loop(step, 0, h)
                ag_send(t.N2, g, 1 + 2 * l, h)
                return 0

            pump()
            for g in range(2):
                rs_in(g, s, lambda h, _, g=g: second(g, h))
            pump()
            ag_mid(t.N2, 0, 1 + 2 * l)
            ag_in(t.N2, 0, 1 + 2 * l)
            if l:
                save("H").wait()
                save("GD").wait()
            for k in range(4):
                ready(U, k)
                up(l, 0, holds[k])
            ag_mid(t.N2, 1, 1 + 2 * l)
            pump()
            ag_in(t.N2, 1, 1 + 2 * l)
            for k in range(4):
                up(l, 1, holds[k])
            pump()
            ag_done(t.N2, 1 + 2 * l)
            rs_done(0, s)
            rs_done(1, s)
            if l == 0:
                for name in ("N2", "H", "GD"):
                    save(name).start()
                for name in ("NF", "PR", "PB"):
                    save(name).wait()
            else:
                for cp in tops:
                    cp.wait_recv()
                weight_grad(t.DX, t.GT, t.H)
                y_start(1, 2)
            for k in range(4):
                ready(DN, k)
            if l == 1:
                break
            s = 2 * l + 1
            project(t.H, DN, 0)
            rs_out(0, s)
            pump()
            project(t.H, DN, 1)
            rs_out(1, s)
            pump()
            if l == 0:
                save("N2").wait()

                def last(g, h):
                    gain, shift, bias = t.G[1, 0:1, :], t.G[1, 2:3, :], t.G[0, 5:6, :]

                    def step(r, _):
                        rs = blk(r, RC)
                        o = (t.MID[0, rs, :] + sums(g, r) + bias).astype(BF)
                        t.OUT[0, rs, :] = o
                        t.NF[own_rows(g, r), :] = norm_row(o.astype(F32), gain, shift).astype(BF)
                        return 0

                    rows_loop(step, 0, h)
                    ag_send(t.NF, g, 2, h)
                    return 0

                for g in range(2):
                    rs_in(g, s, lambda h, _, g=g: last(g, h))
                pump()
                ag_mid(t.NF, 0, 2)


        for k in range(1, 4):
            small_red(k).wait_send()
        for l in range(2):
            for k in range(1, nz):
                small_z(l, k).wait_send()
            for k in range(1, Y):
                small_y(l, k).wait_send()
        for m in range(3):
            for k in range(1, 4):
                red(m, k).wait_send()
        for lm in range(6):
            wz(lm, 1).wait_send()
            wz(lm, 2).wait_send()
            for k in (1, 2):

                @pl.when(inner == 1)
                def _():
                    wrelay(lm, k).wait_send()

            for k in range(4):
                for ky in range(1, Y):
                    wy(lm, k, ky).wait_send()

        def final_out(h):
            def step(r, _):
                rs = blk(r, RC)
                v = t.FIN[rs, :] + RB[1, x, rs, :].astype(F32) + XR[1, rs, :].astype(F32)
                t.OUT[1, rs, :] = v.astype(BF)
                return 0

            return rows_loop(step, 0, h)

        def forward_end():
            for g in range(2):
                rs_done(g, 4)
            for g in range(2):
                project(t.H, 5, g)
                rs_help(g, 3)
            for g in range(2):

                @pl.when(c == g)
                def _():
                    def step(r, _):
                        rs = blk(r, RC)
                        t.FIN[rs, :] = t.MID[1, rs, :] + OP[own_rows(g, r), :].astype(F32) + t.G[1, 5:6, :]
                        return 0

                    rows_loop(step)

        zero8 = jnp.zeros((8, D), F32)
        for l in (1, 0):
            A, U, DN = 3 * l, 3 * l + 1, 3 * l + 2
            s = 4 + 2 * (1 - l)
            if l == 0:
                ag_in(t.GT, 0, 6)
                fetch("GD").wait()
            if l == 0:
                rs_done(0, s - 1)
                rs_done(1, s - 1)
            pre(l, 0)
            project(t.GD, U, 0)
            rs_out(0, s)
            push()
            if l == 0:
                ag_mid(t.GT, 1, 6)
                ag_in(t.GT, 1, 6)
                fetch("H").wait()
                push_through(z_sum, 1, 2)
                for kz in range(nz):
                    for k in range(1, Y):
                        y_part(1, 2, k, kz).wait_send()
                z_sent(1, 2)
                weight_grad(t.DX, t.GT, t.H)
                push_through(y_sum, 1, 0)
                y_start(0, 2)
                zf_start()
            pre(l, 1)
            project(t.GD, U, 1)
            rs_out(1, s)
            push()
            if l == 1:
                for cp in tops:
                    cp.wait_send()
            else:
                ag_done(t.GT, 6)

            def fill_up():
                if l == 0:
                    fetch("N2").wait()
                weight_grad(W.at[U], t.N2, t.GD)
                y_start(l, 1)
                if l == 1:
                    fetch("N2").start()
                    fetch("GD").start()

            def mid_back(g, h, init):
                def step(r, acc):
                    rs = blk(r, RC)
                    dy = sums(g, r)
                    top = t.GT[own_rows(g, r), :].astype(F32)
                    dx, dg = norm_back(t.MID[l, rs, :], t.G[l, 1:2, :], dy)
                    gmid = top + dx
                    t.GMID[rs, :] = gmid
                    t.MX[own_rows(g, r), :] = gmid.astype(BF)
                    return acc[0] + fold(dg), acc[1] + fold(dy), acc[2] + fold(gmid), acc[3] + fold(top)

                acc = rows_loop(step, init, h)
                ag_send(t.MX, g, s + 1, h)
                return acc

            def mid_end(acc):
                for i, r in enumerate((1, 4, 3, 5)):
                    put_small(l, r, acc[i])

            rs_in(0, s, lambda h, acc: mid_back(0, h, acc), (zero8,) * 4, mid_end)
            fill_up()
            rs_in(1, s, lambda h, acc: mid_back(1, h, acc), (zero8,) * 4, mid_end)
            if l == 1:
                forward_end()
            push()
            if l == 0:
                s_mid(1)
                for name in ("PR", "PB"):
                    fetch(name).wait()
            ag_mid(t.MX, 0, s + 1)
            ag_in(t.MX, 0, s + 1)
            push()
            mixed_grad(l, 0)
            attend_back(l, 0)
            push()
            if l == 1:
                for g in range(2):
                    rs_own(g, 3)
            rs_done(0, s if l == 0 else 3)
            rs_done(1, s if l == 0 else 3)
            project(t.H, A, 0)
            rs_out(0, s + 1)
            push()
            ag_mid(t.MX, 1, s + 1)
            ag_in(t.MX, 1, s + 1)
            mixed_grad(l, 1)
            attend_back(l, 1)
            push()
            project(t.H, A, 1)
            rs_out(1, s + 1)
            ag_done(t.MX, s + 1)
            if l == 1:
                push_through(y_sum, 1, 1)
            else:
                fetch("NF").wait()
                push_through(y_sum, 0, 2)
            def first_back(g, h, init):
                def step(r, acc):
                    rs = blk(r, RC)
                    dy = sums(g, r)
                    v = (t.XO[x, rs, :] if l == 0 else t.OUT[0, rs, :]).astype(F32)
                    dx, dg = norm_back(v, t.G[l, 0:1, :], dy)
                    gx = (t.GMID[rs, :] + dx).astype(BF)
                    t.IGB[l, rs, :] = gx
                    if l == 1:
                        t.GT[own_rows(g, r), :] = gx
                    return acc[0] + fold(dg), acc[1] + fold(dy)

                acc = rows_loop(step, init, h)
                if l == 1:
                    ag_send(t.GT, g, 6, h)
                return acc

            def first_end(acc):
                put_small(l, 0, acc[0])
                put_small(l, 2, acc[1])

            if l == 0:
                swap(t.OUT, t.LOB, 0).start()

            def fill_attn():
                weight_grad_attn(l, W.at[A])
                y_start(l, 0)
                if l == 1:
                    for name in ("H", "PR", "PB", "NF"):
                        fetch(name).start()

            if l == 0:
                fill_attn()
            rs_in(0, s + 1, lambda h, acc: first_back(0, h, acc), (zero8,) * 2, first_end)
            if l == 1:
                fill_attn()
            rs_in(1, s + 1, lambda h, acc: first_back(1, h, acc), (zero8,) * 2, first_end)
            if l == 1:
                for g in range(2):
                    rs_in(g, 3, lambda h, _: final_out(h))
            s_start(l)

            if l == 1:
                ag_mid(t.GT, 0, 6)

        swap(t.IGB, t.LGB, 1).start()
        push(100)
        s_end(1)
        give = []
        for i, (buf, got, out) in enumerate(((t.OUT, t.LOB, t.lo), (t.IGB, t.LGB, t.ig))):
            cp = swap(buf, got, i)
            cp.wait_recv()
            cp.wait_send()
            give.append(pltpu.make_async_copy(buf.at[x], out.at[x], t.io.at[2 + 2 * i]))
            give.append(pltpu.make_async_copy(got, out.at[1 - x], t.io.at[3 + 2 * i]))
            for cp in give[-2:]:
                cp.start()
        for m in (2, 1, 0):
            for jj in range(4):
                b = t.CR.at[m, jj]
                pltpu.make_async_copy(b, b, t.c_r.at[m, jj]).wait()
                give.append(pltpu.make_async_copy(b, t.cr.at[m, :, blk(jj, TILE)], t.cr_s.at[m, jj]))
                give[-1].start()
        for jj in range(4):
            b = t.SCR.at[jj]
            pltpu.make_async_copy(b, b, t.sc_r.at[jj]).wait()
            t.gs_out[jj] = t.SCR[jj]
        for cp in give:
            cp.wait()
        for g in range(2):
            rs_done(g, 7)
        for h in range(2):
            chip_part(3, h).wait_send()
        for k in (1, 2, 3):
            zf_part(k).wait_send()
        for k in range(1, Y):
            zf_y(k).wait_send()
        for l in range(2):
            for m in range(3 if l == 0 else 2):
                for kz in range(nz):
                    for k in range(1, Y):
                        y_part(l, m, k, kz).wait_send()
                z_sent(l, m)
            for k in range(1, Y):
                s_y(l, k).wait_send()
            for k in range(1, nz):
                s_z(l, k).wait_send()
            for cp in range(2):

                @pl.when(jnp.logical_not(jnp.logical_and(x == l, c == cp)))
                def _():
                    s_c(l, cp).wait_send()
                    for m in range(3):
                        c_part(l, m, cp).wait_send()

    vm = pl.BlockSpec(memory_space=pltpu.VMEM)
    hbm = pl.BlockSpec(memory_space=pl.ANY)
    return pl.pallas_call(
        body,
        out_shape=[jax.ShapeDtypeStruct(*a) for a in outputs.values()]
        + [jax.ShapeDtypeStruct(a, BF) for a in spilled.values()],
        in_specs=[hbm] * 6,
        out_specs=[hbm] * (len(outputs) - 1) + [vm] + [hbm] * len(spilled),
        scratch_shapes=[pltpu.VMEM(*a) for a in vmem.values()] + [dma(a) for a in sems.values()],
        compiler_params=pltpu.CompilerParams(
            collective_id=0, has_side_effects=True, vmem_limit_bytes=VMEM_LIMIT
        ),
    )


def small_pack(norm_gains, row_shifts, head_bias, unit_bias, dpn, nz):
    dp, z = lax.axis_index("dp"), lax.axis_index("tensor")
    rows = jnp.concatenate([norm_gains[0], row_shifts[0]], axis=0)
    w = rows.shape[1]
    rows = lax.dynamic_update_slice(jnp.zeros((6, D), BF), rows, (0, (dp * nz + z) * w)).reshape(1, 24, TILE)
    hw, uw = head_bias.shape[3], unit_bias.shape[2]
    head = jnp.zeros((4, 4, TILE), BF)
    head = lax.dynamic_update_slice(head, head_bias[0, 0][:, None], (0, z, dp * hw))
    head = lax.dynamic_update_slice(head, head_bias[0, 1][:, None], (0, z, 2 * HD + dp * hw))
    unit = lax.dynamic_update_slice(jnp.zeros((4, 4, TILE), BF), unit_bias[0][:, None], (0, z, dp * uw))
    return jnp.concatenate([jnp.broadcast_to(rows, (4, 24, TILE)), head, unit], axis=1)


def solution(mesh):
    dpn, nz = mesh.shape["dp"], mesh.shape["tensor"]

    def on_device(
        images_in, cotangent, w_qkv, w_out, w_up, w_down, norm_gains, row_shifts, head_bias, unit_bias
    ):
        R = w_up.shape[1]
        sp = small_pack(norm_gains, row_shifts, head_bias, unit_bias, dpn, nz)
        imgs = jnp.pad(jnp.concatenate([images_in, cotangent]), ((0, 0), (0, RP - SEQ), (0, 0)))
        lo, ig, cr, gs = both_layers(dpn, nz, R)(
            imgs, w_qkv[0].reshape(R, 3 * TILE), w_out[0], w_up[0], w_down[0], sp
        )[:4]
        lo, ig = lo[:, :SEQ], ig[:, :SEQ]
        gu, gd = cr[1].astype(F32), cr[2].astype(F32)
        dp, z = lax.axis_index("dp"), lax.axis_index("tensor")
        ga = cr[0].astype(F32).reshape(R, 4, TILE)
        g_qkv = ga[:, :, : 3 * HD].reshape(R, 4, 3, HD).transpose(0, 2, 1, 3).reshape(w_qkv.shape)
        g_out = ga[:, :, 3 * HD :].reshape(w_out.shape)
        w, hw, uw = norm_gains.shape[2], head_bias.shape[3], unit_bias.shape[2]
        rows = lax.dynamic_slice(jnp.sum(gs[:, :24], axis=0).reshape(6, D), (0, (dp * nz + z) * w), (6, w))
        head = lax.dynamic_slice(gs, (0, 24 + z, 0), (4, 1, TILE))[:, 0]
        unit = lax.dynamic_slice(gs, (0, 28 + z, dp * uw), (4, 1, uw))[:, 0]
        g_head = jnp.stack([lax.dynamic_slice(head, (0, o + dp * hw), (4, hw)) for o in (0, 2 * HD)])
        return (
            lo[None], ig[None], g_qkv, g_out, gu[None], gd[None],
            rows[None, :2], rows[None, 2:], g_head[None], unit[None],
        )

    in_specs = (
        P(None, ("dp", "tensor"), None),
        P(None, ("dp", "tensor"), None),
        P("section", "dp", None, "tensor"),
        P("section", "dp", "tensor"),
        P("section", "dp", "tensor"),
        P("section", "dp", "tensor"),
        P("section", None, ("dp", "tensor")),
        P("section", None, ("dp", "tensor")),
        P("section", None, "tensor", "dp"),
        P("section", "tensor", "dp"),
    )
    out_specs = (
        P("section", None, ("dp", "tensor"), None),
        P("section", None, ("dp", "tensor"), None),
        P("section", "dp", None, "tensor"),
        P("section", "dp", "tensor"),
        P("section", "dp", "tensor"),
        P("section", "dp", "tensor"),
        P("section", None, ("dp", "tensor")),
        P("section", None, ("dp", "tensor")),
        P("section", None, "tensor", "dp"),
        P("section", "tensor", "dp"),
    )
    return jax.shard_map(
        on_device, mesh=mesh, in_specs=in_specs, out_specs=out_specs, check_vma=False
    )
```
